32 devices in a mesh: dp: 8 (over y, x, core), tp: 4 (over z).
Axes of the slice: x: 2, y: 2, z: 4, core: 2. Of those that a mesh axis runs over, the one named last changes fastest.
Arguments:
- tokens: bfloat16 [16, 788, 768], P('dp', 'tp'), may hold values from -6 to 6
- first_gain: bfloat16 [768], replicated, may hold values from 0.25 to 1.75
- first_shift: bfloat16 [768], replicated, may hold values from -3 to 3
- mixing_in: bfloat16 [768, 2304], replicated, may hold values from -0.21875 to 0.21875
- query_bias: bfloat16 [768], replicated, may hold values from -3 to 3
- value_bias: bfloat16 [768], replicated, may hold values from -3 to 3
- relative_table: bfloat16 [732, 12], replicated, may hold values from -4 to 4
- mixing_out: bfloat16 [768, 768], replicated, may hold values from -1.25 to 1.25
- out_bias: bfloat16 [768], replicated, may hold values from -2.5 to 2.5
- scale_attention: bfloat16 [768], replicated, may hold values from 0.25 to 1.75
- second_gain: bfloat16 [768], replicated, may hold values from 0.25 to 1.75
- second_shift: bfloat16 [768], replicated, may hold values from -3 to 3
- hidden_in: bfloat16 [768, 3072], P(None, 'tp'), may hold values from -0.21875 to 0.21875
- hidden_bias: bfloat16 [3072], P('tp'), may hold values from -3 to 3
- hidden_out: bfloat16 [3072, 768], P('tp'), may hold values from -0.109375 to 0.109375
- output_bias: bfloat16 [768], replicated, may hold values from -2.5 to 2.5
- scale_hidden: bfloat16 [768], replicated, may hold values from 0.25 to 1.75
- cotangent: bfloat16 [16, 788, 768], P('dp', 'tp'), may hold values from -6 to 6
Outputs:
- result: bfloat16 [16, 788, 768], P('dp', 'tp')
- token_grad: bfloat16 [16, 788, 768], P('dp', 'tp')
- first_gain_grad: float32 [768], replicated
- first_shift_grad: float32 [768], replicated
- mixing_in_grad: float32 [768, 2304], replicated
- query_bias_grad: float32 [768], replicated
- value_bias_grad: float32 [768], replicated
- relative_table_grad: float32 [732, 12], replicated
- mixing_out_grad: float32 [768, 768], replicated
- out_bias_grad: float32 [768], replicated
- scale_attention_grad: float32 [768], replicated
- second_gain_grad: float32 [768], replicated
- second_shift_grad: float32 [768], replicated
- hidden_in_grad: float32 [768, 3072], P(None, 'tp')
- hidden_bias_grad: float32 [3072], P('tp')
- hidden_out_grad: float32 [3072, 768], P('tp')
- output_bias_grad: float32 [768], replicated
- scale_hidden_grad: float32 [768], replicated
The draws below stay inside these ranges and needn't reach their ends.
All inputs are finite; a program needn't handle non-finite values.
Results may differ from the reference program's by a relative error of at most 0.014.
Values may be sent and summed in bfloat16 or wider, within the bound.
No kernel may reach another device: no remote copies, remote signals or barrier semaphores. Data moves between devices by JAX's collectives and lax.ppermute only.
A program may use at most 192 MiB of HBM per device.

```python
import jax
import jax.numpy as jnp
from jax import lax

D = 768
HEADS = 12
HEAD = 64
FF = 3072
GRID = 14
SEQ_DEV = 2
PATCHES = 197
TABLE = 732
SEQS = 16
PACK_ROWS = 788
N_DP = 8


def block_scale(key, shape, pieces, least, high):
    factor_of, own = 1.0, jax.random.fold_in(key, 6)
    for position, parts in pieces:
        heights = jnp.exp(jax.random.uniform(jax.random.fold_in(own, position), (parts,), jnp.float32, least / len(pieces), high / len(pieces)))
        factor_of = factor_of * jnp.repeat(heights, shape[position] // parts).reshape([-1 if axis == position else 1 for axis in range(len(shape))])
    return factor_of


def centred(rng, extent, deviation, bound, cuts=(), held_as=jnp.bfloat16):
    level = block_scale(rng, extent, cuts, -0.22, 0.18) if cuts else 1.0
    array = jax.random.normal(rng, extent, jnp.float32) * deviation * level
    return jnp.minimum(jnp.maximum(array, -bound), bound).astype(held_as)


def setup_inputs(seed: int = 0) -> dict:
    keys = jax.random.split(jax.random.key(seed), 19)
    return {
        "tokens": centred(keys[0], (SEQS, PACK_ROWS, D), 1.0, 6.0, ((0, 8), (1, 4))),
        "first_gain": jnp.clip(1.0 + 0.15 * jax.random.normal(keys[1], (D,), jnp.float32), 0.25, 1.75).astype(jnp.bfloat16),
        "first_shift": centred(keys[2], (D,), 0.5, 3.0),
        "mixing_in": centred(keys[3], (D, 3 * D), D ** -0.5, 0.21875),
        "query_bias": centred(keys[4], (D,), 0.5, 3.0),
        "value_bias": centred(keys[5], (D,), 0.5, 3.0),
        "relative_table": centred(keys[6], (TABLE, HEADS), 1.0, 4.0),
        "mixing_out": centred(keys[7], (D, D), (D // 32) ** -0.5, 1.25),
        "out_bias": centred(keys[8], (D,), 0.4, 2.5),
        "scale_attention": jnp.clip(1.0 + 0.15 * jax.random.normal(keys[9], (D,), jnp.float32), 0.25, 1.75).astype(jnp.bfloat16),
        "second_gain": jnp.clip(1.0 + 0.15 * jax.random.normal(keys[10], (D,), jnp.float32), 0.25, 1.75).astype(jnp.bfloat16),
        "second_shift": centred(keys[11], (D,), 0.5, 3.0),
        "hidden_in": centred(keys[12], (D, FF), D ** -0.5, 0.21875, ((1, 4),)),
        "hidden_bias": centred(keys[13], (FF,), 0.5, 3.0, ((0, 4),)),
        "hidden_out": centred(keys[14], (FF, D), FF ** -0.5, 0.109375, ((0, 4),)),
        "output_bias": centred(keys[15], (D,), 0.4, 2.5),
        "scale_hidden": jnp.clip(1.0 + 0.15 * jax.random.normal(keys[16], (D,), jnp.float32), 0.25, 1.75).astype(jnp.bfloat16),
        "cotangent": centred(keys[17], (SEQS, PACK_ROWS, D), 1.0, 6.0, ((0, 8), (1, 4))),
    }


HIGH = lax.Precision.HIGHEST
EPSILON = 1e-06

@jax.custom_vjp
def low(v):
    return lax.optimization_barrier(v.astype(jnp.bfloat16)).astype(jnp.float32)

@jax.custom_vjp
def low_back(v):
    return v

def low_keep(v):
    return (low(v), None)

def low_pass(kept, grad):
    return (grad,)

def back_keep(v):
    return (v, None)

def back_low(kept, grad):
    return (low(grad),)
low.defvjp(low_keep, low_pass)
low_back.defvjp(back_keep, back_low)

def layer_norm(values, gain, shift):
    center = values - lax.optimization_barrier(jnp.mean(values, axis=-1, keepdims=True))
    spread = lax.optimization_barrier(jnp.mean(center * center, axis=-1, keepdims=True))
    return center * lax.rsqrt(spread + EPSILON) * gain + shift

def offsets_onehot(grid):
    reach = 2 * grid - 1
    places = jnp.arange(grid)
    slots = jnp.arange(reach)
    return (places[:, None, None] - places[None, :, None] + grid - 1 == slots[None, None, :]).astype(jnp.float32)

def position_bias(table, grid):
    reach = 2 * grid - 1
    heads = table.shape[1]
    inner = reach * reach
    count = grid * grid
    onehot = offsets_onehot(grid)
    grid_table = table[:inner].reshape(reach, reach, heads)
    half_bias = jnp.einsum('ija,abh->ijbh', onehot, grid_table, precision=HIGH)
    patch_bias = jnp.einsum('ijbh,klb->hikjl', half_bias, onehot, precision=HIGH).reshape(heads, count, count)
    corner = jnp.broadcast_to(table[inner + 2][:, None, None], (heads, 1, 1))
    from_class = jnp.broadcast_to(table[inner][:, None, None], (heads, 1, count))
    to_class = jnp.broadcast_to(table[inner + 1][:, None, None], (heads, count, 1))
    upper = jnp.concatenate([corner, from_class], axis=2)
    lower = jnp.concatenate([to_class, patch_bias], axis=2)
    return jnp.concatenate([upper, lower], axis=1)

def block_forward(params, group):
    first_gain, first_shift, mixing_in, query_bias, value_bias, relative_table, mixing_out, out_bias, scale_attention, second_gain, second_shift, hidden_in, hidden_bias, hidden_out, output_bias, scale_hidden = params
    flat_rows = group.reshape(-1, D)
    images = flat_rows.shape[0] // PATCHES
    normed = low(layer_norm(flat_rows, first_gain, first_shift))
    packed_bias = jnp.concatenate([query_bias, jnp.zeros_like(query_bias), value_bias])
    packed = low(low_back(jnp.dot(normed, mixing_in, precision=HIGH) + packed_bias))
    split = packed.reshape(images, PATCHES, 3, HEADS, HEAD)
    queries, key_rows, value_rows = (split[:, :, 0], split[:, :, 1], split[:, :, 2])
    scores = jnp.einsum('nqhd,nkhd->nhqk', queries, key_rows, precision=HIGH) * HEAD ** (-0.5)
    scores = low_back(scores + position_bias(relative_table, GRID)[None])
    attend = low(jax.nn.softmax(scores, axis=-1))
    mixed = jnp.einsum('nhqk,nkhd->nqhd', attend, value_rows, precision=HIGH).reshape(-1, D)
    mixed = low(low_back(mixed))
    branch_attention = low_back(jnp.dot(mixed, mixing_out, precision=HIGH) + out_bias)
    middle = flat_rows + scale_attention * branch_attention
    normed_two = low(layer_norm(middle, second_gain, second_shift))
    before = low_back(jnp.dot(normed_two, hidden_in, precision=HIGH) + hidden_bias)
    active = low(jax.nn.gelu(before, approximate=False))
    branch_full = low_back(jnp.dot(active, hidden_out, precision=HIGH) + output_bias)
    return (middle + scale_hidden * branch_full).reshape(group.shape)

def reference(tokens, first_gain, first_shift, mixing_in, query_bias, value_bias, relative_table, mixing_out, out_bias, scale_attention, second_gain, second_shift, hidden_in, hidden_bias, hidden_out, output_bias, scale_hidden, cotangent):
    params = tuple((item.astype(jnp.float32) for item in (first_gain, first_shift, mixing_in, query_bias, value_bias, relative_table, mixing_out, out_bias, scale_attention, second_gain, second_shift, hidden_in, hidden_bias, hidden_out, output_bias, scale_hidden)))
    groups = tokens.astype(jnp.float32).reshape(N_DP, SEQ_DEV, PACK_ROWS, D)
    upstream = cotangent.astype(jnp.float32).reshape(N_DP, SEQ_DEV, PACK_ROWS, D)

    def one_group(totals, pair):
        group, group_cot = pair
        output, pullback = jax.vjp(block_forward, params, group)
        param_grads, group_grad = pullback(group_cot)
        totals = jax.tree.map(jnp.add, totals, param_grads)
        return (totals, (output.astype(jnp.bfloat16), group_grad.astype(jnp.bfloat16)))
    zeros = jax.tree.map(jnp.zeros_like, params)
    totals, (outputs, row_grads) = lax.scan(one_group, zeros, (groups, upstream))
    result = outputs.reshape(SEQS, PACK_ROWS, D)
    token_grad = row_grads.reshape(SEQS, PACK_ROWS, D)
    return (result, token_grad, totals[0], totals[1], totals[2], totals[3], totals[4], totals[5], totals[6], totals[7], totals[8], totals[9], totals[10], totals[11], totals[12], totals[13], totals[14], totals[15])
```

```python
import functools

import jax
import jax.numpy as jnp
from jax import lax
from jax.experimental import pallas as pl
from jax.experimental.pallas import tpu as pltpu
from jax.sharding import PartitionSpec as P

GRID = 14
EPSILON = 1e-06
ROWS = 208
LANES = 768
SPREAD = 384
VMEM = 56 * 1024 * 1024

f32 = jnp.float32
bf16 = jnp.bfloat16

NN = (((1,), (0,)), ((), ()))
NT = (((1,), (1,)), ((), ()))
TN = (((0,), (0,)), ((), ()))

(
    FIRST_GAIN,
    FIRST_SHIFT,
    QUERY_BIAS,
    VALUE_BIAS,
    OUT_BIAS,
    SCALE_ATTENTION,
    SECOND_GAIN,
    SECOND_SHIFT,
    OUTPUT_BIAS,
    SCALE_HIDDEN,
) = range(10)


def dot(a, b, dims=NN):
    return lax.dot_general(a, b, dims, preferred_element_type=f32)


def call(kernel, name, outs, scratch=(), vmem=VMEM, flops=0, **kw):
    def run(*args):
        traffic = sum(a.size * a.dtype.itemsize for a in args)
        traffic += sum(o.size * o.dtype.itemsize for o in outs)
        return pl.pallas_call(
            kernel,
            out_shape=outs,
            in_specs=[pl.BlockSpec(memory_space=pltpu.VMEM)] * len(args),
            out_specs=tuple(pl.BlockSpec(memory_space=pltpu.VMEM) for _ in outs),
            scratch_shapes=scratch,
            name=name,
            compiler_params=pltpu.CompilerParams(vmem_limit_bytes=vmem),
            cost_estimate=pl.CostEstimate(
                flops=int(flops), bytes_accessed=int(traffic), transcendentals=0
            ),
            **kw,
        )(*args)

    return run


def norm_parts(values):
    center = values - jnp.mean(values, axis=-1, keepdims=True)
    spread = jnp.mean(center * center, axis=-1, keepdims=True)
    rate = lax.rsqrt(spread + EPSILON)
    return center * rate, rate


def spread_onehot():
    entry = lax.broadcasted_iota(jnp.int32, (LANES, SPREAD), 0)
    column = lax.broadcasted_iota(jnp.int32, (LANES, SPREAD), 1)
    d = lax.div(column, GRID)
    x = column - d * GRID
    return entry == d * (2 * GRID - 1) + x + GRID - 1


def expand_table(table_ref, spread_ref, bias_ref, heads):
    onehot = spread_onehot().astype(bf16)
    reach = 2 * GRID - 1
    inner = reach * reach
    for h in range(heads):
        rows = jnp.broadcast_to(table_ref[h : h + 1, :], (16, LANES))
        spread_ref[h * 16 : (h + 1) * 16, :] = pltpu.roll(rows, 0, 1, stride=1, stride_axis=0)
    rolled = spread_ref[...].astype(bf16)
    wide = dot(rolled, onehot)
    lane = lax.broadcasted_iota(jnp.int32, (16, 256), 1)
    hidden = lane > GRID * GRID
    for h in range(heads):
        bias_ref[h, 192:ROWS, :] = jnp.where(hidden, -1e30, 0.0)
        own = wide[h * 16 : (h + 1) * 16, :]
        to_class = table_ref[h : h + 1, inner + 1 : inner + 2]
        for y in range(GRID):
            part = pltpu.roll(own, (1 - GRID * (GRID - 1 - y)) % SPREAD, 1)[:, :256]
            part = jnp.where(lane == 0, to_class, jnp.where(hidden, -1e30, part))
            bias_ref[h, 1 + GRID * y : 1 + GRID * (y + 1), :] = part[:GRID, :]
        from_class = table_ref[h : h + 1, inner : inner + 1]
        corner = table_ref[h : h + 1, inner + 2 : inner + 3]
        top = jnp.where(lane == 0, corner, jnp.where(hidden, -1e30, from_class))
        bias_ref[h, 0:1, :] = top[:1, :]


def forward_kernel(
    images,
    heads,
    tok_ref,
    cot_ref,
    vec_ref,
    mixing_in_ref,
    table_ref,
    mixing_out_ref,
    normed_ref,
    packed_ref,
    attend_ref,
    mixed_ref,
    branch_ref,
    middle_ref,
    n2_ref,
    bg_ref,
    tok_pad,
    spread_ref,
    bias_ref,
):
    width = tok_ref.shape[2]
    patches = tok_ref.shape[1]
    vec = lambda i: vec_ref[i : i + 1, :]
    expand_table(table_ref, spread_ref, bias_ref, heads)
    for n in range(images):
        lo = n * ROWS
        tok_pad[lo + 192 : lo + ROWS, :] = jnp.zeros((ROWS - 192, width), f32)
        tok_pad[lo : lo + patches, :] = tok_ref[n].astype(f32)
        bg_ref[lo + 192 : lo + ROWS, :] = jnp.zeros((ROWS - 192, width), bf16)
        bg_ref[lo : lo + patches, :] = (vec(SCALE_HIDDEN) * cot_ref[n].astype(f32)).astype(bf16)
    hat, _ = norm_parts(tok_pad[...])
    normed_ref[...] = (hat * vec(FIRST_GAIN) + vec(FIRST_SHIFT)).astype(bf16)
    for part in range(3):
        cols = slice(part * width, (part + 1) * width)
        value = dot(normed_ref[...], mixing_in_ref[:, cols])
        if part == 0:
            value = value + vec(QUERY_BIAS)
        if part == 2:
            value = value + vec(VALUE_BIAS)
        packed_ref[:, cols] = value.astype(bf16)
    first = lax.broadcasted_iota(jnp.int32, (1, 128), 1) < 64
    for n in range(images):
        rows = slice(n * ROWS, (n + 1) * ROWS)
        for pair in range(heads // 2):
            cols = [slice(k * width + pair * 128, k * width + (pair + 1) * 128) for k in range(3)]
            q, k, v = (packed_ref[rows, c] for c in cols)
            q = q * jnp.asarray(0.125, bf16)
            zero = jnp.zeros_like(q)
            outs = []
            for side in range(2):
                h = pair * 2 + side
                keep = first if side == 0 else jnp.logical_not(first)
                scores = dot(jnp.where(keep, q, zero), k, NT) + bias_ref[h, :, :ROWS]
                top = jnp.max(scores, axis=-1, keepdims=True)
                weights = jnp.exp(scores - top)
                total = jnp.sum(weights, axis=-1, keepdims=True)
                attend = (weights * (1.0 / total)).astype(bf16)
                attend_ref[n * heads + h] = attend
                outs.append(dot(attend, v))
            mixed_ref[rows, cols[0]] = jnp.where(first, outs[0], outs[1]).astype(bf16)
    branch = dot(mixed_ref[...], mixing_out_ref[...]) + vec(OUT_BIAS)
    branch_ref[...] = branch
    middle = tok_pad[...] + vec(SCALE_ATTENTION) * branch
    middle_ref[...] = middle
    hat, _ = norm_parts(middle)
    n2_ref[...] = (hat * vec(SECOND_GAIN) + vec(SECOND_SHIFT)).astype(bf16)


def gelu_and_slope(v):
    cdf = 0.5 * (1.0 + lax.erf(v * 0.7071067811865476))
    density = jnp.exp(-0.5 * v * v) * 0.3989422804014327
    return v * cdf, cdf + v * density


def hidden_kernel(
    last,
    core_ref,
    own_n2_ref,
    own_bg_ref,
    mate_n2_ref,
    mate_bg_ref,
    w1_ref,
    w2_ref,
    hb_ref,
    *rest,
):
    if last:
        (own_out_in, own_grad_in, mate_out_in, mate_grad_in) = rest[:4]
        rest = rest[4:]
    own_out, own_grad, mate_out, mate_grad, keep_ref, send_ref, hb_grad, act, slope_grad = rest
    width = w1_ref.shape[0]
    hidden = w1_ref.shape[1]
    count = own_n2_ref.shape[0]
    hb_sum = [jnp.zeros((1, 256), f32) for _ in range(hidden // 256)]
    for g, (n2, bg) in enumerate(((own_n2_ref, own_bg_ref), (mate_n2_ref, mate_bg_ref))):
        for f in range(hidden // 256):
            cols = slice(f * 256, (f + 1) * 256)
            before = dot(n2[...], w1_ref[:, cols]) + hb_ref[0:1, cols]
            value, slope = gelu_and_slope(before)
            act[g * count : (g + 1) * count, cols] = value.astype(bf16)
            low = (dot(bg[...], w2_ref[cols, :], NT) * slope).astype(bf16)
            slope_grad[g * count : (g + 1) * count, cols] = low
            hb_sum[f] = hb_sum[f] + jnp.sum(low.astype(f32), axis=0, keepdims=True)
    for f in range(hidden // 256):
        hb_grad[0:1, f * 256 : (f + 1) * 256] = hb_sum[f]
    for g, (out, grad) in enumerate(((own_out, own_grad), (mate_out, mate_grad))):
        rows = slice(g * count, (g + 1) * count)
        for f in range(width // 256):
            cols = slice(f * 256, (f + 1) * 256)
            value = dot(act[rows, :], w2_ref[:, cols])
            back = dot(slope_grad[rows, :], w1_ref[cols, :], NT)
            if last:
                value = value + (own_out_in, mate_out_in)[g][:, cols]
                back = back + (own_grad_in, mate_grad_in)[g][:, cols]
            out[:, cols] = value.astype(out.dtype)
            grad[:, cols] = back.astype(grad.dtype)

    def weights(first_ref, second_ref):
        for f in range(width // 256):
            cols = slice(f * 256, (f + 1) * 256)
            total = dot(own_n2_ref[:, cols], slope_grad[:count, :], TN)
            total = total + dot(mate_n2_ref[:, cols], slope_grad[count:, :], TN)
            first_ref[cols, :] = total.astype(bf16)
            total = dot(act[:count, cols], own_bg_ref[...], TN)
            total = total + dot(act[count:, cols], mate_bg_ref[...], TN)
            second_ref[cols, :] = total.astype(bf16)

    core = core_ref[0]

    @pl.when(core == 0)
    def _():
        weights(keep_ref, send_ref)

    @pl.when(core != 0)
    def _():
        weights(send_ref, keep_ref)


def result_kernel(images, patches, middle_ref, cot_ref, own_ref, recv_ref, vec_ref, result_ref, sums_ref):
    vec = lambda i: vec_ref[i : i + 1, :]
    scale_sum = jnp.zeros((1, middle_ref.shape[1]), f32)
    bias_sum = jnp.zeros((1, middle_ref.shape[1]), f32)
    for n in range(images):
        rows = slice(n * ROWS, n * ROWS + patches)
        cot = cot_ref[n].astype(f32)
        full = own_ref[rows, :] + recv_ref[rows, :].astype(f32) + vec(OUTPUT_BIAS)
        result_ref[n] = (middle_ref[rows, :] + vec(SCALE_HIDDEN) * full).astype(bf16)
        scale_sum = scale_sum + jnp.sum(cot * full, axis=0, keepdims=True)
        low = (vec(SCALE_HIDDEN) * cot).astype(bf16).astype(f32)
        bias_sum = bias_sum + jnp.sum(low, axis=0, keepdims=True)
    sums_ref[0:1, :] = bias_sum
    sums_ref[1:2, :] = scale_sum


def norm_back(grad, hat, rate, gain):
    scaled = grad * gain
    mean = jnp.mean(scaled, axis=-1, keepdims=True)
    cross = jnp.mean(scaled * hat, axis=-1, keepdims=True)
    return rate * (scaled - mean - hat * cross)


def backward_kernel(
    images,
    heads,
    patches,
    tok_ref,
    cot_ref,
    middle_ref,
    branch_ref,
    own_ref,
    recv_ref,
    mixed_ref,
    packed_ref,
    attend_ref,
    normed_ref,
    mixing_in_ref,
    mixing_out_ref,
    vec_ref,
    token_grad_ref,
    parts_ref,
    sums_ref,
    middle_grad,
    low_ref,
    mixed_grad,
    packed_grad,
    table_ref,
    spread_ref,
):
    width = tok_ref.shape[2]
    vec = lambda i: vec_ref[i : i + 1, :]
    column_sum = lambda v: jnp.sum(v, axis=0, keepdims=True)
    for n in range(images):
        rows = slice(n * ROWS, (n + 1) * ROWS)
        middle_grad[n * ROWS + 192 : (n + 1) * ROWS, :] = jnp.zeros((ROWS - 192, width), f32)
        middle_grad[n * ROWS : n * ROWS + patches, :] = cot_ref[n].astype(f32)
    sums = [jnp.zeros((1, width), f32) for _ in range(4)]
    for n in range(images):
        rows = slice(n * ROWS, (n + 1) * ROWS)
        grad = own_ref[rows, :] + recv_ref[rows, :].astype(f32)
        hat, rate = norm_parts(middle_ref[rows, :])
        sums[0] = sums[0] + column_sum(grad * hat)
        sums[1] = sums[1] + column_sum(grad)
        total = middle_grad[rows, :] + norm_back(grad, hat, rate, vec(SECOND_GAIN))
        middle_grad[rows, :] = total
        sums[2] = sums[2] + column_sum(total * branch_ref[rows, :])
        low = (vec(SCALE_ATTENTION) * total).astype(bf16)
        sums[3] = sums[3] + column_sum(low.astype(f32))
        low_ref[rows, :] = low
    table_ref[...] = jnp.zeros((ROWS, SPREAD), f32)
    spread_ref[...] = jnp.zeros(spread_ref.shape, f32)
    for i, at in enumerate((7, 8, 6, 5)):
        sums_ref[at : at + 1, :] = sums[i]
    mixed_grad[...] = dot(low_ref[...], mixing_out_ref[...], NT).astype(bf16)
    parts_ref[3] = dot(mixed_ref[...], low_ref[...], TN).astype(bf16)

    first = lax.broadcasted_iota(jnp.int32, (1, 128), 1) < 64
    lane = lax.broadcasted_iota(jnp.int32, (ROWS, ROWS), 1)
    row = lax.broadcasted_iota(jnp.int32, (ROWS, ROWS), 0)
    reach = 2 * GRID - 1
    inner = reach * reach
    lane_out = lax.broadcasted_iota(jnp.int32, (1, LANES), 1)
    class_rows = []
    for pair in range(heads // 2):
        cols = [slice(k * width + pair * 128, k * width + (pair + 1) * 128) for k in range(3)]
        totals = [None, None]
        for n in range(images):
            rows = slice(n * ROWS, (n + 1) * ROWS)
            q, k, v = (packed_ref[rows, c] for c in cols)
            back = mixed_grad[rows, cols[0]]
            zero = jnp.zeros_like(back)
            grads = []
            for side in range(2):
                h = pair * 2 + side
                keep = first if side == 0 else jnp.logical_not(first)
                attend = attend_ref[n * heads + h]
                wide = attend.astype(f32)
                attend_grad = dot(jnp.where(keep, back, zero), v, NT)
                carried = jnp.sum(wide * attend_grad, axis=-1, keepdims=True)
                low = (wide * (attend_grad - carried)).astype(bf16)
                totals[side] = low.astype(f32) if n == 0 else totals[side] + low.astype(f32)
                scaled = low * jnp.asarray(0.125, bf16)
                grads.append((dot(scaled, k), dot(scaled, q, TN), dot(attend, back, TN)))
            for i in range(3):
                packed_grad[rows, cols[i]] = jnp.where(first, grads[0][i], grads[1][i]).astype(bf16)
        for side in range(2):
            h = pair * 2 + side
            total = totals[side]
            top = total[0:1, :]
            corner = top[:, 0:1]
            from_class = jnp.sum(top, axis=-1, keepdims=True) - corner
            to_class = jnp.sum(total[:, 0:1], axis=0, keepdims=True) - corner
            class_rows.append(
                jnp.where(lane_out == inner, from_class, 0.0)
                + jnp.where(lane_out == inner + 1, to_class, 0.0)
                + jnp.where(lane_out == inner + 2, corner, 0.0)
            )
            inside = jnp.where(lane == 0, 0.0, total)
            table_ref[:, :ROWS] = inside
            gathered = jnp.zeros((GRID, SPREAD), f32)
            for y in range(GRID):
                part = table_ref[1 + GRID * y : 1 + GRID * (y + 1), :]
                shift = (GRID * (GRID - 1 - y) - 1) % SPREAD
                gathered = gathered + pltpu.roll(part, shift, 1)
            for x in range(GRID):
                spread_ref[x * 16 + h : x * 16 + h + 1, :] = gathered[x : x + 1, :]
    onehot = spread_onehot().astype(bf16)
    value = spread_ref[...]
    high = value.astype(bf16)
    rest = (value - high.astype(f32)).astype(bf16)
    spread = dot(high, onehot, NT) + dot(rest, onehot, NT)
    entries = jnp.zeros((16, LANES), f32)
    for x in range(GRID):
        part = spread[x * 16 : (x + 1) * 16, :]
        entries = entries + (pltpu.roll(part, LANES - x, 1) if x else part)
    for h in range(heads):
        sums_ref[11 + h : 12 + h, :] = entries[h : h + 1, :] + class_rows[h]
    for part in range(3):
        cols = slice(part * width, (part + 1) * width)
        parts_ref[part] = dot(normed_ref[...], packed_grad[:, cols], TN).astype(bf16)
    sums_ref[9:10, :] = column_sum(packed_grad[:, :width].astype(f32))
    sums_ref[10:11, :] = column_sum(packed_grad[:, 2 * width :].astype(f32))
    sums_ref[0:3, :] = jnp.zeros((3, width), f32)
    sums_ref[23:32, :] = jnp.zeros((9, width), f32)
    sums = [jnp.zeros((1, width), f32) for _ in range(2)]
    for n in range(images):
        rows = slice(n * ROWS, (n + 1) * ROWS)
        grad = dot(packed_grad[rows, :], mixing_in_ref[...], NT)
        mixed_grad_f = middle_grad[rows, :]
        low_ref[rows, :] = jnp.zeros((ROWS, width), bf16)
        low_ref[n * ROWS : n * ROWS + patches, :] = tok_ref[n]
        hat, rate = norm_parts(low_ref[rows, :].astype(f32))
        sums[0] = sums[0] + column_sum(grad * hat)
        sums[1] = sums[1] + column_sum(grad)
        total = mixed_grad_f + norm_back(grad, hat, rate, vec(FIRST_GAIN))
        token_grad_ref[n] = total[:patches, :].astype(bf16)
    sums_ref[3:4, :] = sums[0]
    sums_ref[4:5, :] = sums[1]


def per_device(
    n_dp,
    n_tp,
    tokens,
    first_gain,
    first_shift,
    mixing_in,
    query_bias,
    value_bias,
    relative_table,
    mixing_out,
    out_bias,
    scale_attention,
    second_gain,
    second_shift,
    hidden_in,
    hidden_bias,
    hidden_out,
    output_bias,
    scale_hidden,
    cotangent,
):
    images, patches, width = tokens.shape
    heads = relative_table.shape[1]
    count = images * ROWS
    hidden = hidden_in.shape[1]
    chips = n_dp // 2
    plane = [[2 * i + c for i in range(chips)] for c in range(2)]
    dp, tp = lax.axis_index("dp"), lax.axis_index("tp")
    core, chip = dp % 2, dp // 2
    mate = lambda a: lax.ppermute(a, "tp", [(i, i ^ 1) for i in range(n_tp)])
    far = lambda a: lax.ppermute(a, "tp", [(i, i ^ 2) for i in range(n_tp)])
    twin = lambda a: lax.ppermute(a, "dp", [(i, i ^ 1) for i in range(n_dp)])
    over_plane = lambda a: lax.all_to_all(a, "dp", 0, 0, axis_index_groups=plane, tiled=True)
    over_line = lambda a: lax.all_to_all(a, "tp", 0, 0, tiled=True)
    copies = lambda a, n: jnp.broadcast_to(a[None], (n, *a.shape))
    by_core = lambda a, b: (jnp.where(core == 0, a, b), jnp.where(core == 0, b, a))
    shape = jax.ShapeDtypeStruct

    slab = width // chips
    piece = lax.dynamic_slice_in_dim(jnp.where(core == 0, hidden_in, hidden_out), chip * slab, slab, 0)
    piece = jnp.concatenate([piece, jnp.broadcast_to(hidden_bias[None], (16, hidden))])
    piece = over_plane(copies(far(piece), chips))
    far_bias = piece[0, slab : slab + 1].astype(f32)
    piece = piece[:, :slab].reshape(width, hidden)
    far_in, far_out = by_core(piece, twin(piece))

    vecs = jnp.stack(
        [
            first_gain,
            first_shift,
            query_bias,
            value_bias,
            out_bias,
            scale_attention,
            second_gain,
            second_shift,
            output_bias,
            scale_hidden,
        ]
    ).astype(f32)
    inner = (2 * GRID - 1) ** 2
    table = relative_table.astype(f32)
    table = jnp.concatenate([table[:inner][::-1], table[inner:]]).T
    table = jnp.pad(table, ((0, 0), (0, LANES - table.shape[1])))

    rows = (count, width)
    normed, packed, attend, mixed, branch, middle, n2, bg = call(
        functools.partial(forward_kernel, images, heads),
        "attention_forward",
        [
            shape(rows, bf16),
            shape((count, 3 * width), bf16),
            shape((images * heads, ROWS, ROWS), bf16),
            shape(rows, bf16),
            shape(rows, f32),
            shape(rows, f32),
            shape(rows, bf16),
            shape(rows, bf16),
        ],
        [
            pltpu.VMEM(rows, f32),
            pltpu.VMEM((heads * 16, LANES), f32),
            pltpu.VMEM((heads, ROWS, 256), f32),
        ],
        flops=2.5e9,
    )(tokens, cotangent, vecs, mixing_in, table, mixing_out)

    mate_bg = mate(bg)
    mate_n2 = mate(n2)

    core_index = core.astype(jnp.int32).reshape(1)

    def hidden_call(last, w1, w2, bias, carried):
        args = (core_index, n2, bg, mate_n2, mate_bg, w1, w2, bias, *carried)
        kind = bf16 if last else f32
        outs = [
            shape(rows, f32),
            shape(rows, f32),
            shape(rows, kind),
            shape(rows, kind),
            shape((width, width), bf16),
            shape((width, width), bf16),
            shape((1, hidden), f32),
        ]
        spec = pl.BlockSpec(memory_space=pltpu.VMEM)
        return pl.pallas_call(
            functools.partial(hidden_kernel, last),
            out_shape=outs,
            in_specs=[pl.BlockSpec(memory_space=pltpu.SMEM)] + [spec] * (len(args) - 1),
            out_specs=tuple(spec for _ in outs),
            scratch_shapes=[
                pltpu.VMEM((2 * count, hidden), bf16),
                pltpu.VMEM((2 * count, hidden), bf16),
            ],
            name="hidden_last" if last else "hidden_first",
            compiler_params=pltpu.CompilerParams(vmem_limit_bytes=VMEM),
            cost_estimate=pl.CostEstimate(
                flops=int(12 * 2 * count * width * hidden), bytes_accessed=20_000_000, transcendentals=0
            ),
        )(*args)

    near_bias = hidden_bias.astype(f32)[None]
    *carried, keep_near, send_near, hb_near = hidden_call(False, hidden_in, hidden_out, near_bias, ())
    own_out, own_grad, mate_out, mate_grad, keep_far, send_far, hb_far = hidden_call(
        True, far_in, far_out, far_bias, carried
    )
    recv_grad = mate(mate_grad)
    recv_out = mate(mate_out)

    sent = twin(jnp.stack([send_near, send_far]))
    both = (jnp.stack([keep_near, keep_far]).astype(f32) + sent.astype(f32)).astype(bf16)
    both = both.reshape(2, chips, slab, width).transpose(1, 0, 2, 3)
    both = jnp.sum(over_plane(both).astype(f32), axis=0)
    share = (both[0] + far(both[1].astype(bf16)).astype(f32)).astype(bf16)
    whole = over_plane(copies(share, chips)).reshape(width, width)
    hidden_in_grad, hidden_out_grad = by_core(whole, twin(whole))

    result, sums_a = call(
        functools.partial(result_kernel, images, patches),
        "result",
        [shape(tokens.shape, bf16), shape((2, width), f32)],
    )(middle, cotangent, own_out, recv_out, vecs)

    token_grad, parts, sums_b = call(
        functools.partial(backward_kernel, images, heads, patches),
        "attention_backward",
        [shape(tokens.shape, bf16), shape((4, width, width), bf16), shape((32, width), f32)],
        [
            pltpu.VMEM(rows, f32),
            pltpu.VMEM(rows, bf16),
            pltpu.VMEM(rows, bf16),
            pltpu.VMEM((count, 3 * width), bf16),
            pltpu.VMEM((ROWS, SPREAD), f32),
            pltpu.VMEM((GRID * 16, SPREAD), f32),
        ],
        flops=6e9,
    )(
        tokens,
        cotangent,
        middle,
        branch,
        own_grad,
        recv_grad,
        mixed,
        packed,
        attend,
        normed,
        mixing_in,
        mixing_out,
        vecs,
    )
    place = lambda a, at: jnp.where(jnp.arange(n_tp)[:, None] == at, a, 0.0)
    hb = place(hb_near, tp) + place(hb_far, tp ^ 2)
    sums = jnp.concatenate([sums_b[:23], sums_a, hb, jnp.zeros((32 - 25 - n_tp, width), f32)])

    total = parts.shape[0] // 2 * width
    two = parts.reshape(2, total, width)
    keep, send = by_core(two[0], two[1])
    low_sums = sums.astype(bf16)
    got = twin(jnp.concatenate([send, low_sums]))
    half = (keep.astype(f32) + got[:total].astype(f32)).astype(bf16)
    sums = (sums + got[total:].astype(f32)).astype(bf16)
    got = over_plane(jnp.concatenate([half.reshape(chips, total // chips, width), copies(sums, chips)], axis=1))
    got = jnp.sum(got.astype(f32), axis=0).astype(bf16)
    per_chip, per_line = total // chips, total // chips // n_tp
    got = over_line(
        jnp.concatenate([got[:per_chip].reshape(n_tp, per_line, width), copies(got[per_chip:], n_tp)], axis=1)
    )
    got = jnp.sum(got.astype(f32), axis=0)
    sums = got[per_line:]
    got = over_line(copies(got[:per_line].astype(bf16), n_tp)).reshape(per_chip, width)
    got = over_plane(copies(got, chips)).reshape(total, width)
    low, high = by_core(got, twin(got))
    mixing_in_grad = jnp.concatenate([low[:width], low[width:], high[:width]], axis=1).astype(f32)
    mixing_out_grad = high[width:].astype(f32)

    table_grad = sums[11 : 11 + heads].T
    table_grad = jnp.concatenate([table_grad[:inner][::-1], table_grad[inner : relative_table.shape[0]]])
    hidden_bias_grad = lax.dynamic_index_in_dim(sums[25 : 25 + n_tp], tp, 0, keepdims=False)
    return (
        result,
        token_grad,
        sums[3],
        sums[4],
        mixing_in_grad,
        sums[9],
        sums[10],
        table_grad,
        mixing_out_grad,
        sums[5],
        sums[6],
        sums[7],
        sums[8],
        hidden_in_grad.astype(f32),
        hidden_bias_grad,
        hidden_out_grad.astype(f32),
        sums[23],
        sums[24],
    )


def solution(mesh):
    everywhere = P()
    rows = P("dp", "tp", None)
    hidden = (P(None, "tp"), P("tp"), P("tp", None))
    return jax.shard_map(
        functools.partial(per_device, mesh.shape["dp"], mesh.shape["tp"]),
        mesh=mesh,
        in_specs=(rows, *[everywhere] * 11, *hidden, everywhere, everywhere, rows),
        out_specs=(rows, rows, *[everywhere] * 11, *hidden, everywhere, everywhere),
        check_vma=False,
    )
```

```python
import functools

import jax
import jax.numpy as jnp
from jax import lax
from jax.experimental import pallas as pl
from jax.experimental.pallas import tpu as pltpu
from jax.sharding import PartitionSpec as P

GRID = 14
EPSILON = 1e-06
ROWS = 208
LANES = 768
SPREAD = 384
VMEM = 56 * 1024 * 1024

f32 = jnp.float32
bf16 = jnp.bfloat16

NN = (((1,), (0,)), ((), ()))
NT = (((1,), (1,)), ((), ()))
TN = (((0,), (0,)), ((), ()))

(
    FIRST_GAIN,
    FIRST_SHIFT,
    QUERY_BIAS,
    VALUE_BIAS,
    OUT_BIAS,
    SCALE_ATTENTION,
    SECOND_GAIN,
    SECOND_SHIFT,
    OUTPUT_BIAS,
    SCALE_HIDDEN,
) = range(10)


def dot(a, b, dims=NN):
    return lax.dot_general(a, b, dims, preferred_element_type=f32)


class Order:
    def __init__(self):
        self.last = None

    def tie(self, value):
        if self.last is not None:
            value, _ = lax.optimization_barrier((value, self.last))
        return value

    def step(self, value):
        self.last = value
        return value


US = {
    "attention_forward": 0.01,
    "hidden_near_own": 3,
    "hidden_near_mate": 1,
    "hidden_near_weights": 1,
    "hidden_far_mate": 3,
    "hidden_far_own": 0.01,
    "hidden_far_weights": 0.01,
    "backward_zero": 20,
    "sum_far": 20,
    "backward_one": 0.01,
    "backward_two": 5,
    "result": 0.01,
    "backward_three": 1,
}


def cost(us):
    return pl.CostEstimate(flops=int(us * 1.15e9), bytes_accessed=1000, transcendentals=0)


def call(kernel, name, outs, scratch=(), vmem=VMEM, scalars=0, **kw):
    def run(*args):
        return pl.pallas_call(
            kernel,
            out_shape=outs,
            in_specs=[pl.BlockSpec(memory_space=pltpu.SMEM)] * scalars
            + [pl.BlockSpec(memory_space=pltpu.VMEM)] * (len(args) - scalars),
            out_specs=tuple(pl.BlockSpec(memory_space=pltpu.VMEM) for _ in outs),
            scratch_shapes=scratch,
            name=name,
            compiler_params=pltpu.CompilerParams(vmem_limit_bytes=vmem),
            cost_estimate=cost(US.get(name, 1.0)),
            **kw,
        )(*args)

    return run


def norm_parts(values):
    center = values - jnp.mean(values, axis=-1, keepdims=True)
    spread = jnp.mean(center * center, axis=-1, keepdims=True)
    rate = lax.rsqrt(spread + EPSILON)
    return center * rate, rate


def spread_onehot():
    entry = lax.broadcasted_iota(jnp.int32, (LANES, SPREAD), 0)
    column = lax.broadcasted_iota(jnp.int32, (LANES, SPREAD), 1)
    d = lax.div(column, GRID)
    x = column - d * GRID
    return entry == d * (2 * GRID - 1) + x + GRID - 1


def expand_table(table_ref, spread_ref, bias_ref, heads):
    onehot = spread_onehot().astype(bf16)
    reach = 2 * GRID - 1
    inner = reach * reach
    for h in range(heads):
        rows = jnp.broadcast_to(table_ref[h : h + 1, :], (16, LANES))
        spread_ref[h * 16 : (h + 1) * 16, :] = pltpu.roll(rows, 0, 1, stride=1, stride_axis=0)
    rolled = spread_ref[...].astype(bf16)
    wide = dot(rolled, onehot)
    lane = lax.broadcasted_iota(jnp.int32, (16, 256), 1)
    hidden = lane > GRID * GRID
    for h in range(heads):
        bias_ref[h, 192:ROWS, :] = jnp.where(hidden, -1e30, 0.0)
        own = wide[h * 16 : (h + 1) * 16, :]
        to_class = table_ref[h : h + 1, inner + 1 : inner + 2]
        for y in range(GRID):
            part = pltpu.roll(own, (1 - GRID * (GRID - 1 - y)) % SPREAD, 1)[:, :256]
            part = jnp.where(lane == 0, to_class, jnp.where(hidden, -1e30, part))
            bias_ref[h, 1 + GRID * y : 1 + GRID * (y + 1), :] = part[:GRID, :]
        from_class = table_ref[h : h + 1, inner : inner + 1]
        corner = table_ref[h : h + 1, inner + 2 : inner + 3]
        top = jnp.where(lane == 0, corner, jnp.where(hidden, -1e30, from_class))
        bias_ref[h, 0:1, :] = top[:1, :]


def forward_kernel(
    images,
    heads,
    tok_ref,
    vec_ref,
    mixing_in_ref,
    table_ref,
    mixing_out_ref,
    normed_ref,
    packed_ref,
    attend_ref,
    mixed_ref,
    branch_ref,
    middle_ref,
    n2_ref,
    tok_pad,
    spread_ref,
    bias_ref,
):
    width = tok_ref.shape[2]
    patches = tok_ref.shape[1]
    vec = lambda i: vec_ref[i : i + 1, :]
    expand_table(table_ref, spread_ref, bias_ref, heads)
    for n in range(images):
        lo = n * ROWS
        tok_pad[lo + 192 : lo + ROWS, :] = jnp.zeros((ROWS - 192, width), f32)
        tok_pad[lo : lo + patches, :] = tok_ref[n].astype(f32)
    hat, _ = norm_parts(tok_pad[...])
    normed_ref[...] = (hat * vec(FIRST_GAIN) + vec(FIRST_SHIFT)).astype(bf16)
    for part in range(3):
        cols = slice(part * width, (part + 1) * width)
        value = dot(normed_ref[...], mixing_in_ref[:, cols])
        if part == 0:
            value = value + vec(QUERY_BIAS)
        if part == 2:
            value = value + vec(VALUE_BIAS)
        packed_ref[:, cols] = value.astype(bf16)
    first = lax.broadcasted_iota(jnp.int32, (1, 128), 1) < 64
    for n in range(images):
        rows = slice(n * ROWS, (n + 1) * ROWS)
        for pair in range(heads // 2):
            cols = [slice(k * width + pair * 128, k * width + (pair + 1) * 128) for k in range(3)]
            q, k, v = (packed_ref[rows, c] for c in cols)
            q = q * jnp.asarray(0.125, bf16)
            zero = jnp.zeros_like(q)
            outs = []
            for side in range(2):
                h = pair * 2 + side
                keep = first if side == 0 else jnp.logical_not(first)
                scores = dot(jnp.where(keep, q, zero), k, NT) + bias_ref[h, :, :ROWS]
                top = jnp.max(scores, axis=-1, keepdims=True)
                weights = jnp.exp(scores - top)
                total = jnp.sum(weights, axis=-1, keepdims=True)
                attend = (weights * (1.0 / total)).astype(bf16)
                attend_ref[n * heads + h] = attend
                outs.append(dot(attend, v))
            mixed_ref[rows, cols[0]] = jnp.where(first, outs[0], outs[1]).astype(bf16)
    branch = dot(mixed_ref[...], mixing_out_ref[...]) + vec(OUT_BIAS)
    branch_ref[...] = branch
    middle = tok_pad[...] + vec(SCALE_ATTENTION) * branch
    middle_ref[...] = middle
    hat, _ = norm_parts(middle)
    n2_ref[...] = (hat * vec(SECOND_GAIN) + vec(SECOND_SHIFT)).astype(bf16)


def gelu_and_slope(v):
    cdf = 0.5 * (1.0 + lax.erf(v * 0.7071067811865476))
    density = jnp.exp(-0.5 * v * v) * 0.3989422804014327
    return v * cdf, cdf + v * density


def hidden_rows_kernel(carried, n2_ref, bg_ref, w1_ref, w2_ref, hb_ref, *rest):
    if carried:
        out_in, grad_in = rest[:2]
        rest = rest[2:]
    act_ref, slope_ref, out_ref, grad_ref = rest
    width, hidden = w1_ref.shape
    for f in range(hidden // 256):
        cols = slice(f * 256, (f + 1) * 256)
        before = dot(n2_ref[...], w1_ref[:, cols]) + hb_ref[0:1, cols]
        value, slope = gelu_and_slope(before)
        act_ref[:, cols] = value.astype(bf16)
        slope_ref[:, cols] = (dot(bg_ref[...], w2_ref[cols, :], NT) * slope).astype(bf16)
    for f in range(width // 256):
        cols = slice(f * 256, (f + 1) * 256)
        value = dot(act_ref[...], w2_ref[:, cols])
        back = dot(slope_ref[...], w1_ref[cols, :], NT)
        if carried:
            value = value + out_in[:, cols]
            back = back + grad_in[:, cols]
        out_ref[:, cols] = value.astype(out_ref.dtype)
        grad_ref[:, cols] = back.astype(grad_ref.dtype)


def half_columns(ref, half):
    width = ref.shape[1] // 2
    return ref[:, pl.ds(pl.multiple_of(half * width, 128), width)]


def put_chips(ref, block, value):
    chips, rows = ref.shape[0], ref.shape[2]
    for j in range(chips):
        ref[j, block] = value[j * rows : (j + 1) * rows, :].astype(ref.dtype)


def hidden_weights_kernel(
    core_ref, n2_ref, bg_ref, act_ref, slope_ref, n2_mate, bg_mate, act_mate, slope_mate, keep_ref, send_ref, hb_ref
):
    core = core_ref[0]
    for ref, half in ((keep_ref, core), (send_ref, 1 - core)):
        total = dot(half_columns(n2_ref, half), slope_ref[...], TN)
        put_chips(ref, 0, total + dot(half_columns(n2_mate, half), slope_mate[...], TN))
        total = dot(half_columns(act_ref, half), bg_ref[...], TN)
        put_chips(ref, 1, total + dot(half_columns(act_mate, half), bg_mate[...], TN))
    total = jnp.sum(slope_ref[...].astype(f32), axis=0, keepdims=True)
    hb_ref[...] = total + jnp.sum(slope_mate[...].astype(f32), axis=0, keepdims=True)


def result_kernel(images, patches, middle_ref, cot_ref, own_ref, recv_ref, vec_ref, result_ref, sums_ref):
    vec = lambda i: vec_ref[i : i + 1, :]
    scale_sum = jnp.zeros((1, middle_ref.shape[1]), f32)
    bias_sum = jnp.zeros((1, middle_ref.shape[1]), f32)
    for n in range(images):
        rows = slice(n * ROWS, n * ROWS + patches)
        cot = cot_ref[n].astype(f32)
        full = own_ref[rows, :] + recv_ref[rows, :].astype(f32) + vec(OUTPUT_BIAS)
        result_ref[n] = (middle_ref[rows, :] + vec(SCALE_HIDDEN) * full).astype(bf16)
        scale_sum = scale_sum + jnp.sum(cot * full, axis=0, keepdims=True)
        low = (vec(SCALE_HIDDEN) * cot).astype(bf16).astype(f32)
        bias_sum = bias_sum + jnp.sum(low, axis=0, keepdims=True)
    sums_ref[0:1, :] = bias_sum
    sums_ref[1:2, :] = scale_sum


def norm_back(grad, hat, rate, gain):
    scaled = grad * gain
    mean = jnp.mean(scaled, axis=-1, keepdims=True)
    cross = jnp.mean(scaled * hat, axis=-1, keepdims=True)
    return rate * (scaled - mean - hat * cross)


def attention_part(
    images, heads, first_pair, pairs, packed_ref, attend_ref, mixed_grad, packed_grad, spread_ref, class_ref, table_ref
):
    width = mixed_grad.shape[1]
    part = pairs * 128
    first = lax.broadcasted_iota(jnp.int32, (1, 128), 1) < 64
    lane = lax.broadcasted_iota(jnp.int32, (ROWS, ROWS), 1)
    inner = (2 * GRID - 1) ** 2
    lane_out = lax.broadcasted_iota(jnp.int32, (1, LANES), 1)
    table_ref[...] = jnp.zeros(table_ref.shape, f32)
    spread_ref[...] = jnp.zeros(spread_ref.shape, f32)
    class_ref[...] = jnp.zeros(class_ref.shape, f32)
    for index in range(pairs):
        pair = first_pair + index
        cols = [slice(k * width + pair * 128, k * width + (pair + 1) * 128) for k in range(3)]
        outs = [slice(k * part + index * 128, k * part + (index + 1) * 128) for k in range(3)]
        totals = [None, None]
        for n in range(images):
            rows = slice(n * ROWS, (n + 1) * ROWS)
            q, k, v = (packed_ref[rows, c] for c in cols)
            back = mixed_grad[rows, cols[0]]
            zero = jnp.zeros_like(back)
            grads = []
            for side in range(2):
                h = pair * 2 + side
                keep = first if side == 0 else jnp.logical_not(first)
                attend = attend_ref[n * heads + h]
                wide = attend.astype(f32)
                attend_grad = dot(jnp.where(keep, back, zero), v, NT)
                carried = jnp.sum(wide * attend_grad, axis=-1, keepdims=True)
                low = (wide * (attend_grad - carried)).astype(bf16)
                totals[side] = low.astype(f32) if n == 0 else totals[side] + low.astype(f32)
                scaled = low * jnp.asarray(0.125, bf16)
                grads.append((dot(scaled, k), dot(scaled, q, TN), dot(attend, back, TN)))
            for i in range(3):
                packed_grad[rows, outs[i]] = jnp.where(first, grads[0][i], grads[1][i]).astype(bf16)
        for side in range(2):
            h = pair * 2 + side
            total = totals[side]
            top = total[0:1, :]
            corner = top[:, 0:1]
            from_class = jnp.sum(top, axis=-1, keepdims=True) - corner
            to_class = jnp.sum(total[:, 0:1], axis=0, keepdims=True) - corner
            class_ref[h : h + 1, :] = (
                jnp.where(lane_out == inner, from_class, 0.0)
                + jnp.where(lane_out == inner + 1, to_class, 0.0)
                + jnp.where(lane_out == inner + 2, corner, 0.0)
            )
            table_ref[:, :ROWS] = jnp.where(lane == 0, 0.0, total)
            gathered = jnp.zeros((GRID, SPREAD), f32)
            for y in range(GRID):
                block = table_ref[1 + GRID * y : 1 + GRID * (y + 1), :]
                gathered = gathered + pltpu.roll(block, (GRID * (GRID - 1 - y) - 1) % SPREAD, 1)
            for x in range(GRID):
                spread_ref[x * 16 + h : x * 16 + h + 1, :] = gathered[x : x + 1, :]


def backward_zero_kernel(
    images,
    patches,
    cot_ref,
    middle_ref,
    branch_ref,
    own_ref,
    recv_ref,
    mixing_out_ref,
    vec_ref,
    middle_grad,
    mixed_grad,
    low_ref,
    sums_ref,
):
    width = middle_ref.shape[1]
    vec = lambda i: vec_ref[i : i + 1, :]
    column_sum = lambda v: jnp.sum(v, axis=0, keepdims=True)
    for n in range(images):
        middle_grad[n * ROWS + 192 : (n + 1) * ROWS, :] = jnp.zeros((ROWS - 192, width), f32)
        middle_grad[n * ROWS : n * ROWS + patches, :] = cot_ref[n].astype(f32)
    sums = [jnp.zeros((1, width), f32) for _ in range(4)]
    for n in range(images):
        rows = slice(n * ROWS, (n + 1) * ROWS)
        grad = own_ref[rows, :] + recv_ref[rows, :].astype(f32)
        hat, rate = norm_parts(middle_ref[rows, :])
        sums[0] = sums[0] + column_sum(grad * hat)
        sums[1] = sums[1] + column_sum(grad)
        total = middle_grad[rows, :] + norm_back(grad, hat, rate, vec(SECOND_GAIN))
        middle_grad[rows, :] = total
        sums[2] = sums[2] + column_sum(total * branch_ref[rows, :])
        low = (vec(SCALE_ATTENTION) * total).astype(bf16)
        sums[3] = sums[3] + column_sum(low.astype(f32))
        low_ref[rows, :] = low
    for i, at in enumerate((2, 3, 1, 0)):
        sums_ref[at : at + 1, :] = sums[i]
    mixed_grad[...] = dot(low_ref[...], mixing_out_ref[...], NT).astype(bf16)


def backward_one_kernel(
    images,
    heads,
    pairs,
    core_ref,
    low_ref,
    mixed_grad,
    mixed_ref,
    packed_ref,
    attend_ref,
    normed_ref,
    packed_grad,
    spread_ref,
    class_ref,
    keep_ref,
    send_ref,
    table_ref,
):
    core = core_ref[0]
    attention_part(
        images, heads, 0, pairs, packed_ref, attend_ref, mixed_grad, packed_grad, spread_ref, class_ref, table_ref
    )
    part = pairs * 128
    for ref, half in ((keep_ref, core), (send_ref, 1 - core)):
        for b in range(2):
            put_chips(ref, b, dot(half_columns(mixed_ref, half), low_ref[:, b * part : (b + 1) * part], TN))
        for b in range(3):
            put_chips(ref, 2 + b, dot(half_columns(normed_ref, half), packed_grad[:, b * part : (b + 1) * part], TN))


def backward_two_kernel(
    images,
    heads,
    pairs,
    core_ref,
    mixed_grad,
    packed_ref,
    attend_ref,
    normed_ref,
    packed_grad,
    spread_ref,
    class_ref,
    keep_ref,
    send_ref,
    table_ref,
):
    core = core_ref[0]
    attention_part(
        images, heads, pairs, pairs, packed_ref, attend_ref, mixed_grad, packed_grad, spread_ref, class_ref, table_ref
    )
    part = pairs * 128
    for ref, half in ((keep_ref, core), (send_ref, 1 - core)):
        for b in range(3):
            put_chips(ref, b, dot(half_columns(normed_ref, half), packed_grad[:, b * part : (b + 1) * part], TN))


def backward_three_kernel(
    images,
    heads,
    patches,
    tok_ref,
    middle_grad,
    grad_one,
    grad_two,
    spread_one,
    spread_two,
    class_one,
    class_two,
    sums_one,
    mixing_in_ref,
    vec_ref,
    token_grad_ref,
    sums_ref,
    packed_grad,
    tok_pad,
):
    width = tok_ref.shape[2]
    part = width // 2
    vec = lambda i: vec_ref[i : i + 1, :]
    column_sum = lambda v: jnp.sum(v, axis=0, keepdims=True)
    for b in range(3):
        packed_grad[:, b * width : b * width + part] = grad_one[:, b * part : (b + 1) * part]
        packed_grad[:, b * width + part : (b + 1) * width] = grad_two[:, b * part : (b + 1) * part]
    onehot = spread_onehot().astype(bf16)
    value = spread_one[...] + spread_two[...]
    high = value.astype(bf16)
    rest = (value - high.astype(f32)).astype(bf16)
    spread = dot(high, onehot, NT) + dot(rest, onehot, NT)
    entries = class_one[...] + class_two[...]
    for x in range(GRID):
        block = spread[x * 16 : (x + 1) * 16, :]
        entries = entries + (pltpu.roll(block, LANES - x, 1) if x else block)
    sums_ref[8:24, :] = entries
    sums_ref[0:4, :] = sums_one[0:4, :]
    sums_ref[6:7, :] = column_sum(packed_grad[:, :width].astype(f32))
    sums_ref[7:8, :] = column_sum(packed_grad[:, 2 * width :].astype(f32))
    sums = [jnp.zeros((1, width), f32) for _ in range(2)]
    for n in range(images):
        rows = slice(n * ROWS, (n + 1) * ROWS)
        grad = dot(packed_grad[rows, :], mixing_in_ref[...], NT)
        tok_pad[192:ROWS, :] = jnp.zeros((ROWS - 192, width), f32)
        tok_pad[:patches, :] = tok_ref[n].astype(f32)
        hat, rate = norm_parts(tok_pad[...])
        sums[0] = sums[0] + column_sum(grad * hat)
        sums[1] = sums[1] + column_sum(grad)
        total = middle_grad[rows, :] + norm_back(grad, hat, rate, vec(FIRST_GAIN))
        token_grad_ref[n] = total[:patches, :].astype(bf16)
    sums_ref[4:5, :] = sums[0]
    sums_ref[5:6, :] = sums[1]


def sum_kernel(parts_ref, total_ref):
    total = parts_ref[0].astype(f32)
    for j in range(1, parts_ref.shape[0]):
        total = total + parts_ref[j].astype(f32)
    total_ref[...] = total.astype(bf16)


def hidden_final_kernel(core_ref, mine_ref, recv_ref, in_ref, out_ref):
    core = core_ref[0]
    chips, _, rows, _ = mine_ref.shape
    for ref, half in ((mine_ref, core), (recv_ref, 1 - core)):
        for j in range(chips):
            in_ref[half, j * rows : (j + 1) * rows, :] = ref[j, 0].astype(f32)
            out_ref[half, j * rows : (j + 1) * rows, :] = ref[j, 1].astype(f32)


def mixing_one_kernel(core_ref, mine_ref, recv_ref, mine_out, recv_out, in_ref, out_ref):
    core = core_ref[0]
    chips, _, rows, part = mine_ref.shape
    first = pl.program_id(0) == 0
    for ref, outer, half in ((mine_ref, mine_out, core), (recv_ref, recv_out, 1 - core)):
        for j in range(chips):
            in_ref[half, j * rows : (j + 1) * rows, :] = ref[j, 0].astype(f32)

        @pl.when(first)
        def _(outer=outer, half=half):
            for j in range(chips):
                for b in range(2):
                    out_ref[half, j * rows : (j + 1) * rows, b * part : (b + 1) * part] = outer[j, b].astype(f32)


def mixing_two_kernel(core_ref, before_ref, mine_ref, recv_ref, in_ref):
    core = core_ref[0]
    chips, _, rows, _ = mine_ref.shape
    for ref, half in ((mine_ref, core), (recv_ref, 1 - core)):
        for j in range(chips):
            in_ref[half, j * rows : (j + 1) * rows, :] = ref[j, 0].astype(f32)


def per_device(
    n_dp,
    n_tp,
    tokens,
    first_gain,
    first_shift,
    mixing_in,
    query_bias,
    value_bias,
    relative_table,
    mixing_out,
    out_bias,
    scale_attention,
    second_gain,
    second_shift,
    hidden_in,
    hidden_bias,
    hidden_out,
    output_bias,
    scale_hidden,
    cotangent,
):
    images, patches, width = tokens.shape
    heads = relative_table.shape[1]
    count = images * ROWS
    hidden = hidden_in.shape[1]
    chips = n_dp // 2
    half = width // 2
    pairs = heads // 4
    plane = [[2 * i + c for i in range(chips)] for c in range(2)]
    dp, tp = lax.axis_index("dp"), lax.axis_index("tp")
    core, chip = dp % 2, dp // 2
    mate = lambda a: lax.ppermute(a, "tp", [(i, i ^ 1) for i in range(n_tp)])
    far = lambda a: lax.ppermute(a, "tp", [(i, i ^ 2) for i in range(n_tp)])
    twin = lambda a: lax.ppermute(a, "dp", [(i, i ^ 1) for i in range(n_dp)])
    over_plane = lambda a: lax.all_to_all(a, "dp", 0, 0, axis_index_groups=plane, tiled=True)
    over_line = lambda a: lax.all_to_all(a, "tp", 0, 0, tiled=True)
    copies = lambda a, n: jnp.broadcast_to(a[None], (n, *a.shape))
    by_core = lambda a, b: (jnp.where(core == 0, a, b), jnp.where(core == 0, b, a))
    add = lambda a, b: (a.astype(f32) + b.astype(f32)).astype(bf16)
    total = lambda a: jnp.sum(a.astype(f32), axis=0)
    shape = jax.ShapeDtypeStruct
    core_index = core.astype(jnp.int32).reshape(1)
    rows = (count, width)

    order = Order()
    tie, step = order.tie, order.step

    slab = width // chips
    piece = lax.dynamic_slice_in_dim(jnp.where(core == 0, hidden_in, hidden_out), chip * slab, slab, 0)
    piece = jnp.concatenate([piece, jnp.broadcast_to(hidden_bias[None], (16, hidden))])
    far_piece = far(step(piece))
    bg = (scale_hidden.astype(f32) * tie(cotangent).astype(f32)).astype(bf16)
    bg = step(jnp.pad(bg, ((0, 0), (0, ROWS - patches), (0, 0))).reshape(rows))
    bg_mate = mate(bg)

    vecs = jnp.stack(
        [
            first_gain,
            first_shift,
            query_bias,
            value_bias,
            out_bias,
            scale_attention,
            second_gain,
            second_shift,
            output_bias,
            scale_hidden,
        ]
    ).astype(f32)
    inner = (2 * GRID - 1) ** 2
    table = relative_table.astype(f32)
    table = jnp.concatenate([table[:inner][::-1], table[inner:]]).T
    table = jnp.pad(table, ((0, 0), (0, LANES - table.shape[1])))

    normed, packed, attend, mixed, branch, middle, n2 = call(
        functools.partial(forward_kernel, images, heads),
        "attention_forward",
        [
            shape(rows, bf16),
            shape((count, 3 * width), bf16),
            shape((images * heads, ROWS, ROWS), bf16),
            shape(rows, bf16),
            shape(rows, f32),
            shape(rows, f32),
            shape(rows, bf16),
        ],
        [
            pltpu.VMEM(rows, f32),
            pltpu.VMEM((heads * 16, LANES), f32),
            pltpu.VMEM((heads, ROWS, 256), f32),
        ],
    )(tokens, tie(vecs), mixing_in, table, mixing_out)

    n2_mate = mate(step(n2))
    pieces = over_plane(step(copies(tie(far_piece), chips)))

    def hidden_rows(name, n2, bg, w1, w2, bias, carried, kind):
        return call(
            functools.partial(hidden_rows_kernel, bool(carried)),
            name,
            [shape((count, hidden), bf16), shape((count, hidden), bf16), shape(rows, kind), shape(rows, kind)],
        )(n2, bg, w1, w2, tie(bias), *carried)

    def hidden_weights(name, own, other):
        out = shape((chips, 2, half // chips, width), bf16)
        return call(
            hidden_weights_kernel,
            name,
            [out, out, shape((1, hidden), f32)],
            scalars=1,
        )(tie(core_index), *own, *other)

    near_bias = hidden_bias.astype(f32)[None]
    bg_mate = step(tie(bg_mate))
    act_no, slope_no, out_own, grad_own = hidden_rows(
        "hidden_near_own", n2, bg, hidden_in, hidden_out, near_bias, (), f32
    )
    step(act_no)
    act_nm, slope_nm, out_mate, grad_mate = hidden_rows(
        "hidden_near_mate", n2_mate, bg_mate, hidden_in, hidden_out, near_bias, (), f32
    )
    step(act_nm)
    pieces = tie(pieces)
    far_bias = pieces[0, slab : slab + 1].astype(f32)
    pieces = step(pieces[:, :slab].reshape(width, hidden))
    other_pieces = twin(pieces)
    keep_near, send_near, hb_near = hidden_weights(
        "hidden_near_weights", (n2, bg, act_no, slope_no), (n2_mate, bg_mate, act_nm, slope_nm)
    )
    recv_near = twin(step(send_near))
    far_in, far_out = by_core(pieces, tie(other_pieces))
    act_fm, slope_fm, out_mate, grad_mate = hidden_rows(
        "hidden_far_mate", n2_mate, bg_mate, far_in, far_out, far_bias, (out_mate, grad_mate), bf16
    )
    grad_recv = mate(step(grad_mate))
    share_near = over_plane(step(add(keep_near, tie(recv_near))))
    act_fo, slope_fo, out_own, grad_own = hidden_rows(
        "hidden_far_own", n2, bg, far_in, far_out, far_bias, (out_own, grad_own), f32
    )
    out_recv = mate(step(out_mate))
    step(act_fo)
    keep_far, send_far, hb_far = hidden_weights(
        "hidden_far_weights", (n2, bg, act_fo, slope_fo), (n2_mate, bg_mate, act_fm, slope_fm)
    )
    recv_far = twin(step(send_far))

    part = pairs * 128
    chip_rows = half // chips
    spread, classes = shape((GRID * 16, SPREAD), f32), shape((16, LANES), f32)
    share_near = step(tie(share_near))
    middle_grad, mixed_grad, attention_grad, sums_one = call(
        functools.partial(backward_zero_kernel, images, patches),
        "backward_zero",
        [shape(rows, f32), shape(rows, bf16), shape(rows, bf16), shape((4, width), f32)],
    )(cotangent, middle, branch, grad_own, grad_recv, mixing_out, tie(vecs))
    step(attention_grad)
    share_far = over_plane(step(add(keep_far, tie(recv_far))))
    packed_one, spread_one, class_one, keep_one, send_one = call(
        functools.partial(backward_one_kernel, images, heads, pairs),
        "backward_one",
        [
            shape((count, 3 * part), bf16),
            spread,
            classes,
            shape((chips, 5, chip_rows, part), bf16),
            shape((chips, 5, chip_rows, part), bf16),
        ],
        [pltpu.VMEM((ROWS, SPREAD), f32)],
        scalars=1,
    )(tie(core_index), attention_grad, mixed_grad, mixed, packed, attend, normed)
    recv_one = twin(step(send_one))
    out_recv = step(tie(out_recv))
    packed_two, spread_two, class_two, keep_two, send_two = call(
        functools.partial(backward_two_kernel, images, heads, pairs),
        "backward_two",
        [
            shape((count, 3 * part), bf16),
            spread,
            classes,
            shape((chips, 3, chip_rows, part), bf16),
            shape((chips, 3, chip_rows, part), bf16),
        ],
        [pltpu.VMEM((ROWS, SPREAD), f32)],
        scalars=1,
    )(tie(core_index), mixed_grad, packed, attend, normed)
    recv_two = twin(step(send_two))
    (share_far_low,) = call(sum_kernel, "sum_far", [shape((2, chip_rows, width), bf16)])(
        tie(share_far).reshape(chips, 2, chip_rows, width)
    )
    share_far_low = far(step(share_far_low))
    one = over_plane(step(add(keep_one, tie(recv_one))))
    result, sums_out = call(
        functools.partial(result_kernel, images, patches),
        "result",
        [shape(tokens.shape, bf16), shape((2, width), f32)],
    )(middle, cotangent, out_own, out_recv, tie(vecs))
    step(sums_out)
    token_grad, sums = call(
        functools.partial(backward_three_kernel, images, heads, patches),
        "backward_three",
        [shape(tokens.shape, bf16), shape((24, width), f32)],
        [pltpu.VMEM((count, 3 * width), bf16), pltpu.VMEM((ROWS, width), f32)],
    )(
        tokens,
        middle_grad,
        packed_one,
        packed_two,
        spread_one,
        spread_two,
        class_one,
        class_two,
        sums_one,
        mixing_in,
        tie(vecs),
    )
    place = lambda a, at: jnp.where(jnp.arange(n_tp)[:, None] == at, a, 0.0)
    hb = place(hb_near, tp) + place(hb_far, tp ^ 2)
    sums = jnp.concatenate([sums, sums_out, hb, jnp.zeros((32 - 26 - n_tp, width), f32)])
    sums = step(jnp.concatenate([sums[:, :half], sums[:, half:]]).astype(bf16))
    two = add(keep_two, tie(recv_two)).reshape(chips, 3 * chip_rows, part)
    two = step(jnp.concatenate([two, copies(sums, chips)], axis=1))
    one = step(tie(one))
    two = over_plane(two)
    one = step(total(one).astype(bf16))
    one_near = mate(one)
    share = step(copies(add(total(share_near), tie(share_far_low)), chips))
    one = step(add(one, tie(one_near)))
    one_far = far(one)
    two = step(tie(two))
    hidden_mine = over_plane(share)
    two = step(total(two).astype(bf16))
    two_near = mate(two)
    one = step(copies(add(one, tie(one_far)), chips))
    two = step(add(two, tie(two_near)))
    two_far = far(two)
    hidden_mine = step(tie(hidden_mine)).reshape(chips, 2, chip_rows, width)
    hidden_recv = twin(hidden_mine)
    one = over_plane(one)
    two = two.astype(f32) + tie(two_far).astype(f32)
    sums = step(two[3 * chip_rows :])
    sums_recv = twin(sums)
    two = step(copies(two[: 3 * chip_rows].astype(bf16), chips))
    hidden_in_grad, hidden_out_grad = call(
        hidden_final_kernel,
        "hidden_final",
        [shape((2, half, width), f32)] * 2,
        scalars=1,
    )(tie(core_index), hidden_mine, hidden_recv)
    step(hidden_in_grad)
    one = step(tie(one)).reshape(keep_one.shape)
    two = over_plane(two)
    one_recv = twin(one)
    sums = sums + tie(sums_recv)
    sums = step(jnp.concatenate([sums[: sums.shape[0] // 2], sums[sums.shape[0] // 2 :]], axis=1))
    scalar = pl.BlockSpec(memory_space=pltpu.SMEM)
    third = (chips, 1, chip_rows, part)
    params = pltpu.CompilerParams(vmem_limit_bytes=VMEM)
    in_shape, out_shape = shape((2, half, 3 * width), f32), shape((2, half, width), f32)
    mixing_in_grad, mixing_out_grad = pl.pallas_call(
        mixing_one_kernel,
        grid=(3,),
        out_shape=(in_shape, out_shape),
        in_specs=[scalar]
        + [pl.BlockSpec(third, lambda b: (0, 2 + b, 0, 0))] * 2
        + [pl.BlockSpec((chips, 2, chip_rows, part), lambda b: (0, 0, 0, 0))] * 2,
        out_specs=(
            pl.BlockSpec((2, half, part), lambda b: (0, 0, 2 * b)),
            pl.BlockSpec((2, half, width), lambda b: (0, 0, 0)),
        ),
        name="mixing_one",
        compiler_params=params,
        cost_estimate=cost(1.0),
    )(tie(core_index), one, one_recv, one, one_recv)
    step(mixing_out_grad)
    two = two.reshape(keep_two.shape)
    two = tie(two)
    mixing_in_grad = pl.pallas_call(
        mixing_two_kernel,
        grid=(3,),
        out_shape=in_shape,
        in_specs=[scalar, pl.BlockSpec(memory_space=pl.ANY)] + [pl.BlockSpec(third, lambda b: (0, b, 0, 0))] * 2,
        out_specs=pl.BlockSpec((2, half, part), lambda b: (0, 0, 2 * b + 1)),
        input_output_aliases={1: 0},
        name="mixing_two",
        compiler_params=params,
        cost_estimate=cost(1.0),
    )(core_index, mixing_in_grad, two, twin(two))

    table_grad = sums[8 : 8 + heads].T
    table_grad = jnp.concatenate([table_grad[:inner][::-1], table_grad[inner : relative_table.shape[0]]])
    hidden_bias_grad = lax.dynamic_index_in_dim(sums[26 : 26 + n_tp], tp, 0, keepdims=False)
    return (
        result,
        token_grad,
        sums[4],
        sums[5],
        mixing_in_grad.reshape(width, 3 * width),
        sums[6],
        sums[7],
        table_grad,
        mixing_out_grad.reshape(width, width),
        sums[0],
        sums[1],
        sums[2],
        sums[3],
        hidden_in_grad.reshape(width, width),
        hidden_bias_grad,
        hidden_out_grad.reshape(width, width),
        sums[24],
        sums[25],
    )


def solution(mesh):
    everywhere = P()
    rows = P("dp", "tp", None)
    hidden = (P(None, "tp"), P("tp"), P("tp", None))
    return jax.shard_map(
        functools.partial(per_device, mesh.shape["dp"], mesh.shape["tp"]),
        mesh=mesh,
        in_specs=(rows, *[everywhere] * 11, *hidden, everywhere, everywhere, rows),
        out_specs=(rows, rows, *[everywhere] * 11, *hidden, everywhere, everywhere),
        check_vma=False,
    )
```

```python
import functools

import jax
import jax.numpy as jnp
from jax import lax
from jax.experimental import pallas as pl
from jax.experimental.pallas import tpu as pltpu
from jax.sharding import PartitionSpec as P

GRID = 14
EPSILON = 1e-06
ROWS = 208
LANES = 768
SPREAD = 384
VMEM = 56 * 1024 * 1024
SMALL = 8 * 1024 * 1024
LIGHT = ("add", "sum", "share", "last", "spread")

f32 = jnp.float32
bf16 = jnp.bfloat16

NN = (((1,), (0,)), ((), ()))
NT = (((1,), (1,)), ((), ()))
TN = (((0,), (0,)), ((), ()))

(
    FIRST_GAIN,
    FIRST_SHIFT,
    QUERY_BIAS,
    VALUE_BIAS,
    OUT_BIAS,
    SCALE_ATTENTION,
    SECOND_GAIN,
    SECOND_SHIFT,
    OUTPUT_BIAS,
    SCALE_HIDDEN,
) = range(10)


def dot(a, b, dims=NN):
    return lax.dot_general(a, b, dims, preferred_element_type=f32)


class Order:
    def __init__(self):
        self.last = None

    def tie(self, value):
        if self.last is not None:
            value, _ = lax.optimization_barrier((value, self.last))
        return value

    def step(self, value):
        self.last = value
        return value


US = {
    "hidden_near_own": 3,
    "hidden_near_mate": 1,
    "hidden_near_weights": 1,
    "hidden_far_mate": 3,
    "backward_zero": 20,
    "backward_three": 20,
    "sum_hidden": 20,
    "sum_two": 20,
    "sum_one": 20,
    "hidden_final": 20,
    "mixing_one": 20,
}


def cost(us):
    return pl.CostEstimate(flops=int(us * 1.15e9), bytes_accessed=1000, transcendentals=0)


def call(kernel, name, outs, scratch=(), vmem=VMEM, scalars=0, **kw):
    def run(*args):
        return pl.pallas_call(
            kernel,
            out_shape=outs,
            in_specs=[pl.BlockSpec(memory_space=pltpu.SMEM)] * scalars
            + [pl.BlockSpec(memory_space=pltpu.VMEM)] * (len(args) - scalars),
            out_specs=tuple(pl.BlockSpec(memory_space=pltpu.VMEM) for _ in outs),
            scratch_shapes=scratch,
            name=name,
            compiler_params=pltpu.CompilerParams(vmem_limit_bytes=SMALL if name.split("_")[0] in LIGHT else VMEM),
            cost_estimate=cost(US.get(name, 0.01)),
            **kw,
        )(*args)

    return run


def norm_parts(values):
    center = values - jnp.mean(values, axis=-1, keepdims=True)
    spread = jnp.mean(center * center, axis=-1, keepdims=True)
    rate = lax.rsqrt(spread + EPSILON)
    return center * rate, rate


def spread_onehot():
    entry = lax.broadcasted_iota(jnp.int32, (LANES, SPREAD), 0)
    column = lax.broadcasted_iota(jnp.int32, (LANES, SPREAD), 1)
    d = lax.div(column, GRID)
    x = column - d * GRID
    return entry == d * (2 * GRID - 1) + x + GRID - 1


def expand_table(table_ref, spread_ref, bias_ref, heads):
    onehot = spread_onehot().astype(bf16)
    reach = 2 * GRID - 1
    inner = reach * reach
    for h in range(heads):
        rows = jnp.broadcast_to(table_ref[h : h + 1, :], (16, LANES))
        spread_ref[h * 16 : (h + 1) * 16, :] = pltpu.roll(rows, 0, 1, stride=1, stride_axis=0)
    rolled = spread_ref[...].astype(bf16)
    wide = dot(rolled, onehot)
    lane = lax.broadcasted_iota(jnp.int32, (16, 256), 1)
    hidden = lane > GRID * GRID
    for h in range(heads):
        bias_ref[h, 192:ROWS, :] = jnp.where(hidden, -1e30, 0.0)
        own = wide[h * 16 : (h + 1) * 16, :]
        to_class = table_ref[h : h + 1, inner + 1 : inner + 2]
        for y in range(GRID):
            part = pltpu.roll(own, (1 - GRID * (GRID - 1 - y)) % SPREAD, 1)[:, :256]
            part = jnp.where(lane == 0, to_class, jnp.where(hidden, -1e30, part))
            bias_ref[h, 1 + GRID * y : 1 + GRID * (y + 1), :] = part[:GRID, :]
        from_class = table_ref[h : h + 1, inner : inner + 1]
        corner = table_ref[h : h + 1, inner + 2 : inner + 3]
        top = jnp.where(lane == 0, corner, jnp.where(hidden, -1e30, from_class))
        bias_ref[h, 0:1, :] = top[:1, :]


def forward_kernel(
    images,
    heads,
    tok_ref,
    vec_ref,
    mixing_in_ref,
    table_ref,
    mixing_out_ref,
    normed_ref,
    packed_ref,
    attend_ref,
    mixed_ref,
    branch_ref,
    middle_ref,
    n2_ref,
    tok_pad,
    spread_ref,
    bias_ref,
):
    width = tok_ref.shape[2]
    patches = tok_ref.shape[1]
    vec = lambda i: vec_ref[i : i + 1, :]
    expand_table(table_ref, spread_ref, bias_ref, heads)
    for n in range(images):
        lo = n * ROWS
        tok_pad[lo + 192 : lo + ROWS, :] = jnp.zeros((ROWS - 192, width), f32)
        tok_pad[lo : lo + patches, :] = tok_ref[n].astype(f32)
    hat, _ = norm_parts(tok_pad[...])
    normed_ref[...] = (hat * vec(FIRST_GAIN) + vec(FIRST_SHIFT)).astype(bf16)
    for part in range(3):
        cols = slice(part * width, (part + 1) * width)
        value = dot(normed_ref[...], mixing_in_ref[:, cols])
        if part == 0:
            value = value + vec(QUERY_BIAS)
        if part == 2:
            value = value + vec(VALUE_BIAS)
        packed_ref[:, cols] = value.astype(bf16)
    first = lax.broadcasted_iota(jnp.int32, (1, 128), 1) < 64
    for n in range(images):
        rows = slice(n * ROWS, (n + 1) * ROWS)
        for pair in range(heads // 2):
            cols = [slice(k * width + pair * 128, k * width + (pair + 1) * 128) for k in range(3)]
            q, k, v = (packed_ref[rows, c] for c in cols)
            q = q * jnp.asarray(0.125, bf16)
            zero = jnp.zeros_like(q)
            outs = []
            for side in range(2):
                h = pair * 2 + side
                keep = first if side == 0 else jnp.logical_not(first)
                scores = dot(jnp.where(keep, q, zero), k, NT) + bias_ref[h, :, :ROWS]
                top = jnp.max(scores, axis=-1, keepdims=True)
                weights = jnp.exp(scores - top)
                total = jnp.sum(weights, axis=-1, keepdims=True)
                attend = (weights * (1.0 / total)).astype(bf16)
                attend_ref[n * heads + h] = attend
                outs.append(dot(attend, v))
            mixed_ref[rows, cols[0]] = jnp.where(first, outs[0], outs[1]).astype(bf16)
    branch = dot(mixed_ref[...], mixing_out_ref[...]) + vec(OUT_BIAS)
    branch_ref[...] = branch
    middle = tok_pad[...] + vec(SCALE_ATTENTION) * branch
    middle_ref[...] = middle
    hat, _ = norm_parts(middle)
    n2_ref[...] = (hat * vec(SECOND_GAIN) + vec(SECOND_SHIFT)).astype(bf16)


def gelu_and_slope(v):
    cdf = 0.5 * (1.0 + lax.erf(v * 0.7071067811865476))
    density = jnp.exp(-0.5 * v * v) * 0.3989422804014327
    return v * cdf, cdf + v * density


def hidden_rows_kernel(carried, n2_ref, bg_ref, w1_ref, w2_ref, hb_ref, *rest):
    if carried:
        out_in, grad_in = rest[:2]
        rest = rest[2:]
    act_ref, slope_ref, out_ref, grad_ref = rest
    width, hidden = w1_ref.shape
    for f in range(hidden // 256):
        cols = slice(f * 256, (f + 1) * 256)
        before = dot(n2_ref[...], w1_ref[:, cols]) + hb_ref[0:1, cols]
        value, slope = gelu_and_slope(before)
        act_ref[:, cols] = value.astype(bf16)
        slope_ref[:, cols] = (dot(bg_ref[...], w2_ref[cols, :], NT) * slope).astype(bf16)
    for f in range(width // 256):
        cols = slice(f * 256, (f + 1) * 256)
        value = dot(act_ref[...], w2_ref[:, cols])
        back = dot(slope_ref[...], w1_ref[cols, :], NT)
        if carried:
            value = value + out_in[:, cols]
            back = back + grad_in[:, cols]
        out_ref[:, cols] = value.astype(out_ref.dtype)
        grad_ref[:, cols] = back.astype(grad_ref.dtype)


def half_columns(ref, half):
    width = ref.shape[1] // 2
    return ref[:, pl.ds(pl.multiple_of(half * width, 128), width)]


def put_chips(ref, block, value):
    chips, rows = ref.shape[0], ref.shape[2]
    for j in range(chips):
        ref[j, block] = value[j * rows : (j + 1) * rows, :].astype(ref.dtype)


def hidden_weights_kernel(
    core_ref, n2_ref, bg_ref, act_ref, slope_ref, n2_mate, bg_mate, act_mate, slope_mate, keep_ref, send_ref, hb_ref
):
    core = core_ref[0]
    for ref, half in ((keep_ref, core), (send_ref, 1 - core)):
        total = dot(half_columns(n2_ref, half), slope_ref[...], TN)
        put_chips(ref, 0, total + dot(half_columns(n2_mate, half), slope_mate[...], TN))
        total = dot(half_columns(act_ref, half), bg_ref[...], TN)
        put_chips(ref, 1, total + dot(half_columns(act_mate, half), bg_mate[...], TN))
    total = jnp.sum(slope_ref[...].astype(f32), axis=0, keepdims=True)
    hb_ref[...] = total + jnp.sum(slope_mate[...].astype(f32), axis=0, keepdims=True)


def result_kernel(images, patches, middle_ref, cot_ref, own_ref, recv_ref, vec_ref, result_ref, sums_ref):
    vec = lambda i: vec_ref[i : i + 1, :]
    scale_sum = jnp.zeros((1, middle_ref.shape[1]), f32)
    bias_sum = jnp.zeros((1, middle_ref.shape[1]), f32)
    for n in range(images):
        rows = slice(n * ROWS, n * ROWS + patches)
        cot = cot_ref[n].astype(f32)
        full = own_ref[rows, :] + recv_ref[rows, :].astype(f32) + vec(OUTPUT_BIAS)
        result_ref[n] = (middle_ref[rows, :] + vec(SCALE_HIDDEN) * full).astype(bf16)
        scale_sum = scale_sum + jnp.sum(cot * full, axis=0, keepdims=True)
        low = (vec(SCALE_HIDDEN) * cot).astype(bf16).astype(f32)
        bias_sum = bias_sum + jnp.sum(low, axis=0, keepdims=True)
    sums_ref[0:1, :] = bias_sum
    sums_ref[1:2, :] = scale_sum


def norm_back(grad, hat, rate, gain):
    scaled = grad * gain
    mean = jnp.mean(scaled, axis=-1, keepdims=True)
    cross = jnp.mean(scaled * hat, axis=-1, keepdims=True)
    return rate * (scaled - mean - hat * cross)


def attention_back(
    images, heads, packed_ref, attend_ref, mixed_grad, packed_grad, spread_ref, class_ref, table_ref
):
    width = mixed_grad.shape[1]
    first = lax.broadcasted_iota(jnp.int32, (1, 128), 1) < 64
    lane = lax.broadcasted_iota(jnp.int32, (ROWS, ROWS), 1)
    inner = (2 * GRID - 1) ** 2
    lane_out = lax.broadcasted_iota(jnp.int32, (1, LANES), 1)
    table_ref[...] = jnp.zeros(table_ref.shape, f32)
    spread_ref[...] = jnp.zeros(spread_ref.shape, f32)
    class_ref[...] = jnp.zeros(class_ref.shape, f32)
    for pair in range(heads // 2):
        cols = [slice(k * width + pair * 128, k * width + (pair + 1) * 128) for k in range(3)]
        totals = [None, None]
        for n in range(images):
            rows = slice(n * ROWS, (n + 1) * ROWS)
            q, k, v = (packed_ref[rows, c] for c in cols)
            back = mixed_grad[rows, cols[0]]
            zero = jnp.zeros_like(back)
            grads = []
            for side in range(2):
                h = pair * 2 + side
                keep = first if side == 0 else jnp.logical_not(first)
                attend = attend_ref[n * heads + h]
                wide = attend.astype(f32)
                attend_grad = dot(jnp.where(keep, back, zero), v, NT)
                carried = jnp.sum(wide * attend_grad, axis=-1, keepdims=True)
                low = (wide * (attend_grad - carried)).astype(bf16)
                totals[side] = low.astype(f32) if n == 0 else totals[side] + low.astype(f32)
                scaled = low * jnp.asarray(0.125, bf16)
                grads.append((dot(scaled, k), dot(scaled, q, TN), dot(attend, back, TN)))
            for i in range(3):
                packed_grad[rows, cols[i]] = jnp.where(first, grads[0][i], grads[1][i]).astype(bf16)
        for side in range(2):
            h = pair * 2 + side
            total = totals[side]
            top = total[0:1, :]
            corner = top[:, 0:1]
            from_class = jnp.sum(top, axis=-1, keepdims=True) - corner
            to_class = jnp.sum(total[:, 0:1], axis=0, keepdims=True) - corner
            class_ref[h : h + 1, :] = (
                jnp.where(lane_out == inner, from_class, 0.0)
                + jnp.where(lane_out == inner + 1, to_class, 0.0)
                + jnp.where(lane_out == inner + 2, corner, 0.0)
            )
            table_ref[:, :ROWS] = jnp.where(lane == 0, 0.0, total)
            gathered = jnp.zeros((GRID, SPREAD), f32)
            for y in range(GRID):
                block = table_ref[1 + GRID * y : 1 + GRID * (y + 1), :]
                gathered = gathered + pltpu.roll(block, (GRID * (GRID - 1 - y) - 1) % SPREAD, 1)
            for x in range(GRID):
                spread_ref[x * 16 + h : x * 16 + h + 1, :] = gathered[x : x + 1, :]


def backward_zero_kernel(
    images,
    patches,
    cot_ref,
    middle_ref,
    branch_ref,
    own_ref,
    recv_ref,
    mixing_out_ref,
    vec_ref,
    middle_grad,
    mixed_grad,
    low_ref,
    sums_ref,
):
    width = middle_ref.shape[1]
    vec = lambda i: vec_ref[i : i + 1, :]
    column_sum = lambda v: jnp.sum(v, axis=0, keepdims=True)
    for n in range(images):
        middle_grad[n * ROWS + 192 : (n + 1) * ROWS, :] = jnp.zeros((ROWS - 192, width), f32)
        middle_grad[n * ROWS : n * ROWS + patches, :] = cot_ref[n].astype(f32)
    sums = [jnp.zeros((1, width), f32) for _ in range(4)]
    for n in range(images):
        rows = slice(n * ROWS, (n + 1) * ROWS)
        grad = own_ref[rows, :] + recv_ref[rows, :].astype(f32)
        hat, rate = norm_parts(middle_ref[rows, :])
        sums[0] = sums[0] + column_sum(grad * hat)
        sums[1] = sums[1] + column_sum(grad)
        total = middle_grad[rows, :] + norm_back(grad, hat, rate, vec(SECOND_GAIN))
        middle_grad[rows, :] = total
        sums[2] = sums[2] + column_sum(total * branch_ref[rows, :])
        low = (vec(SCALE_ATTENTION) * total).astype(bf16)
        sums[3] = sums[3] + column_sum(low.astype(f32))
        low_ref[rows, :] = low
    for i, at in enumerate((2, 3, 1, 0)):
        sums_ref[at : at + 1, :] = sums[i]
    mixed_grad[...] = dot(low_ref[...], mixing_out_ref[...], NT).astype(bf16)


def backward_one_kernel(
    images,
    heads,
    part,
    core_ref,
    low_ref,
    mixed_grad,
    mixed_ref,
    packed_ref,
    attend_ref,
    normed_ref,
    packed_grad,
    spread_ref,
    class_ref,
    keep_one,
    send_one,
    keep_two,
    send_two,
    table_ref,
):
    core = core_ref[0]
    attention_back(images, heads, packed_ref, attend_ref, mixed_grad, packed_grad, spread_ref, class_ref, table_ref)
    for one, two, half in ((send_one, send_two, 1 - core), (keep_one, keep_two, core)):
        for b in range(2):
            put_chips(one, b, dot(half_columns(mixed_ref, half), low_ref[:, b * part : (b + 1) * part], TN))
        for b in range(6):
            value = dot(half_columns(normed_ref, half), packed_grad[:, b * part : (b + 1) * part], TN)
            put_chips(two if b % 2 else one, b // 2 if b % 2 else 2 + b // 2, value)


def backward_three_kernel(
    images,
    heads,
    patches,
    tok_ref,
    middle_grad,
    packed_grad,
    spread_ref,
    class_ref,
    sums_one,
    mixing_in_ref,
    vec_ref,
    token_grad_ref,
    sums_ref,
    tok_pad,
):
    width = tok_ref.shape[2]
    vec = lambda i: vec_ref[i : i + 1, :]
    column_sum = lambda v: jnp.sum(v, axis=0, keepdims=True)
    onehot = spread_onehot().astype(bf16)
    value = spread_ref[...]
    high = value.astype(bf16)
    rest = (value - high.astype(f32)).astype(bf16)
    spread = dot(high, onehot, NT) + dot(rest, onehot, NT)
    entries = class_ref[...]
    for x in range(GRID):
        block = spread[x * 16 : (x + 1) * 16, :]
        entries = entries + (pltpu.roll(block, LANES - x, 1) if x else block)
    sums_ref[8:24, :] = entries
    sums_ref[0:4, :] = sums_one[0:4, :]
    sums_ref[6:7, :] = column_sum(packed_grad[:, :width].astype(f32))
    sums_ref[7:8, :] = column_sum(packed_grad[:, 2 * width :].astype(f32))
    sums = [jnp.zeros((1, width), f32) for _ in range(2)]
    for n in range(images):
        rows = slice(n * ROWS, (n + 1) * ROWS)
        grad = dot(packed_grad[rows, :], mixing_in_ref[...], NT)
        tok_pad[192:ROWS, :] = jnp.zeros((ROWS - 192, width), f32)
        tok_pad[:patches, :] = tok_ref[n].astype(f32)
        hat, rate = norm_parts(tok_pad[...])
        sums[0] = sums[0] + column_sum(grad * hat)
        sums[1] = sums[1] + column_sum(grad)
        total = middle_grad[rows, :] + norm_back(grad, hat, rate, vec(FIRST_GAIN))
        token_grad_ref[n] = total[:patches, :].astype(bf16)
    sums_ref[4:5, :] = sums[0]
    sums_ref[5:6, :] = sums[1]


def add_kernel(chip_ref, *refs):
    chip = chip_ref[0]
    chips = refs[0].shape[0]
    pairs, outs = refs[:-chips], refs[-chips:]
    for k, out in enumerate(outs):
        for i in range(0, len(pairs), 2):
            total = pairs[i][chip ^ k].astype(f32) + pairs[i + 1][chip ^ k].astype(f32)
            out[i // 2] = total.astype(bf16)


def add_two_kernel(keep_ref, recv_ref, out_ref):
    out_ref[...] = (keep_ref[...].astype(f32) + recv_ref[...].astype(f32)).astype(bf16)


def share_kernel(line_ref, near_ref, far_ref, sums_ref, out_sums_ref, hb_near, hb_far, out_ref, small):
    rows = near_ref.shape[1]
    for m in range(2):
        total = near_ref[m].astype(f32) + far_ref[m].astype(f32)
        out_ref[m * rows : (m + 1) * rows, :] = total.astype(bf16)
    count = sums_ref.shape[0]
    small[...] = jnp.zeros(small.shape, f32)
    small[0:count, :] = sums_ref[...]
    small[count : count + 2, :] = out_sums_ref[...]
    small[pl.ds(count + 2 + line_ref[0], 1), :] = hb_near[...]
    small[pl.ds(count + 2 + line_ref[1], 1), :] = hb_far[...]
    out_ref[2 * rows :, :] = small[...].astype(bf16)


def sum_sums_kernel(*refs):
    count = refs[-1].shape[0]
    at = slice(refs[0].shape[0] - count, refs[0].shape[0])
    total = refs[0][at, :].astype(f32)
    for ref in refs[1:-1]:
        total = total + ref[at, :].astype(f32)
    refs[-1][...] = total


def add_spread_kernel(one_ref, two_ref, out_ref):
    total = (one_ref[...].astype(f32) + two_ref[...].astype(f32)).astype(bf16)
    for j in range(out_ref.shape[0]):
        out_ref[j] = total


def sum_pair_kernel(*refs):
    count = (len(refs) - 2) // 2
    for parts, out in ((refs[:count], refs[-2]), (refs[count:-2], refs[-1])):
        total = parts[0][0].astype(f32)
        for ref in parts[1:]:
            total = total + ref[0].astype(f32)
        out[...] = total.astype(bf16)


def sum_all_kernel(parts_ref, total_ref):
    total = parts_ref[0].astype(f32)
    for j in range(1, parts_ref.shape[0]):
        total = total + parts_ref[j].astype(f32)
    total_ref[...] = total.astype(bf16)


def sum_kernel(*refs):
    total = refs[0][...].astype(f32)
    for ref in refs[1:-1]:
        total = total + ref[...].astype(f32)
    refs[-1][...] = total.astype(bf16)


def hidden_final_kernel(place_ref, *refs):
    core, chip = place_ref[0], place_ref[1]
    in_ref, out_ref = refs[-2:]
    chips = (len(refs) - 2) // 2
    for k in range(chips):
        for ref, half in ((refs[k], core), (refs[chips + k], 1 - core)):
            rows = in_ref.shape[2]
            in_ref[half, chip ^ k] = ref[:rows, :].astype(f32)
            out_ref[half, chip ^ k] = ref[rows : 2 * rows, :].astype(f32)


def mixing_one_kernel(place_ref, *refs):
    core, chip = place_ref[0], place_ref[1]
    in_ref, out_ref = refs[-2:]
    chips = (len(refs) - 2) // 4
    first = pl.program_id(0) == 0
    for k in range(chips):
        for ref, half in ((refs[k], core), (refs[chips + k], 1 - core)):
            in_ref[half, chip ^ k] = ref[0].astype(f32)

    @pl.when(first)
    def _():
        for k in range(chips):
            for ref, half in ((refs[2 * chips + k], core), (refs[3 * chips + k], 1 - core)):
                part = ref.shape[2]
                for b in range(2):
                    out_ref[half, chip ^ k, :, b * part : (b + 1) * part] = ref[b].astype(f32)


def mixing_two_kernel(place_ref, before_ref, mine_ref, recv_ref, in_ref):
    core = place_ref[0]
    for j in range(mine_ref.shape[0]):
        for ref, half in ((mine_ref, core), (recv_ref, 1 - core)):
            in_ref[half, j] = ref[j, 0].astype(f32)


def per_device(
    n_dp,
    n_tp,
    tokens,
    first_gain,
    first_shift,
    mixing_in,
    query_bias,
    value_bias,
    relative_table,
    mixing_out,
    out_bias,
    scale_attention,
    second_gain,
    second_shift,
    hidden_in,
    hidden_bias,
    hidden_out,
    output_bias,
    scale_hidden,
    cotangent,
):
    images, patches, width = tokens.shape
    heads = relative_table.shape[1]
    count = images * ROWS
    hidden = hidden_in.shape[1]
    chips = n_dp // 2
    half = width // 2
    part = half
    chip_rows = half // chips
    plane = [[2 * i + c for i in range(chips)] for c in range(2)]
    dp, tp = lax.axis_index("dp"), lax.axis_index("tp")
    core, chip = dp % 2, dp // 2
    mate = lambda a: lax.ppermute(a, "tp", [(i, i ^ 1) for i in range(n_tp)])
    far = lambda a: lax.ppermute(a, "tp", [(i, i ^ 2) for i in range(n_tp)])
    twin = lambda a: lax.ppermute(a, "dp", [(i, i ^ 1) for i in range(n_dp)])
    over_plane = lambda a: lax.all_to_all(a, "dp", 0, 0, axis_index_groups=plane, tiled=True)
    over_line = lambda a: lax.all_to_all(a, "tp", 0, 0, tiled=True)
    copies = lambda a, n: jnp.broadcast_to(a[None], (n, *a.shape))
    by_core = lambda a, b: (jnp.where(core == 0, a, b), jnp.where(core == 0, b, a))
    add = lambda a, b: (a.astype(f32) + b.astype(f32)).astype(bf16)
    def hop(value, k):
        return lax.ppermute(value, "dp", [(i, i ^ (2 * k)) for i in range(n_dp)])

    def to_chips(values):
        if chips <= 4:
            return [hop(value, k) for k, value in enumerate(values) if k]
        order = lambda a, k: lax.dynamic_index_in_dim(a, chip ^ k, 0, keepdims=False)
        stacked = jnp.stack(values)
        stacked = jnp.stack([order(stacked, j) for j in range(chips)])
        stacked = over_plane(stacked)
        return [order(stacked, k) for k in range(1, chips)]

    shape = jax.ShapeDtypeStruct
    core_index = core.astype(jnp.int32).reshape(1)
    chip_index = chip.astype(jnp.int32).reshape(1)
    place = jnp.concatenate([core_index, chip_index])
    rows = (count, width)

    order = Order()
    tie, step = order.tie, order.step

    slab = width // chips
    piece = lax.dynamic_slice_in_dim(jnp.where(core == 0, hidden_in, hidden_out), chip * slab, slab, 0)
    piece = jnp.concatenate([piece, jnp.broadcast_to(hidden_bias[None], (16, hidden))])
    far_piece = far(step(piece))
    bg = (scale_hidden.astype(f32) * tie(cotangent).astype(f32)).astype(bf16)
    bg = step(jnp.pad(bg, ((0, 0), (0, ROWS - patches), (0, 0))).reshape(rows))
    bg_mate = mate(bg)

    vecs = jnp.stack(
        [
            first_gain,
            first_shift,
            query_bias,
            value_bias,
            out_bias,
            scale_attention,
            second_gain,
            second_shift,
            output_bias,
            scale_hidden,
        ]
    ).astype(f32)
    inner = (2 * GRID - 1) ** 2
    table = relative_table.astype(f32)
    table = jnp.concatenate([table[:inner][::-1], table[inner:]]).T
    table = jnp.pad(table, ((0, 0), (0, LANES - table.shape[1])))

    normed, packed, attend, mixed, branch, middle, n2 = call(
        functools.partial(forward_kernel, images, heads),
        "attention_forward",
        [
            shape(rows, bf16),
            shape((count, 3 * width), bf16),
            shape((images * heads, ROWS, ROWS), bf16),
            shape(rows, bf16),
            shape(rows, f32),
            shape(rows, f32),
            shape(rows, bf16),
        ],
        [
            pltpu.VMEM(rows, f32),
            pltpu.VMEM((heads * 16, LANES), f32),
            pltpu.VMEM((heads, ROWS, 256), f32),
        ],
    )(tokens, tie(vecs), mixing_in, table, mixing_out)

    n2_mate = mate(step(n2))
    pieces = over_plane(step(copies(tie(far_piece), chips)))

    def hidden_rows(name, n2, bg, w1, w2, bias, carried, kind):
        return call(
            functools.partial(hidden_rows_kernel, bool(carried)),
            name,
            [shape((count, hidden), bf16), shape((count, hidden), bf16), shape(rows, kind), shape(rows, kind)],
        )(n2, bg, w1, w2, tie(bias), *carried)

    def hidden_weights(name, own, other):
        out = shape((chips, 2, half // chips, width), bf16)
        return call(
            hidden_weights_kernel,
            name,
            [out, out, shape((1, hidden), f32)],
            scalars=1,
        )(tie(core_index), *own, *other)

    near_bias = hidden_bias.astype(f32)[None]
    bg_mate = step(tie(bg_mate))
    act_no, slope_no, out_own, grad_own = hidden_rows(
        "hidden_near_own", n2, bg, hidden_in, hidden_out, near_bias, (), f32
    )
    step(act_no)
    act_nm, slope_nm, out_mate, grad_mate = hidden_rows(
        "hidden_near_mate", n2_mate, bg_mate, hidden_in, hidden_out, near_bias, (), f32
    )
    step(act_nm)
    pieces = tie(pieces)
    far_bias = pieces[0, slab : slab + 1].astype(f32)
    pieces = step(pieces[:, :slab].reshape(width, hidden))
    other_pieces = twin(pieces)
    keep_near, send_near, hb_near = hidden_weights(
        "hidden_near_weights", (n2, bg, act_no, slope_no), (n2_mate, bg_mate, act_nm, slope_nm)
    )
    recv_near = twin(step(send_near))
    far_in, far_out = by_core(pieces, tie(other_pieces))
    act_fm, slope_fm, out_mate, grad_mate = hidden_rows(
        "hidden_far_mate", n2_mate, bg_mate, far_in, far_out, far_bias, (out_mate, grad_mate), bf16
    )
    grad_recv = mate(step(grad_mate))
    block = shape((1, 2, chip_rows, width), bf16)
    nears = call(add_kernel, "add_near", [block] * chips, scalars=1)(tie(chip_index), keep_near, recv_near)
    step(nears[0])
    nears = [nears[0], *to_chips(nears)]
    act_fo, slope_fo, out_own, grad_own = hidden_rows(
        "hidden_far_own", n2, bg, far_in, far_out, far_bias, (out_own, grad_own), f32
    )
    out_recv = mate(step(out_mate))
    step(act_fo)
    keep_far, send_far, hb_far = hidden_weights(
        "hidden_far_weights", (n2, bg, act_fo, slope_fo), (n2_mate, bg_mate, act_fm, slope_fm)
    )
    recv_far = twin(step(send_far))

    spread, classes = shape((GRID * 16, SPREAD), f32), shape((16, LANES), f32)
    nears = [step(tie(a)) for a in nears]
    middle_grad, mixed_grad, attention_grad, sums_one = call(
        functools.partial(backward_zero_kernel, images, patches),
        "backward_zero",
        [shape(rows, f32), shape(rows, bf16), shape(rows, bf16), shape((4, width), f32)],
    )(cotangent, middle, branch, grad_own, grad_recv, mixing_out, tie(vecs))
    step(attention_grad)
    fars = call(add_kernel, "add_far", [block] * chips, scalars=1)(tie(chip_index), keep_far, recv_far)
    step(fars[0])
    fars = [fars[0], *to_chips(fars)]
    packed_grad, spread, classes, keep_one, send_one, keep_two, send_two = call(
        functools.partial(backward_one_kernel, images, heads, part),
        "backward_one",
        [
            shape((count, 3 * width), bf16),
            spread,
            classes,
            shape((chips, 5, chip_rows, part), bf16),
            shape((chips, 5, chip_rows, part), bf16),
            shape((chips, 3, chip_rows, part), bf16),
            shape((chips, 3, chip_rows, part), bf16),
        ],
        [pltpu.VMEM((ROWS, SPREAD), f32)],
        scalars=1,
    )(tie(core_index), attention_grad, mixed_grad, mixed, packed, attend, normed)
    step(send_one)
    recv_one = twin(send_one)
    recv_two = twin(send_two)
    result, sums_out = call(
        functools.partial(result_kernel, images, patches),
        "result",
        [shape(tokens.shape, bf16), shape((2, width), f32)],
    )(middle, cotangent, out_own, out_recv, tie(vecs))
    step(sums_out)
    share_near, share_far = call(sum_pair_kernel, "sum_hidden", [shape((2, chip_rows, width), bf16)] * 2)(
        *nears, tie(fars[0]), *fars[1:]
    )
    share_far = far(step(share_far))
    block = shape((1, 5, chip_rows, part), bf16)
    ones = call(add_kernel, "add_one", [block] * chips, scalars=1)(tie(chip_index), keep_one, recv_one)
    step(ones[0])
    ones = [ones[0], *to_chips(ones)]
    token_grad, sums = call(
        functools.partial(backward_three_kernel, images, heads, patches),
        "backward_three",
        [shape(tokens.shape, bf16), shape((24, width), f32)],
        [pltpu.VMEM((ROWS, width), f32)],
    )(
        tokens,
        middle_grad,
        packed_grad,
        spread,
        classes,
        sums_one,
        mixing_in,
        tie(vecs),
    )
    step(token_grad)
    two_shape = shape((3, chip_rows, part), bf16)
    (twos,) = call(add_two_kernel, "add_two", [shape(keep_two.shape, bf16)])(tie(keep_two), recv_two)
    twos = over_plane(step(twos))
    (one,) = call(sum_kernel, "sum_one", [block])(tie(ones[0]), *ones[1:])
    one_near = mate(step(one))
    line_index = jnp.stack([tp, tp ^ 2]).astype(jnp.int32)
    (share,) = call(
        share_kernel,
        "share",
        [shape((2 * chip_rows + 32, width), bf16)],
        [pltpu.VMEM((32, width), f32)],
        scalars=1,
    )(line_index, share_near, tie(share_far), sums, sums_out, hb_near, hb_far)
    step(share)
    share = [share, *to_chips([share] * chips)]
    (two,) = call(sum_all_kernel, "sum_two", [two_shape])(tie(twos))
    two_near = mate(step(two))
    (one,) = call(add_two_kernel, "add_line_one", [block])(one, tie(one_near))
    one_far = far(step(one))
    (two,) = call(add_two_kernel, "add_line_two", [two_shape])(two, tie(two_near))
    two_far = far(step(two))
    (sums,) = call(sum_sums_kernel, "sum_sums", [shape((32, width), f32)])(tie(share[0]), *share[1:])
    sums_near = mate(step(sums))
    share_recv = [twin(a) for a in share]
    (one,) = call(add_two_kernel, "last_one", [shape(block.shape[1:], bf16)])(one[0], tie(one_far)[0])
    step(one)
    one = [one, *to_chips([one] * chips)]
    wide = shape((2, chips, chip_rows, width), f32)
    hidden_in_grad, hidden_out_grad = call(hidden_final_kernel, "hidden_final", [wide, wide], scalars=1)(
        tie(place), *share, *share_recv
    )
    step(hidden_in_grad)
    (two,) = call(add_spread_kernel, "spread_two", [shape((chips, *two_shape.shape), bf16)])(two, tie(two_far))
    two = over_plane(step(two))
    one = [step(tie(a)) for a in one]
    one_recv = [twin(a) for a in one]
    sums = step(sums + tie(sums_near))
    sums_far = far(sums)
    scalar = pl.BlockSpec(memory_space=pltpu.SMEM)
    third = (1, chip_rows, part)
    params = pltpu.CompilerParams(vmem_limit_bytes=2 * SMALL)
    in_shape = shape((2, chips, chip_rows, 3 * width), f32)
    mixing_in_grad, mixing_out_grad = pl.pallas_call(
        mixing_one_kernel,
        grid=(3,),
        out_shape=(in_shape, wide),
        in_specs=[scalar]
        + [pl.BlockSpec(third, lambda b: (2 + b, 0, 0))] * (2 * chips)
        + [pl.BlockSpec((2, chip_rows, part), lambda b: (0, 0, 0))] * (2 * chips),
        out_specs=(
            pl.BlockSpec((2, chips, chip_rows, part), lambda b: (0, 0, 0, 2 * b)),
            pl.BlockSpec((2, chips, chip_rows, width), lambda b: (0, 0, 0, 0)),
        ),
        name="mixing_one",
        compiler_params=params,
        cost_estimate=cost(20),
    )(tie(place), *one, *one_recv, *one, *one_recv)
    step(mixing_out_grad)
    sums = step(sums + tie(sums_far))
    sums = sums + twin(sums)
    two = tie(two)
    mixing_in_grad = pl.pallas_call(
        mixing_two_kernel,
        grid=(3,),
        out_shape=in_shape,
        in_specs=[scalar, pl.BlockSpec(memory_space=pl.ANY)]
        + [pl.BlockSpec((chips, *third), lambda b: (0, b, 0, 0))] * 2,
        out_specs=pl.BlockSpec((2, chips, chip_rows, part), lambda b: (0, 0, 0, 2 * b + 1)),
        input_output_aliases={1: 0},
        name="mixing_two",
        compiler_params=params,
        cost_estimate=cost(0.01),
    )(place, mixing_in_grad, two, twin(two))

    table_grad = sums[8 : 8 + heads].T
    table_grad = jnp.concatenate([table_grad[:inner][::-1], table_grad[inner : relative_table.shape[0]]])
    hidden_bias_grad = lax.dynamic_index_in_dim(sums[26 : 26 + n_tp], tp, 0, keepdims=False)
    return (
        result,
        token_grad,
        sums[4],
        sums[5],
        mixing_in_grad.reshape(width, 3 * width),
        sums[6],
        sums[7],
        table_grad,
        mixing_out_grad.reshape(width, width),
        sums[0],
        sums[1],
        sums[2],
        sums[3],
        hidden_in_grad.reshape(width, width),
        hidden_bias_grad,
        hidden_out_grad.reshape(width, width),
        sums[24],
        sums[25],
    )


def solution(mesh):
    everywhere = P()
    rows = P("dp", "tp", None)
    hidden = (P(None, "tp"), P("tp"), P("tp", None))
    return jax.shard_map(
        functools.partial(per_device, mesh.shape["dp"], mesh.shape["tp"]),
        mesh=mesh,
        in_specs=(rows, *[everywhere] * 11, *hidden, everywhere, everywhere, rows),
        out_specs=(rows, rows, *[everywhere] * 11, *hidden, everywhere, everywhere),
        check_vma=False,
    )
```

```python
import functools

import jax
import jax.numpy as jnp
from jax import lax
from jax.experimental import pallas as pl
from jax.experimental.pallas import tpu as pltpu
from jax.sharding import PartitionSpec as P

GRID = 14
EPSILON = 1e-06
ROWS = 208
LANES = 768
SPREAD = 384
VMEM = 56 * 1024 * 1024
SMALL = 8 * 1024 * 1024
LIGHT = ("add", "sum", "share", "last", "spread")

f32 = jnp.float32
bf16 = jnp.bfloat16

NN = (((1,), (0,)), ((), ()))
NT = (((1,), (1,)), ((), ()))
TN = (((0,), (0,)), ((), ()))

(
    FIRST_GAIN,
    FIRST_SHIFT,
    QUERY_BIAS,
    VALUE_BIAS,
    OUT_BIAS,
    SCALE_ATTENTION,
    SECOND_GAIN,
    SECOND_SHIFT,
    OUTPUT_BIAS,
    SCALE_HIDDEN,
) = range(10)


def dot(a, b, dims=NN):
    return lax.dot_general(a, b, dims, preferred_element_type=f32)


class Order:
    def __init__(self):
        self.last = None

    def tie(self, value):
        if self.last is not None:
            value, _ = lax.optimization_barrier((value, self.last))
        return value

    def step(self, value):
        self.last = value
        return value


US = {
    "hidden_near_own": 3,
    "hidden_near_mate": 20,
    "hidden_far_mate": 20,
    "backward_zero": 20,
    "backward_three": 20,
    "sum_hidden": 20,
    "sum_two": 0.01,
    "sum_one": 20,
}


def cost(us):
    return pl.CostEstimate(flops=int(us * 1.15e9), bytes_accessed=1000, transcendentals=0)


class Arriving:
    def __init__(self, ref, copy):
        self.ref, self.copy, self.shape = ref, copy, ref.shape

    def __getitem__(self, index):
        if self.copy is not None:
            self.copy.wait()
            self.copy = None
        return self.ref[index]


class Leaving:
    def __init__(self, ref, target, semaphores):
        self.ref, self.target, self.semaphores = ref, target, semaphores
        self.shape, self.dtype, self.copies = ref.shape, ref.dtype, []

    def __getitem__(self, index):
        return self.ref[index]

    def __setitem__(self, index, value):
        self.ref[index] = value

    def done(self, index=None):
        source = self.ref if index is None else self.ref.at[index]
        target = self.target if index is None else self.target.at[index]
        self.copies.append(pltpu.make_async_copy(source, target, self.semaphores.at[len(self.copies)]))
        self.copies[-1].start()


LARGE = 1 << 16


def streamed(kernel, n_in, n_out, scalars, moved, sent, n_own):
    def body(*refs):
        ins, rest = list(refs[:n_in]), refs[n_in:]
        targets, rest = list(rest[:n_out]), rest[n_out:]
        own, rest = rest[:n_own], rest[n_own:]
        buffers, (in_sem, out_sem) = list(rest[:-2]), rest[-2:]
        for i in range(n_in):
            if moved[i]:
                copy = pltpu.make_async_copy(ins[i], buffers[0], in_sem.at[i])
                copy.start()
                ins[i] = Arriving(buffers.pop(0), copy)
        leaving = []
        for o in range(n_out):
            if sent[o]:
                targets[o] = Leaving(buffers.pop(0), targets[o], out_sem.at[o])
                leaving.append(targets[o])
        kernel(*ins, *targets, *own)
        for ref in ins:
            if isinstance(ref, Arriving) and ref.copy is not None:
                ref.copy.wait()
        for ref in leaving:
            if not ref.copies:
                ref.done()
        for ref in leaving:
            for copy in ref.copies:
                copy.wait()

    return body


def call(kernel, name, outs, scratch=(), scalars=0, stream=False):
    def run(*args):
        size = lambda a: a.size * a.dtype.itemsize
        moved = [stream and i >= scalars and size(a) > LARGE for i, a in enumerate(args)]
        sent = [stream and size(o) > LARGE for o in outs]
        vmem, smem = pl.BlockSpec(memory_space=pltpu.VMEM), pl.BlockSpec(memory_space=pltpu.SMEM)
        anywhere = pl.BlockSpec(memory_space=pl.ANY)
        body, shapes = kernel, list(scratch)
        if stream:
            body = streamed(kernel, len(args), len(outs), scalars, moved, sent, len(scratch))
            shapes += [pltpu.VMEM(a.shape, a.dtype) for i, a in enumerate(args) if moved[i]]
            shapes += [pltpu.VMEM(o.shape, o.dtype) for i, o in enumerate(outs) if sent[i]]
            shapes += [pltpu.SemaphoreType.DMA((len(args),)), pltpu.SemaphoreType.DMA((len(outs), 4))]
        return pl.pallas_call(
            body,
            out_shape=outs,
            in_specs=[smem if i < scalars else anywhere if moved[i] else vmem for i in range(len(args))],
            out_specs=tuple(anywhere if flag else vmem for flag in sent),
            scratch_shapes=shapes,
            name=name,
            compiler_params=pltpu.CompilerParams(
                vmem_limit_bytes=SMALL if name.split("_")[0] in LIGHT else VMEM
            ),
            cost_estimate=cost(US.get(name, 0.01)),
        )(*args)

    return run


def norm_parts(values):
    center = values - jnp.mean(values, axis=-1, keepdims=True)
    spread = jnp.mean(center * center, axis=-1, keepdims=True)
    rate = lax.rsqrt(spread + EPSILON)
    return center * rate, rate


def spread_onehot():
    entry = lax.broadcasted_iota(jnp.int32, (LANES, SPREAD), 0)
    column = lax.broadcasted_iota(jnp.int32, (LANES, SPREAD), 1)
    d = lax.div(column, GRID)
    x = column - d * GRID
    return entry == d * (2 * GRID - 1) + x + GRID - 1


def expand_table(table_ref, spread_ref, bias_ref, heads):
    onehot = spread_onehot().astype(bf16)
    reach = 2 * GRID - 1
    inner = reach * reach
    for h in range(heads):
        rows = jnp.broadcast_to(table_ref[h : h + 1, :], (16, LANES))
        spread_ref[h * 16 : (h + 1) * 16, :] = pltpu.roll(rows, 0, 1, stride=1, stride_axis=0)
    rolled = spread_ref[...].astype(bf16)
    wide = dot(rolled, onehot)
    lane = lax.broadcasted_iota(jnp.int32, (16, 256), 1)
    hidden = lane > GRID * GRID
    for h in range(heads):
        bias_ref[h, 192:ROWS, :] = jnp.where(hidden, -1e30, 0.0)
        own = wide[h * 16 : (h + 1) * 16, :]
        to_class = table_ref[h : h + 1, inner + 1 : inner + 2]
        for y in range(GRID):
            part = pltpu.roll(own, (1 - GRID * (GRID - 1 - y)) % SPREAD, 1)[:, :256]
            part = jnp.where(lane == 0, to_class, jnp.where(hidden, -1e30, part))
            bias_ref[h, 1 + GRID * y : 1 + GRID * (y + 1), :] = part[:GRID, :]
        from_class = table_ref[h : h + 1, inner : inner + 1]
        corner = table_ref[h : h + 1, inner + 2 : inner + 3]
        top = jnp.where(lane == 0, corner, jnp.where(hidden, -1e30, from_class))
        bias_ref[h, 0:1, :] = top[:1, :]


def forward_kernel(
    images,
    heads,
    tok_ref,
    vec_ref,
    mixing_in_ref,
    table_ref,
    mixing_out_ref,
    normed_ref,
    packed_ref,
    attend_ref,
    mixed_ref,
    branch_ref,
    middle_ref,
    n2_ref,
    tok_pad,
    spread_ref,
    bias_ref,
):
    width = tok_ref.shape[2]
    patches = tok_ref.shape[1]
    vec = lambda i: vec_ref[i : i + 1, :]
    expand_table(table_ref, spread_ref, bias_ref, heads)
    for n in range(images):
        lo = n * ROWS
        tok_pad[lo + 192 : lo + ROWS, :] = jnp.zeros((ROWS - 192, width), f32)
        tok_pad[lo : lo + patches, :] = tok_ref[n].astype(f32)
    hat, _ = norm_parts(tok_pad[...])
    normed_ref[...] = (hat * vec(FIRST_GAIN) + vec(FIRST_SHIFT)).astype(bf16)
    normed_ref.done()
    for part in range(3):
        cols = slice(part * width, (part + 1) * width)
        value = dot(normed_ref[...], mixing_in_ref[:, cols])
        if part == 0:
            value = value + vec(QUERY_BIAS)
        if part == 2:
            value = value + vec(VALUE_BIAS)
        packed_ref[:, cols] = value.astype(bf16)
    packed_ref.done()
    first = lax.broadcasted_iota(jnp.int32, (1, 128), 1) < 64
    for n in range(images):
        rows = slice(n * ROWS, (n + 1) * ROWS)
        for pair in range(heads // 2):
            cols = [slice(k * width + pair * 128, k * width + (pair + 1) * 128) for k in range(3)]
            q, k, v = (packed_ref[rows, c] for c in cols)
            q = q * jnp.asarray(0.125, bf16)
            zero = jnp.zeros_like(q)
            outs = []
            for side in range(2):
                h = pair * 2 + side
                keep = first if side == 0 else jnp.logical_not(first)
                scores = dot(jnp.where(keep, q, zero), k, NT) + bias_ref[h, :, :ROWS]
                top = jnp.max(scores, axis=-1, keepdims=True)
                weights = jnp.exp(scores - top)
                total = jnp.sum(weights, axis=-1, keepdims=True)
                attend = (weights * (1.0 / total)).astype(bf16)
                attend_ref[n * heads + h] = attend
                outs.append(dot(attend, v))
            mixed_ref[rows, cols[0]] = jnp.where(first, outs[0], outs[1]).astype(bf16)
        attend_ref.done(pl.ds(n * heads, heads))
    mixed_ref.done()
    branch = dot(mixed_ref[...], mixing_out_ref[...]) + vec(OUT_BIAS)
    branch_ref[...] = branch.astype(bf16)
    branch_ref.done()
    middle = tok_pad[...] + vec(SCALE_ATTENTION) * branch
    middle_ref[...] = middle
    middle_ref.done()
    hat, _ = norm_parts(middle)
    n2_ref[...] = (hat * vec(SECOND_GAIN) + vec(SECOND_SHIFT)).astype(bf16)


def gelu_and_slope(v):
    cdf = 0.5 * (1.0 + lax.erf(v * 0.7071067811865476))
    density = jnp.exp(-0.5 * v * v) * 0.3989422804014327
    return v * cdf, cdf + v * density


def hidden_rows_kernel(carried, n2_ref, bg_ref, w1_ref, w2_ref, hb_ref, *rest):
    if carried:
        out_in, grad_in = rest[:2]
        rest = rest[2:]
    act_ref, slope_ref, out_ref, grad_ref = rest
    width, hidden = w1_ref.shape
    for f in range(hidden // 256):
        cols = slice(f * 256, (f + 1) * 256)
        before = dot(n2_ref[...], w1_ref[:, cols]) + hb_ref[0:1, cols]
        value, slope = gelu_and_slope(before)
        act_ref[:, cols] = value.astype(bf16)
        slope_ref[:, cols] = (dot(bg_ref[...], w2_ref[cols, :], NT) * slope).astype(bf16)
    for f in range(width // 256):
        cols = slice(f * 256, (f + 1) * 256)
        value = dot(act_ref[...], w2_ref[:, cols])
        back = dot(slope_ref[...], w1_ref[cols, :], NT)
        if carried:
            value = value + out_in[:, cols].astype(f32)
            back = back + grad_in[:, cols].astype(f32)
        out_ref[:, cols] = value.astype(out_ref.dtype)
        grad_ref[:, cols] = back.astype(grad_ref.dtype)


def half_columns(ref, half):
    width = ref.shape[1] // 2
    return ref[:, pl.ds(pl.multiple_of(half * width, 128), width)]


def put_chips(ref, block, value):
    chips, rows = ref.shape[0], ref.shape[2]
    for j in range(chips):
        ref[j, block] = value[j * rows : (j + 1) * rows, :].astype(ref.dtype)


def hidden_weights_kernel(
    core_ref, n2_ref, bg_ref, act_ref, slope_ref, n2_mate, bg_mate, act_mate, slope_mate, keep_ref, send_ref, hb_ref
):
    core = core_ref[0]
    for ref, half in ((send_ref, 1 - core), (keep_ref, core)):
        total = dot(half_columns(n2_ref, half), slope_ref[...], TN)
        put_chips(ref, 0, total + dot(half_columns(n2_mate, half), slope_mate[...], TN))
        total = dot(half_columns(act_ref, half), bg_ref[...], TN)
        put_chips(ref, 1, total + dot(half_columns(act_mate, half), bg_mate[...], TN))
    total = jnp.sum(slope_ref[...].astype(f32), axis=0, keepdims=True)
    hb_ref[...] = total + jnp.sum(slope_mate[...].astype(f32), axis=0, keepdims=True)


def hidden_first_kernel(place_ref, n2_ref, bg_ref, out_in, grad_in, *refs):
    pieces, (first_ref, second_ref, bias_ref, *outs) = refs[:-7], refs[-7:]
    assemble(place_ref, pieces, first_ref, second_ref, bias_ref)
    hidden_rows_kernel(
        True, n2_ref, bg_ref, Whole(first_ref), Whole(second_ref), bias_ref, out_in, grad_in, *outs
    )


class Whole:
    def __init__(self, ref):
        self.ref = ref
        self.slab = ref.shape[1]
        self.shape = (ref.shape[0] * ref.shape[1], ref.shape[2])

    def __getitem__(self, index):
        rows, cols = index
        value = self.ref[:, :, cols]
        return value.reshape(self.shape[0], value.shape[2])[rows, :]


def hidden_both_kernel(carried, core_ref, n2_ref, bg_ref, w1_ref, w2_ref, hb_ref, *rest):
    carry = rest[: 2 * carried]
    n2_other, bg_other, act_other, slope_other, out, grad, keep, send, hb_grad, act, slope = rest[2 * carried :]
    hidden_rows_kernel(carried, n2_ref, bg_ref, w1_ref, w2_ref, hb_ref, *carry, act, slope, out, grad)
    hidden_weights_kernel(
        core_ref, n2_other, bg_other, act_other, slope_other, n2_ref, bg_ref, act, slope, keep, send, hb_grad
    )


def result_kernel(images, patches, middle_ref, cot_ref, own_ref, recv_ref, vec_ref, result_ref, sums_ref):
    vec = lambda i: vec_ref[i : i + 1, :]
    scale_sum = jnp.zeros((1, middle_ref.shape[1]), f32)
    bias_sum = jnp.zeros((1, middle_ref.shape[1]), f32)
    for n in range(images):
        rows = slice(n * ROWS, n * ROWS + patches)
        cot = cot_ref[n].astype(f32)
        full = own_ref[rows, :].astype(f32) + recv_ref[rows, :].astype(f32) + vec(OUTPUT_BIAS)
        result_ref[n] = (middle_ref[rows, :] + vec(SCALE_HIDDEN) * full).astype(bf16)
        scale_sum = scale_sum + jnp.sum(cot * full, axis=0, keepdims=True)
        low = (vec(SCALE_HIDDEN) * cot).astype(bf16).astype(f32)
        bias_sum = bias_sum + jnp.sum(low, axis=0, keepdims=True)
    sums_ref[0:1, :] = bias_sum
    sums_ref[1:2, :] = scale_sum


def norm_back(grad, hat, rate, gain):
    scaled = grad * gain
    mean = jnp.mean(scaled, axis=-1, keepdims=True)
    cross = jnp.mean(scaled * hat, axis=-1, keepdims=True)
    return rate * (scaled - mean - hat * cross)


def attention_back(
    images, heads, packed_ref, attend_ref, mixed_grad, packed_grad, spread_ref, class_ref, table_ref
):
    width = mixed_grad.shape[1]
    first = lax.broadcasted_iota(jnp.int32, (1, 128), 1) < 64
    lane = lax.broadcasted_iota(jnp.int32, (ROWS, ROWS), 1)
    inner = (2 * GRID - 1) ** 2
    lane_out = lax.broadcasted_iota(jnp.int32, (1, LANES), 1)
    table_ref[...] = jnp.zeros(table_ref.shape, f32)
    spread_ref[...] = jnp.zeros(spread_ref.shape, f32)
    class_ref[...] = jnp.zeros(class_ref.shape, f32)
    for pair in range(heads // 2):
        cols = [slice(k * width + pair * 128, k * width + (pair + 1) * 128) for k in range(3)]
        totals = [None, None]
        for n in range(images):
            rows = slice(n * ROWS, (n + 1) * ROWS)
            q, k, v = (packed_ref[rows, c] for c in cols)
            back = mixed_grad[rows, cols[0]]
            zero = jnp.zeros_like(back)
            grads = []
            for side in range(2):
                h = pair * 2 + side
                keep = first if side == 0 else jnp.logical_not(first)
                attend = attend_ref[n * heads + h]
                wide = attend.astype(f32)
                attend_grad = dot(jnp.where(keep, back, zero), v, NT)
                carried = jnp.sum(wide * attend_grad, axis=-1, keepdims=True)
                low = (wide * (attend_grad - carried)).astype(bf16)
                totals[side] = low.astype(f32) if n == 0 else totals[side] + low.astype(f32)
                scaled = low * jnp.asarray(0.125, bf16)
                grads.append((dot(scaled, k), dot(scaled, q, TN), dot(attend, back, TN)))
            for i in range(3):
                packed_grad[rows, cols[i]] = jnp.where(first, grads[0][i], grads[1][i]).astype(bf16)
        for side in range(2):
            h = pair * 2 + side
            total = totals[side]
            top = total[0:1, :]
            corner = top[:, 0:1]
            from_class = jnp.sum(top, axis=-1, keepdims=True) - corner
            to_class = jnp.sum(total[:, 0:1], axis=0, keepdims=True) - corner
            class_ref[h : h + 1, :] = (
                jnp.where(lane_out == inner, from_class, 0.0)
                + jnp.where(lane_out == inner + 1, to_class, 0.0)
                + jnp.where(lane_out == inner + 2, corner, 0.0)
            )
            table_ref[:, :ROWS] = jnp.where(lane == 0, 0.0, total)
            gathered = jnp.zeros((GRID, SPREAD), f32)
            for y in range(GRID):
                block = table_ref[1 + GRID * y : 1 + GRID * (y + 1), :]
                gathered = gathered + pltpu.roll(block, (GRID * (GRID - 1 - y) - 1) % SPREAD, 1)
            for x in range(GRID):
                spread_ref[x * 16 + h : x * 16 + h + 1, :] = gathered[x : x + 1, :]


def backward_zero_kernel(
    images,
    patches,
    cot_ref,
    middle_ref,
    branch_ref,
    own_ref,
    recv_ref,
    mixing_out_ref,
    vec_ref,
    middle_grad,
    mixed_grad,
    low_ref,
    sums_ref,
):
    width = middle_ref.shape[1]
    vec = lambda i: vec_ref[i : i + 1, :]
    column_sum = lambda v: jnp.sum(v, axis=0, keepdims=True)
    for n in range(images):
        middle_grad[n * ROWS + 192 : (n + 1) * ROWS, :] = jnp.zeros((ROWS - 192, width), f32)
        middle_grad[n * ROWS : n * ROWS + patches, :] = cot_ref[n].astype(f32)
    sums = [jnp.zeros((1, width), f32) for _ in range(4)]
    for n in range(images):
        rows = slice(n * ROWS, (n + 1) * ROWS)
        grad = own_ref[rows, :].astype(f32) + recv_ref[rows, :].astype(f32)
        hat, rate = norm_parts(middle_ref[rows, :])
        sums[0] = sums[0] + column_sum(grad * hat)
        sums[1] = sums[1] + column_sum(grad)
        total = middle_grad[rows, :] + norm_back(grad, hat, rate, vec(SECOND_GAIN))
        middle_grad[rows, :] = total
        sums[2] = sums[2] + column_sum(total * branch_ref[rows, :].astype(f32))
        low = (vec(SCALE_ATTENTION) * total).astype(bf16)
        sums[3] = sums[3] + column_sum(low.astype(f32))
        low_ref[rows, :] = low
    for i, at in enumerate((2, 3, 1, 0)):
        sums_ref[at : at + 1, :] = sums[i]
    mixed_grad[...] = dot(low_ref[...], mixing_out_ref[...], NT).astype(bf16)


def backward_one_kernel(
    images,
    heads,
    part,
    core_ref,
    low_ref,
    mixed_ref,
    mixed_grad,
    packed_ref,
    attend_ref,
    normed_ref,
    packed_grad,
    spread_ref,
    class_ref,
    keep_one,
    send_one,
    keep_two,
    send_two,
    table_ref,
):
    core = core_ref[0]
    order = ((send_one, send_two, 1 - core), (keep_one, keep_two, core))
    for one, _, half in order:
        for b in range(2):
            put_chips(one, b, dot(half_columns(mixed_ref, half), low_ref[:, b * part : (b + 1) * part], TN))
    attention_back(images, heads, packed_ref, attend_ref, mixed_grad, packed_grad, spread_ref, class_ref, table_ref)
    packed_grad.done()
    for one, two, half in order:
        for b in range(6):
            value = dot(half_columns(normed_ref, half), packed_grad[:, b * part : (b + 1) * part], TN)
            put_chips(two if b % 2 else one, b // 2 if b % 2 else 2 + b // 2, value)
        one.done()
        two.done()


def backward_three_kernel(
    images,
    heads,
    patches,
    tok_ref,
    middle_grad,
    packed_grad,
    spread_ref,
    class_ref,
    sums_one,
    mixing_in_ref,
    vec_ref,
    token_grad_ref,
    sums_ref,
    tok_pad,
):
    width = tok_ref.shape[2]
    vec = lambda i: vec_ref[i : i + 1, :]
    column_sum = lambda v: jnp.sum(v, axis=0, keepdims=True)
    onehot = spread_onehot().astype(bf16)
    value = spread_ref[...]
    high = value.astype(bf16)
    rest = (value - high.astype(f32)).astype(bf16)
    spread = dot(high, onehot, NT) + dot(rest, onehot, NT)
    entries = class_ref[...]
    for x in range(GRID):
        block = spread[x * 16 : (x + 1) * 16, :]
        entries = entries + (pltpu.roll(block, LANES - x, 1) if x else block)
    sums_ref[8:24, :] = entries
    sums_ref[0:4, :] = sums_one[0:4, :]
    sums_ref[6:7, :] = column_sum(packed_grad[:, :width].astype(f32))
    sums_ref[7:8, :] = column_sum(packed_grad[:, 2 * width :].astype(f32))
    sums = [jnp.zeros((1, width), f32) for _ in range(2)]
    for n in range(images):
        rows = slice(n * ROWS, (n + 1) * ROWS)
        grad = dot(packed_grad[rows, :], mixing_in_ref[...], NT)
        tok_pad[192:ROWS, :] = jnp.zeros((ROWS - 192, width), f32)
        tok_pad[:patches, :] = tok_ref[n].astype(f32)
        hat, rate = norm_parts(tok_pad[...])
        sums[0] = sums[0] + column_sum(grad * hat)
        sums[1] = sums[1] + column_sum(grad)
        total = middle_grad[rows, :] + norm_back(grad, hat, rate, vec(FIRST_GAIN))
        token_grad_ref[n] = total[:patches, :].astype(bf16)
    sums_ref[4:5, :] = sums[0]
    sums_ref[5:6, :] = sums[1]


def add_kernel(chip_ref, *refs):
    chip = chip_ref[0]
    chips = refs[0].shape[0]
    pairs, outs = refs[:-chips], refs[-chips:]
    for k, out in enumerate(outs):
        for i in range(0, len(pairs), 2):
            total = pairs[i][chip ^ k].astype(f32) + pairs[i + 1][chip ^ k].astype(f32)
            out[i // 2] = total.astype(bf16)


def add_two_kernel(keep_ref, recv_ref, out_ref):
    out_ref[...] = (keep_ref[...].astype(f32) + recv_ref[...].astype(f32)).astype(bf16)


def add_single_kernel(one_ref, two_ref, out_ref):
    out_ref[...] = one_ref[...] + two_ref[...]


def share_kernel(line_ref, near_ref, far_ref, sums_ref, out_sums_ref, hb_near, hb_far, out_ref, small):
    rows = near_ref.shape[1]
    for m in range(2):
        total = near_ref[m].astype(f32) + far_ref[m].astype(f32)
        out_ref[m * rows : (m + 1) * rows, :] = total.astype(bf16)
    count = sums_ref.shape[0]
    small[...] = jnp.zeros(small.shape, f32)
    small[0:count, :] = sums_ref[...]
    small[count : count + 2, :] = out_sums_ref[...]
    small[pl.ds(count + 2 + line_ref[0], 1), :] = hb_near[...]
    small[pl.ds(count + 2 + line_ref[1], 1), :] = hb_far[...]
    out_ref[2 * rows :, :] = small[...].astype(bf16)


def sum_sums_kernel(*refs):
    count = refs[-1].shape[0]
    at = slice(refs[0].shape[0] - count, refs[0].shape[0])
    total = refs[0][at, :].astype(f32)
    for ref in refs[1:-1]:
        total = total + ref[at, :].astype(f32)
    refs[-1][...] = total


def add_spread_kernel(one_ref, two_ref, out_ref):
    total = (one_ref[...].astype(f32) + two_ref[...].astype(f32)).astype(bf16)
    for j in range(out_ref.shape[0]):
        out_ref[j] = total


def sum_pair_kernel(*refs):
    count = (len(refs) - 2) // 2
    for parts, out in ((refs[:count], refs[-2]), (refs[count:-2], refs[-1])):
        total = parts[0][0].astype(f32)
        for ref in parts[1:]:
            total = total + ref[0].astype(f32)
        out[...] = total.astype(bf16)


def sum_all_kernel(parts_ref, total_ref):
    total = parts_ref[0].astype(f32)
    for j in range(1, parts_ref.shape[0]):
        total = total + parts_ref[j].astype(f32)
    total_ref[...] = total.astype(bf16)


def assemble(place_ref, refs, first_ref, second_ref, bias_ref):
    core, chip = place_ref[0], place_ref[1]
    chips, slab, _ = first_ref.shape

    def put(mine, other):
        for k in range(chips):
            mine[chip ^ k] = refs[k][:slab, :]
            other[chip ^ k] = refs[chips + k][:slab, :]

    @pl.when(core == 0)
    def _():
        put(first_ref, second_ref)

    @pl.when(core != 0)
    def _():
        put(second_ref, first_ref)

    bias_ref[...] = refs[0][slab : slab + 8, :].astype(f32)[0:1, :]


def sum_kernel(*refs):
    total = refs[0][...].astype(f32)
    for ref in refs[1:-1]:
        total = total + ref[...].astype(f32)
    refs[-1][...] = total.astype(bf16)


def hidden_final_kernel(place_ref, *refs):
    core, chip = place_ref[0], place_ref[1]
    in_ref, out_ref = refs[-2:]
    chips = (len(refs) - 2) // 2
    for k in range(chips):
        for ref, half in ((refs[k], core), (refs[chips + k], 1 - core)):
            rows = in_ref.shape[2]
            in_ref[half, chip ^ k] = ref[:rows, :].astype(f32)
            out_ref[half, chip ^ k] = ref[rows : 2 * rows, :].astype(f32)


def mixing_one_kernel(place_ref, *refs):
    core, chip = place_ref[0], place_ref[1]
    in_ref, out_ref = refs[-2:]
    chips = (len(refs) - 2) // 4
    first = pl.program_id(0) == 0
    for k in range(chips):
        for ref, half in ((refs[k], core), (refs[chips + k], 1 - core)):
            in_ref[half, chip ^ k] = ref[0].astype(f32)

    @pl.when(first)
    def _():
        for k in range(chips):
            for ref, half in ((refs[2 * chips + k], core), (refs[3 * chips + k], 1 - core)):
                part = ref.shape[2]
                for b in range(2):
                    out_ref[half, chip ^ k, :, b * part : (b + 1) * part] = ref[b].astype(f32)


def mixing_two_kernel(place_ref, before_ref, mine_ref, recv_ref, in_ref):
    core = place_ref[0]
    for j in range(mine_ref.shape[0]):
        for ref, half in ((mine_ref, core), (recv_ref, 1 - core)):
            in_ref[half, j] = ref[j, 0].astype(f32)


def per_device(
    n_dp,
    n_tp,
    tokens,
    first_gain,
    first_shift,
    mixing_in,
    query_bias,
    value_bias,
    relative_table,
    mixing_out,
    out_bias,
    scale_attention,
    second_gain,
    second_shift,
    hidden_in,
    hidden_bias,
    hidden_out,
    output_bias,
    scale_hidden,
    cotangent,
):
    images, patches, width = tokens.shape
    heads = relative_table.shape[1]
    count = images * ROWS
    hidden = hidden_in.shape[1]
    chips = n_dp // 2
    half = width // 2
    part = half
    chip_rows = half // chips
    plane = [[2 * i + c for i in range(chips)] for c in range(2)]
    dp, tp = lax.axis_index("dp"), lax.axis_index("tp")
    core, chip = dp % 2, dp // 2
    mate = lambda a: lax.ppermute(a, "tp", [(i, i ^ 1) for i in range(n_tp)])
    far = lambda a: lax.ppermute(a, "tp", [(i, i ^ 2) for i in range(n_tp)])
    twin = lambda a: lax.ppermute(a, "dp", [(i, i ^ 1) for i in range(n_dp)])
    over_plane = lambda a: lax.all_to_all(a, "dp", 0, 0, axis_index_groups=plane, tiled=True)
    over_line = lambda a: lax.all_to_all(a, "tp", 0, 0, tiled=True)
    copies = lambda a, n: jnp.broadcast_to(a[None], (n, *a.shape))
    by_core = lambda a, b: (jnp.where(core == 0, a, b), jnp.where(core == 0, b, a))
    add = lambda a, b: (a.astype(f32) + b.astype(f32)).astype(bf16)
    def hop(value, k):
        return lax.ppermute(value, "dp", [(i, i ^ (2 * k)) for i in range(n_dp)])

    def to_chips(values):
        if chips <= 4:
            return [hop(value, k) for k, value in enumerate(values) if k]
        order = lambda a, k: lax.dynamic_index_in_dim(a, chip ^ k, 0, keepdims=False)
        stacked = jnp.stack(values)
        stacked = jnp.stack([order(stacked, j) for j in range(chips)])
        stacked = over_plane(stacked)
        return [order(stacked, k) for k in range(1, chips)]

    shape = jax.ShapeDtypeStruct
    core_index = core.astype(jnp.int32).reshape(1)
    chip_index = chip.astype(jnp.int32).reshape(1)
    place = jnp.concatenate([core_index, chip_index])
    rows = (count, width)

    order = Order()
    tie, step = order.tie, order.step

    slab = width // chips
    piece = lax.dynamic_slice_in_dim(jnp.where(core == 0, hidden_in, hidden_out), chip * slab, slab, 0)
    piece = jnp.concatenate([piece, jnp.broadcast_to(hidden_bias[None], (16, hidden))])
    far_piece = far(step(piece))
    bg = (scale_hidden.astype(f32) * tie(cotangent).astype(f32)).astype(bf16)
    bg = step(jnp.pad(bg, ((0, 0), (0, ROWS - patches), (0, 0))).reshape(rows))
    bg_mate = mate(bg)

    vecs = jnp.stack(
        [
            first_gain,
            first_shift,
            query_bias,
            value_bias,
            out_bias,
            scale_attention,
            second_gain,
            second_shift,
            output_bias,
            scale_hidden,
        ]
    ).astype(f32)
    inner = (2 * GRID - 1) ** 2
    table = relative_table.astype(f32)
    table = jnp.concatenate([table[:inner][::-1], table[inner:]]).T
    table = jnp.pad(table, ((0, 0), (0, LANES - table.shape[1])))

    normed, packed, attend, mixed, branch, middle, n2 = call(
        functools.partial(forward_kernel, images, heads),
        "attention_forward",
        [
            shape(rows, bf16),
            shape((count, 3 * width), bf16),
            shape((images * heads, ROWS, ROWS), bf16),
            shape(rows, bf16),
            shape(rows, bf16),
            shape(rows, f32),
            shape(rows, bf16),
        ],
        [
            pltpu.VMEM(rows, f32),
            pltpu.VMEM((heads * 16, LANES), f32),
            pltpu.VMEM((heads, ROWS, 256), f32),
        ],
        stream=True,
    )(tokens, tie(vecs), mixing_in, table, mixing_out)

    n2_mate = mate(step(n2))
    pieces = step(tie(far_piece))
    pieces = [pieces, *to_chips([pieces] * chips)]

    weight = shape((chips, 2, half // chips, width), bf16)
    low_rows = shape(rows, bf16)
    hidden_cols = shape((count, hidden), bf16)

    def hidden_rows(name, n2, bg, w1, w2, bias, carried):
        return call(
            functools.partial(hidden_rows_kernel, bool(carried)),
            name,
            [hidden_cols, hidden_cols, low_rows, low_rows],
        )(n2, bg, w1, w2, tie(bias), *carried)

    def hidden_both(name, n2, bg, w1, w2, bias, carried, other):
        return call(
            functools.partial(hidden_both_kernel, len(carried) // 2),
            name,
            [low_rows, low_rows, weight, weight, shape((1, hidden), f32)],
            [pltpu.VMEM((count, hidden), bf16), pltpu.VMEM((count, hidden), bf16)],
            scalars=1,
        )(tie(core_index), n2, bg, w1, w2, bias, *carried, *other)

    near_bias = hidden_bias.astype(f32)[None]
    act_no, slope_no, out_own, grad_own = hidden_rows("hidden_near_own", n2, bg, hidden_in, hidden_out, near_bias, ())
    step(act_no)
    bg_mate = step(tie(bg_mate))
    n2_mate = step(tie(n2_mate))
    pieces = [step(tie(a)) for a in pieces]
    other_pieces = [twin(a) for a in pieces]
    out_mate, grad_mate, keep_near, send_near, hb_near = hidden_both(
        "hidden_near_mate", n2_mate, bg_mate, hidden_in, hidden_out, near_bias, (), (n2, bg, act_no, slope_no)
    )
    recv_near = twin(step(send_near))
    slabs = shape((chips, slab, hidden), bf16)
    far_in, far_out, far_bias, act_fm, slope_fm, out_mate, grad_mate = call(
        hidden_first_kernel,
        "hidden_far_mate",
        [slabs, slabs, shape((1, hidden), f32), hidden_cols, hidden_cols, low_rows, low_rows],
        scalars=1,
    )(tie(place), n2_mate, bg_mate, out_mate, grad_mate, *pieces, *other_pieces)
    far_in, far_out = far_in.reshape(width, hidden), far_out.reshape(width, hidden)
    grad_recv = mate(step(grad_mate))
    block = shape((1, 2, chip_rows, width), bf16)
    nears = call(add_kernel, "add_near", [block] * chips, scalars=1)(tie(chip_index), keep_near, recv_near)
    step(nears[0])
    nears = [nears[0], *to_chips(nears)]
    out_recv = mate(step(out_mate))
    out_own, grad_own, keep_far, send_far, hb_far = hidden_both(
        "hidden_far_own", n2, bg, far_in, far_out, far_bias, (out_own, grad_own), (n2_mate, bg_mate, act_fm, slope_fm)
    )
    recv_far = twin(step(send_far))

    spread, classes = shape((GRID * 16, SPREAD), f32), shape((16, LANES), f32)
    nears = [step(tie(a)) for a in nears]
    middle_grad, mixed_grad, attention_grad, sums_one = call(
        functools.partial(backward_zero_kernel, images, patches),
        "backward_zero",
        [shape(rows, f32), shape(rows, bf16), shape(rows, bf16), shape((4, width), f32)],
    )(cotangent, middle, branch, grad_own, grad_recv, mixing_out, tie(vecs))
    step(attention_grad)
    fars = call(add_kernel, "add_far", [block] * chips, scalars=1)(tie(chip_index), keep_far, recv_far)
    step(fars[0])
    fars = [fars[0], *to_chips(fars)]
    packed_grad, spread, classes, keep_one, send_one, keep_two, send_two = call(
        functools.partial(backward_one_kernel, images, heads, part),
        "backward_one",
        [
            shape((count, 3 * width), bf16),
            spread,
            classes,
            shape((chips, 5, chip_rows, part), bf16),
            shape((chips, 5, chip_rows, part), bf16),
            shape((chips, 3, chip_rows, part), bf16),
            shape((chips, 3, chip_rows, part), bf16),
        ],
        [pltpu.VMEM((ROWS, SPREAD), f32)],
        scalars=1,
        stream=True,
    )(tie(core_index), attention_grad, mixed, mixed_grad, packed, attend, normed)
    step(send_one)
    recv_one = twin(send_one)
    recv_two = twin(send_two)
    share_near, share_far = call(sum_pair_kernel, "sum_hidden", [shape((2, chip_rows, width), bf16)] * 2)(
        *nears, tie(fars[0]), *fars[1:]
    )
    share_far = far(step(share_far))
    block = shape((1, 5, chip_rows, part), bf16)
    ones = call(add_kernel, "add_one", [block] * chips, scalars=1)(tie(chip_index), keep_one, recv_one)
    step(ones[0])
    ones = [ones[0], *to_chips(ones)]
    token_grad, sums = call(
        functools.partial(backward_three_kernel, images, heads, patches),
        "backward_three",
        [shape(tokens.shape, bf16), shape((24, width), f32)],
        [pltpu.VMEM((ROWS, width), f32)],
    )(
        tokens,
        middle_grad,
        packed_grad,
        spread,
        classes,
        sums_one,
        mixing_in,
        tie(vecs),
    )
    step(token_grad)
    two_shape = shape((3, chip_rows, part), bf16)
    (twos,) = call(add_two_kernel, "add_two", [shape(keep_two.shape, bf16)])(tie(keep_two), recv_two)
    twos = over_plane(step(twos))
    share_far = step(tie(share_far))
    result, sums_out = call(
        functools.partial(result_kernel, images, patches),
        "result",
        [shape(tokens.shape, bf16), shape((2, width), f32)],
    )(middle, cotangent, out_own, out_recv, tie(vecs))
    step(sums_out)
    (one,) = call(sum_kernel, "sum_one", [block])(tie(ones[0]), *ones[1:])
    one_near = mate(step(one))
    line_index = jnp.stack([tp, tp ^ 2]).astype(jnp.int32)
    (share,) = call(
        share_kernel,
        "share",
        [shape((2 * chip_rows + 32, width), bf16)],
        [pltpu.VMEM((32, width), f32)],
        scalars=1,
    )(line_index, share_near, tie(share_far), sums, sums_out, hb_near, hb_far)
    step(share)
    share = [share, *to_chips([share] * chips)]
    (two,) = call(sum_all_kernel, "sum_two", [two_shape])(tie(twos))
    two_near = mate(step(two))
    (one,) = call(add_two_kernel, "add_line_one", [block])(one, tie(one_near))
    one_far = far(step(one))
    (two,) = call(add_two_kernel, "add_line_two", [two_shape])(two, tie(two_near))
    two_far = far(step(two))
    share = [step(tie(a)) for a in share]
    (sums,) = call(sum_sums_kernel, "sum_sums", [shape((32, width), f32)])(*share)
    sums_near = mate(step(sums))
    share_recv = [twin(a) for a in share]
    (one,) = call(add_two_kernel, "last_one", [shape(block.shape[1:], bf16)])(one[0], tie(one_far)[0])
    step(one)
    one = [one, *to_chips([one] * chips)]
    wide = shape((2, chips, chip_rows, width), f32)
    hidden_in_grad, hidden_out_grad = call(hidden_final_kernel, "hidden_final", [wide, wide], scalars=1)(
        tie(place), *share, *share_recv
    )
    step(hidden_in_grad)
    (sums,) = call(add_single_kernel, "add_sums", [shape((32, width), f32)])(sums, tie(sums_near))
    sums_far = far(step(sums))
    (two,) = call(add_spread_kernel, "spread_two", [shape((chips, *two_shape.shape), bf16)])(two, tie(two_far))
    two = over_plane(step(two))
    (sums,) = call(add_single_kernel, "add_sums_far", [shape((32, width), f32)])(sums, tie(sums_far))
    sums_twin = twin(step(sums))
    one = [step(tie(a)) for a in one]
    one_recv = [twin(a) for a in one]
    scalar = pl.BlockSpec(memory_space=pltpu.SMEM)
    third = (1, chip_rows, part)
    params = pltpu.CompilerParams(vmem_limit_bytes=2 * SMALL)
    in_shape = shape((2, chips, chip_rows, 3 * width), f32)
    mixing_in_grad, mixing_out_grad = pl.pallas_call(
        mixing_one_kernel,
        grid=(3,),
        out_shape=(in_shape, wide),
        in_specs=[scalar]
        + [pl.BlockSpec(third, lambda b: (2 + b, 0, 0))] * (2 * chips)
        + [pl.BlockSpec((2, chip_rows, part), lambda b: (0, 0, 0))] * (2 * chips),
        out_specs=(
            pl.BlockSpec((2, chips, chip_rows, part), lambda b: (0, 0, 0, 2 * b)),
            pl.BlockSpec((2, chips, chip_rows, width), lambda b: (0, 0, 0, 0)),
        ),
        name="mixing_one",
        compiler_params=params,
        cost_estimate=cost(0.01),
    )(tie(place), *one, *one_recv, *one, *one_recv)
    step(mixing_out_grad)
    sums = step(sums + tie(sums_twin))
    two = tie(two)
    mixing_in_grad = pl.pallas_call(
        mixing_two_kernel,
        grid=(3,),
        out_shape=in_shape,
        in_specs=[scalar, pl.BlockSpec(memory_space=pl.ANY)]
        + [pl.BlockSpec((chips, *third), lambda b: (0, b, 0, 0))] * 2,
        out_specs=pl.BlockSpec((2, chips, chip_rows, part), lambda b: (0, 0, 0, 2 * b + 1)),
        input_output_aliases={1: 0},
        name="mixing_two",
        compiler_params=params,
        cost_estimate=cost(0.01),
    )(place, mixing_in_grad, two, twin(two))

    table_grad = sums[8 : 8 + heads].T
    table_grad = jnp.concatenate([table_grad[:inner][::-1], table_grad[inner : relative_table.shape[0]]])
    hidden_bias_grad = lax.dynamic_index_in_dim(sums[26 : 26 + n_tp], tp, 0, keepdims=False)
    return (
        result,
        token_grad,
        sums[4],
        sums[5],
        mixing_in_grad.reshape(width, 3 * width),
        sums[6],
        sums[7],
        table_grad,
        mixing_out_grad.reshape(width, width),
        sums[0],
        sums[1],
        sums[2],
        sums[3],
        hidden_in_grad.reshape(width, width),
        hidden_bias_grad,
        hidden_out_grad.reshape(width, width),
        sums[24],
        sums[25],
    )


def solution(mesh):
    everywhere = P()
    rows = P("dp", "tp", None)
    hidden = (P(None, "tp"), P("tp"), P("tp", None))
    return jax.shard_map(
        functools.partial(per_device, mesh.shape["dp"], mesh.shape["tp"]),
        mesh=mesh,
        in_specs=(rows, *[everywhere] * 11, *hidden, everywhere, everywhere, rows),
        out_specs=(rows, rows, *[everywhere] * 11, *hidden, everywhere, everywhere),
        check_vma=False,
    )
```

```python
import functools

import jax
import jax.numpy as jnp
from jax import lax
from jax.experimental import pallas as pl
from jax.experimental.pallas import tpu as pltpu
from jax.sharding import PartitionSpec as P

GRID = 14
EPSILON = 1e-06
ROWS = 208
LANES = 768
SPREAD = 384
VMEM = 56 * 1024 * 1024
SMALL = 8 * 1024 * 1024
LIGHT = ("add", "sum", "share", "last", "spread")

f32 = jnp.float32
bf16 = jnp.bfloat16

NN = (((1,), (0,)), ((), ()))
NT = (((1,), (1,)), ((), ()))
TN = (((0,), (0,)), ((), ()))

(
    FIRST_GAIN,
    FIRST_SHIFT,
    QUERY_BIAS,
    VALUE_BIAS,
    OUT_BIAS,
    SCALE_ATTENTION,
    SECOND_GAIN,
    SECOND_SHIFT,
    OUTPUT_BIAS,
    SCALE_HIDDEN,
) = range(10)


def dot(a, b, dims=NN):
    return lax.dot_general(a, b, dims, preferred_element_type=f32)


class Order:
    def __init__(self):
        self.last = None

    def tie(self, value):
        if self.last is not None:
            value, _ = lax.optimization_barrier((value, self.last))
        return value

    def step(self, value):
        self.last = value
        return value


US = {
    "hidden_near_own": 3,
    "hidden_near_mate": 20,
    "hidden_far_mate": 20,
    "backward_zero": 20,
    "backward_three": 20,
    "sum_hidden": 20,
    "sum_two": 0.01,
    "sum_one": 20,
}


def cost(us):
    return pl.CostEstimate(flops=int(us * 1.15e9), bytes_accessed=1000, transcendentals=0)


class Arriving:
    def __init__(self, ref, copy):
        self.ref, self.copy, self.shape = ref, copy, ref.shape

    def __getitem__(self, index):
        if self.copy is not None:
            self.copy.wait()
            self.copy = None
        return self.ref[index]


class Leaving:
    def __init__(self, ref, target, semaphores):
        self.ref, self.target, self.semaphores = ref, target, semaphores
        self.shape, self.dtype, self.copies = ref.shape, ref.dtype, []

    def __getitem__(self, index):
        return self.ref[index]

    def __setitem__(self, index, value):
        self.ref[index] = value

    def done(self, index=None):
        source = self.ref if index is None else self.ref.at[index]
        target = self.target if index is None else self.target.at[index]
        self.copies.append(pltpu.make_async_copy(source, target, self.semaphores.at[len(self.copies)]))
        self.copies[-1].start()


LARGE = 1 << 16


def streamed(kernel, n_in, n_out, scalars, moved, sent, n_own):
    def body(*refs):
        ins, rest = list(refs[:n_in]), refs[n_in:]
        targets, rest = list(rest[:n_out]), rest[n_out:]
        own, rest = rest[:n_own], rest[n_own:]
        buffers, (in_sem, out_sem) = list(rest[:-2]), rest[-2:]
        for i in range(n_in):
            if moved[i]:
                copy = pltpu.make_async_copy(ins[i], buffers[0], in_sem.at[i])
                copy.start()
                ins[i] = Arriving(buffers.pop(0), copy)
        leaving = []
        for o in range(n_out):
            if sent[o]:
                targets[o] = Leaving(buffers.pop(0), targets[o], out_sem.at[o])
                leaving.append(targets[o])
        kernel(*ins, *targets, *own)
        for ref in ins:
            if isinstance(ref, Arriving) and ref.copy is not None:
                ref.copy.wait()
        for ref in leaving:
            if not ref.copies:
                ref.done()
        for ref in leaving:
            for copy in ref.copies:
                copy.wait()

    return body


def call(kernel, name, outs, scratch=(), scalars=0, stream=False):
    def run(*args):
        size = lambda a: a.size * a.dtype.itemsize
        moved = [stream and i >= scalars and size(a) > LARGE for i, a in enumerate(args)]
        sent = [stream and size(o) > LARGE for o in outs]
        vmem, smem = pl.BlockSpec(memory_space=pltpu.VMEM), pl.BlockSpec(memory_space=pltpu.SMEM)
        anywhere = pl.BlockSpec(memory_space=pl.ANY)
        body, shapes = kernel, list(scratch)
        if stream:
            body = streamed(kernel, len(args), len(outs), scalars, moved, sent, len(scratch))
            shapes += [pltpu.VMEM(a.shape, a.dtype) for i, a in enumerate(args) if moved[i]]
            shapes += [pltpu.VMEM(o.shape, o.dtype) for i, o in enumerate(outs) if sent[i]]
            shapes += [pltpu.SemaphoreType.DMA((len(args),)), pltpu.SemaphoreType.DMA((len(outs), 4))]
        return pl.pallas_call(
            body,
            out_shape=outs,
            in_specs=[smem if i < scalars else anywhere if moved[i] else vmem for i in range(len(args))],
            out_specs=tuple(anywhere if flag else vmem for flag in sent),
            scratch_shapes=shapes,
            name=name,
            compiler_params=pltpu.CompilerParams(
                vmem_limit_bytes=SMALL if name.split("_")[0] in LIGHT else VMEM
            ),
            cost_estimate=cost(US.get(name, 0.01)),
        )(*args)

    return run


def norm_parts(values):
    center = values - jnp.mean(values, axis=-1, keepdims=True)
    spread = jnp.mean(center * center, axis=-1, keepdims=True)
    rate = lax.rsqrt(spread + EPSILON)
    return center * rate, rate


def spread_onehot():
    entry = lax.broadcasted_iota(jnp.int32, (LANES, SPREAD), 0)
    column = lax.broadcasted_iota(jnp.int32, (LANES, SPREAD), 1)
    d = lax.div(column, GRID)
    x = column - d * GRID
    return entry == d * (2 * GRID - 1) + x + GRID - 1


def expand_table(table_ref, spread_ref, bias_ref, heads):
    onehot = spread_onehot().astype(bf16)
    reach = 2 * GRID - 1
    inner = reach * reach
    for h in range(heads):
        rows = jnp.broadcast_to(table_ref[h : h + 1, :], (16, LANES))
        spread_ref[h * 16 : (h + 1) * 16, :] = pltpu.roll(rows, 0, 1, stride=1, stride_axis=0)
    rolled = spread_ref[...].astype(bf16)
    wide = dot(rolled, onehot)
    lane = lax.broadcasted_iota(jnp.int32, (16, 256), 1)
    hidden = lane > GRID * GRID
    for h in range(heads):
        bias_ref[h, 192:ROWS, :] = jnp.where(hidden, -1e30, 0.0)
        own = wide[h * 16 : (h + 1) * 16, :]
        to_class = table_ref[h : h + 1, inner + 1 : inner + 2]
        for y in range(GRID):
            part = pltpu.roll(own, (1 - GRID * (GRID - 1 - y)) % SPREAD, 1)[:, :256]
            part = jnp.where(lane == 0, to_class, jnp.where(hidden, -1e30, part))
            bias_ref[h, 1 + GRID * y : 1 + GRID * (y + 1), :] = part[:GRID, :]
        from_class = table_ref[h : h + 1, inner : inner + 1]
        corner = table_ref[h : h + 1, inner + 2 : inner + 3]
        top = jnp.where(lane == 0, corner, jnp.where(hidden, -1e30, from_class))
        bias_ref[h, 0:1, :] = top[:1, :]


def forward_kernel(
    images,
    heads,
    tok_ref,
    vec_ref,
    mixing_in_ref,
    table_ref,
    mixing_out_ref,
    normed_ref,
    packed_ref,
    attend_ref,
    mixed_ref,
    branch_ref,
    middle_ref,
    n2_ref,
    tok_pad,
    spread_ref,
    bias_ref,
):
    width = tok_ref.shape[2]
    patches = tok_ref.shape[1]
    vec = lambda i: vec_ref[i : i + 1, :]
    expand_table(table_ref, spread_ref, bias_ref, heads)
    for n in range(images):
        lo = n * ROWS
        tok_pad[lo + 192 : lo + ROWS, :] = jnp.zeros((ROWS - 192, width), f32)
        tok_pad[lo : lo + patches, :] = tok_ref[n].astype(f32)
    hat, _ = norm_parts(tok_pad[...])
    normed_ref[...] = (hat * vec(FIRST_GAIN) + vec(FIRST_SHIFT)).astype(bf16)
    normed_ref.done()
    for part in range(3):
        cols = slice(part * width, (part + 1) * width)
        value = dot(normed_ref[...], mixing_in_ref[:, cols])
        if part == 0:
            value = value + vec(QUERY_BIAS)
        if part == 2:
            value = value + vec(VALUE_BIAS)
        packed_ref[:, cols] = value.astype(bf16)
    packed_ref.done()
    first = lax.broadcasted_iota(jnp.int32, (1, 128), 1) < 64
    for n in range(images):
        rows = slice(n * ROWS, (n + 1) * ROWS)
        for pair in range(heads // 2):
            cols = [slice(k * width + pair * 128, k * width + (pair + 1) * 128) for k in range(3)]
            q, k, v = (packed_ref[rows, c] for c in cols)
            q = q * jnp.asarray(0.125, bf16)
            zero = jnp.zeros_like(q)
            outs = []
            for side in range(2):
                h = pair * 2 + side
                keep = first if side == 0 else jnp.logical_not(first)
                scores = dot(jnp.where(keep, q, zero), k, NT) + bias_ref[h, :, :ROWS]
                top = jnp.max(scores, axis=-1, keepdims=True)
                weights = jnp.exp(scores - top)
                total = jnp.sum(weights, axis=-1, keepdims=True)
                attend = (weights * (1.0 / total)).astype(bf16)
                attend_ref[n * heads + h] = attend
                outs.append(dot(attend, v))
            mixed_ref[rows, cols[0]] = jnp.where(first, outs[0], outs[1]).astype(bf16)
        attend_ref.done(pl.ds(n * heads, heads))
    mixed_ref.done()
    branch = dot(mixed_ref[...], mixing_out_ref[...]) + vec(OUT_BIAS)
    branch_ref[...] = branch.astype(bf16)
    branch_ref.done()
    middle = tok_pad[...] + vec(SCALE_ATTENTION) * branch
    middle_ref[...] = middle
    middle_ref.done()
    hat, _ = norm_parts(middle)
    n2_ref[...] = (hat * vec(SECOND_GAIN) + vec(SECOND_SHIFT)).astype(bf16)


def gelu_and_slope(v):
    cdf = 0.5 * (1.0 + lax.erf(v * 0.7071067811865476))
    density = jnp.exp(-0.5 * v * v) * 0.3989422804014327
    return v * cdf, cdf + v * density


def hidden_rows_kernel(carried, n2_ref, bg_ref, w1_ref, w2_ref, hb_ref, *rest):
    if carried:
        out_in, grad_in = rest[:2]
        rest = rest[2:]
    act_ref, slope_ref, out_ref, grad_ref = rest
    width, hidden = w1_ref.shape
    for f in range(hidden // 256):
        cols = slice(f * 256, (f + 1) * 256)
        before = dot(n2_ref[...], w1_ref[:, cols]) + hb_ref[0:1, cols]
        value, slope = gelu_and_slope(before)
        act_ref[:, cols] = value.astype(bf16)
        slope_ref[:, cols] = (dot(bg_ref[...], w2_ref[cols, :], NT) * slope).astype(bf16)
    for f in range(width // 256):
        cols = slice(f * 256, (f + 1) * 256)
        if out_ref is not None:
            hidden_out_columns(act_ref, w2_ref, out_in if carried else None, out_ref, cols)
        back = dot(slope_ref[...], w1_ref[cols, :], NT)
        if carried:
            back = back + grad_in[:, cols].astype(f32)
        grad_ref[:, cols] = back.astype(grad_ref.dtype)


def hidden_out_columns(act_ref, w2_ref, out_in, out_ref, cols):
    value = dot(act_ref[...], w2_ref[:, cols])
    if out_in is not None:
        value = value + out_in[:, cols].astype(f32)
    out_ref[:, cols] = value.astype(out_ref.dtype)


def half_columns(ref, half):
    width = ref.shape[1] // 2
    return ref[:, pl.ds(pl.multiple_of(half * width, 128), width)]


def put_chips(ref, block, value):
    chips, rows = ref.shape[0], ref.shape[2]
    for j in range(chips):
        ref[j, block] = value[j * rows : (j + 1) * rows, :].astype(ref.dtype)


def hidden_weights_kernel(
    core_ref, n2_ref, bg_ref, act_ref, slope_ref, n2_mate, bg_mate, act_mate, slope_mate, keep_ref, send_ref, hb_ref
):
    core = core_ref[0]
    for ref, half in ((send_ref, 1 - core), (keep_ref, core)):
        total = dot(half_columns(n2_ref, half), slope_ref[...], TN)
        put_chips(ref, 0, total + dot(half_columns(n2_mate, half), slope_mate[...], TN))
        total = dot(half_columns(act_ref, half), bg_ref[...], TN)
        put_chips(ref, 1, total + dot(half_columns(act_mate, half), bg_mate[...], TN))
    total = jnp.sum(slope_ref[...].astype(f32), axis=0, keepdims=True)
    hb_ref[...] = total + jnp.sum(slope_mate[...].astype(f32), axis=0, keepdims=True)


def hidden_own_kernel(part, core_ref, n2_ref, bg_ref, w1_ref, w2_ref, hb_ref, *rest):
    if part:
        keep_in, send_in, hb_in = rest[:3]
        rest = rest[3:]
    out, grad, keep_ref, send_ref, hb_grad, act, slope = rest
    hidden_rows_kernel(False, n2_ref, bg_ref, w1_ref, w2_ref, hb_ref, act, slope, out, grad)
    core = core_ref[0]
    chips, _, rows, _ = keep_ref.shape
    sides = [(send_ref, 1 - core), (keep_ref, core)]
    for i, (ref, half) in enumerate(sides):
        for m in range(2):
            if m == 0:
                total = dot(half_columns(n2_ref, half), slope[...], TN)
            else:
                total = dot(half_columns(act, half), bg_ref[...], TN)
            for j in range(chips):
                block = total[j * rows : (j + 1) * rows, :]
                if part:
                    block = block + (send_in, keep_in)[i][j, m].astype(f32)
                ref[j, m] = block.astype(bf16)
    total = jnp.sum(slope[...].astype(f32), axis=0, keepdims=True)
    hb_grad[...] = total + hb_in[...] if part else total


def hidden_first_kernel(place_ref, n2_ref, bg_ref, grad_in, *refs):
    pieces, (first_ref, second_ref, bias_ref, act_ref, slope_ref, grad_ref) = refs[:-6], refs[-6:]
    assemble(place_ref, pieces, first_ref, second_ref, bias_ref)
    weights = Whole(first_ref), Whole(second_ref)
    outs = act_ref, slope_ref, None, grad_ref
    hidden_rows_kernel(True, n2_ref, bg_ref, *weights, bias_ref, None, grad_in, *outs)


class Whole:
    def __init__(self, ref):
        self.ref = ref
        self.slab = ref.shape[1]
        self.shape = (ref.shape[0] * ref.shape[1], ref.shape[2])

    def __getitem__(self, index):
        rows, cols = index
        value = self.ref[:, :, cols]
        return value.reshape(self.shape[0], value.shape[2])[rows, :]


def hidden_both_kernel(core_ref, n2_ref, bg_ref, w1_ref, w2_ref, hb_ref, *rest):
    out_in, grad_in, mate_in, n2_other, bg_other, act_other, slope_other = rest[:7]
    out, grad, mate_out, keep, send, hb_grad, act, slope = rest[7:]
    hidden_rows_kernel(True, n2_ref, bg_ref, w1_ref, w2_ref, hb_ref, out_in, grad_in, act, slope, out, grad)
    for f in range(w2_ref.shape[1] // 256):
        hidden_out_columns(act_other, w2_ref, mate_in, mate_out, slice(f * 256, (f + 1) * 256))
    hidden_weights_kernel(
        core_ref, n2_other, bg_other, act_other, slope_other, n2_ref, bg_ref, act, slope, keep, send, hb_grad
    )


def result_kernel(images, patches, middle_ref, cot_ref, own_ref, recv_ref, vec_ref, result_ref, sums_ref):
    vec = lambda i: vec_ref[i : i + 1, :]
    scale_sum = jnp.zeros((1, middle_ref.shape[1]), f32)
    bias_sum = jnp.zeros((1, middle_ref.shape[1]), f32)
    for n in range(images):
        rows = slice(n * ROWS, n * ROWS + patches)
        cot = cot_ref[n].astype(f32)
        full = own_ref[rows, :].astype(f32) + recv_ref[rows, :].astype(f32) + vec(OUTPUT_BIAS)
        result_ref[n] = (middle_ref[rows, :] + vec(SCALE_HIDDEN) * full).astype(bf16)
        scale_sum = scale_sum + jnp.sum(cot * full, axis=0, keepdims=True)
        low = (vec(SCALE_HIDDEN) * cot).astype(bf16).astype(f32)
        bias_sum = bias_sum + jnp.sum(low, axis=0, keepdims=True)
    sums_ref[0:1, :] = bias_sum
    sums_ref[1:2, :] = scale_sum


def norm_back(grad, hat, rate, gain):
    scaled = grad * gain
    mean = jnp.mean(scaled, axis=-1, keepdims=True)
    cross = jnp.mean(scaled * hat, axis=-1, keepdims=True)
    return rate * (scaled - mean - hat * cross)


def attention_back(
    images, heads, packed_ref, attend_ref, mixed_grad, packed_grad, spread_ref, class_ref, table_ref
):
    width = mixed_grad.shape[1]
    first = lax.broadcasted_iota(jnp.int32, (1, 128), 1) < 64
    lane = lax.broadcasted_iota(jnp.int32, (ROWS, ROWS), 1)
    inner = (2 * GRID - 1) ** 2
    lane_out = lax.broadcasted_iota(jnp.int32, (1, LANES), 1)
    table_ref[...] = jnp.zeros(table_ref.shape, f32)
    spread_ref[...] = jnp.zeros(spread_ref.shape, f32)
    class_ref[...] = jnp.zeros(class_ref.shape, f32)
    for pair in range(heads // 2):
        cols = [slice(k * width + pair * 128, k * width + (pair + 1) * 128) for k in range(3)]
        totals = [None, None]
        for n in range(images):
            rows = slice(n * ROWS, (n + 1) * ROWS)
            q, k, v = (packed_ref[rows, c] for c in cols)
            back = mixed_grad[rows, cols[0]]
            zero = jnp.zeros_like(back)
            grads = []
            for side in range(2):
                h = pair * 2 + side
                keep = first if side == 0 else jnp.logical_not(first)
                attend = attend_ref[n * heads + h]
                wide = attend.astype(f32)
                attend_grad = dot(jnp.where(keep, back, zero), v, NT)
                carried = jnp.sum(wide * attend_grad, axis=-1, keepdims=True)
                low = (wide * (attend_grad - carried)).astype(bf16)
                totals[side] = low.astype(f32) if n == 0 else totals[side] + low.astype(f32)
                scaled = low * jnp.asarray(0.125, bf16)
                grads.append((dot(scaled, k), dot(scaled, q, TN), dot(attend, back, TN)))
            for i in range(3):
                packed_grad[rows, cols[i]] = jnp.where(first, grads[0][i], grads[1][i]).astype(bf16)
        for side in range(2):
            h = pair * 2 + side
            total = totals[side]
            top = total[0:1, :]
            corner = top[:, 0:1]
            from_class = jnp.sum(top, axis=-1, keepdims=True) - corner
            to_class = jnp.sum(total[:, 0:1], axis=0, keepdims=True) - corner
            class_ref[h : h + 1, :] = (
                jnp.where(lane_out == inner, from_class, 0.0)
                + jnp.where(lane_out == inner + 1, to_class, 0.0)
                + jnp.where(lane_out == inner + 2, corner, 0.0)
            )
            table_ref[:, :ROWS] = jnp.where(lane == 0, 0.0, total)
            gathered = jnp.zeros((GRID, SPREAD), f32)
            for y in range(GRID):
                block = table_ref[1 + GRID * y : 1 + GRID * (y + 1), :]
                gathered = gathered + pltpu.roll(block, (GRID * (GRID - 1 - y) - 1) % SPREAD, 1)
            for x in range(GRID):
                spread_ref[x * 16 + h : x * 16 + h + 1, :] = gathered[x : x + 1, :]


def backward_zero_kernel(
    images,
    patches,
    cot_ref,
    middle_ref,
    branch_ref,
    own_ref,
    recv_ref,
    mixing_out_ref,
    vec_ref,
    middle_grad,
    mixed_grad,
    low_ref,
    sums_ref,
):
    width = middle_ref.shape[1]
    vec = lambda i: vec_ref[i : i + 1, :]
    column_sum = lambda v: jnp.sum(v, axis=0, keepdims=True)
    for n in range(images):
        middle_grad[n * ROWS + 192 : (n + 1) * ROWS, :] = jnp.zeros((ROWS - 192, width), f32)
        middle_grad[n * ROWS : n * ROWS + patches, :] = cot_ref[n].astype(f32)
    sums = [jnp.zeros((1, width), f32) for _ in range(4)]
    for n in range(images):
        rows = slice(n * ROWS, (n + 1) * ROWS)
        grad = own_ref[rows, :].astype(f32) + recv_ref[rows, :].astype(f32)
        hat, rate = norm_parts(middle_ref[rows, :])
        sums[0] = sums[0] + column_sum(grad * hat)
        sums[1] = sums[1] + column_sum(grad)
        total = middle_grad[rows, :] + norm_back(grad, hat, rate, vec(SECOND_GAIN))
        middle_grad[rows, :] = total
        sums[2] = sums[2] + column_sum(total * branch_ref[rows, :].astype(f32))
        low = (vec(SCALE_ATTENTION) * total).astype(bf16)
        sums[3] = sums[3] + column_sum(low.astype(f32))
        low_ref[rows, :] = low
    for i, at in enumerate((2, 3, 1, 0)):
        sums_ref[at : at + 1, :] = sums[i]
    mixed_grad[...] = dot(low_ref[...], mixing_out_ref[...], NT).astype(bf16)


def backward_one_kernel(
    images,
    heads,
    part,
    core_ref,
    low_ref,
    mixed_ref,
    mixed_grad,
    packed_ref,
    attend_ref,
    normed_ref,
    packed_grad,
    spread_ref,
    class_ref,
    keep_one,
    send_one,
    keep_two,
    send_two,
    table_ref,
):
    core = core_ref[0]
    order = ((send_one, send_two, 1 - core), (keep_one, keep_two, core))
    for one, _, half in order:
        for b in range(2):
            put_chips(one, b, dot(half_columns(mixed_ref, half), low_ref[:, b * part : (b + 1) * part], TN))
    attention_back(images, heads, packed_ref, attend_ref, mixed_grad, packed_grad, spread_ref, class_ref, table_ref)
    packed_grad.done()
    for one, two, half in order:
        for b in range(6):
            value = dot(half_columns(normed_ref, half), packed_grad[:, b * part : (b + 1) * part], TN)
            put_chips(two if b % 2 else one, b // 2 if b % 2 else 2 + b // 2, value)
        one.done()
        two.done()


def backward_three_kernel(
    images,
    heads,
    patches,
    tok_ref,
    middle_grad,
    packed_grad,
    spread_ref,
    class_ref,
    sums_one,
    mixing_in_ref,
    vec_ref,
    token_grad_ref,
    sums_ref,
    tok_pad,
):
    width = tok_ref.shape[2]
    vec = lambda i: vec_ref[i : i + 1, :]
    column_sum = lambda v: jnp.sum(v, axis=0, keepdims=True)
    onehot = spread_onehot().astype(bf16)
    value = spread_ref[...]
    high = value.astype(bf16)
    rest = (value - high.astype(f32)).astype(bf16)
    spread = dot(high, onehot, NT) + dot(rest, onehot, NT)
    entries = class_ref[...]
    for x in range(GRID):
        block = spread[x * 16 : (x + 1) * 16, :]
        entries = entries + (pltpu.roll(block, LANES - x, 1) if x else block)
    sums_ref[8:24, :] = entries
    sums_ref[0:4, :] = sums_one[0:4, :]
    sums_ref[6:7, :] = column_sum(packed_grad[:, :width].astype(f32))
    sums_ref[7:8, :] = column_sum(packed_grad[:, 2 * width :].astype(f32))
    sums = [jnp.zeros((1, width), f32) for _ in range(2)]
    for n in range(images):
        rows = slice(n * ROWS, (n + 1) * ROWS)
        grad = dot(packed_grad[rows, :], mixing_in_ref[...], NT)
        tok_pad[192:ROWS, :] = jnp.zeros((ROWS - 192, width), f32)
        tok_pad[:patches, :] = tok_ref[n].astype(f32)
        hat, rate = norm_parts(tok_pad[...])
        sums[0] = sums[0] + column_sum(grad * hat)
        sums[1] = sums[1] + column_sum(grad)
        total = middle_grad[rows, :] + norm_back(grad, hat, rate, vec(FIRST_GAIN))
        token_grad_ref[n] = total[:patches, :].astype(bf16)
    sums_ref[4:5, :] = sums[0]
    sums_ref[5:6, :] = sums[1]


def add_kernel(chip_ref, *refs):
    chip = chip_ref[0]
    chips = refs[0].shape[0]
    pairs, outs = refs[:-chips], refs[-chips:]
    for k, out in enumerate(outs):
        for i in range(0, len(pairs), 2):
            total = pairs[i][chip ^ k].astype(f32) + pairs[i + 1][chip ^ k].astype(f32)
            out[i // 2] = total.astype(bf16)


def add_two_kernel(keep_ref, recv_ref, out_ref):
    out_ref[...] = (keep_ref[...].astype(f32) + recv_ref[...].astype(f32)).astype(bf16)


def add_single_kernel(one_ref, two_ref, out_ref):
    out_ref[...] = one_ref[...] + two_ref[...]


def share_kernel(line_ref, near_ref, far_ref, sums_ref, out_sums_ref, hb_near, hb_far, out_ref, small):
    rows = near_ref.shape[1]
    for m in range(2):
        total = near_ref[m].astype(f32) + far_ref[m].astype(f32)
        out_ref[m * rows : (m + 1) * rows, :] = total.astype(bf16)
    count = sums_ref.shape[0]
    small[...] = jnp.zeros(small.shape, f32)
    small[0:count, :] = sums_ref[...]
    small[count : count + 2, :] = out_sums_ref[...]
    small[pl.ds(count + 2 + line_ref[0], 1), :] = hb_near[...]
    small[pl.ds(count + 2 + line_ref[1], 1), :] = hb_far[...]
    out_ref[2 * rows :, :] = small[...].astype(bf16)


def sum_sums_kernel(*refs):
    count = refs[-1].shape[0]
    at = slice(refs[0].shape[0] - count, refs[0].shape[0])
    total = refs[0][at, :].astype(f32)
    for ref in refs[1:-1]:
        total = total + ref[at, :].astype(f32)
    refs[-1][...] = total


def add_spread_kernel(one_ref, two_ref, out_ref):
    total = (one_ref[...].astype(f32) + two_ref[...].astype(f32)).astype(bf16)
    for j in range(out_ref.shape[0]):
        out_ref[j] = total


def sum_pair_kernel(*refs):
    count = (len(refs) - 2) // 2
    for parts, out in ((refs[:count], refs[-2]), (refs[count:-2], refs[-1])):
        total = parts[0][0].astype(f32)
        for ref in parts[1:]:
            total = total + ref[0].astype(f32)
        out[...] = total.astype(bf16)


def sum_all_kernel(parts_ref, total_ref):
    total = parts_ref[0].astype(f32)
    for j in range(1, parts_ref.shape[0]):
        total = total + parts_ref[j].astype(f32)
    total_ref[...] = total.astype(bf16)


def assemble(place_ref, refs, first_ref, second_ref, bias_ref):
    core, chip = place_ref[0], place_ref[1]
    chips, slab, _ = first_ref.shape

    def put(mine, other):
        for k in range(chips):
            mine[chip ^ k] = refs[k][:slab, :]
            other[chip ^ k] = refs[chips + k][:slab, :]

    @pl.when(core == 0)
    def _():
        put(first_ref, second_ref)

    @pl.when(core != 0)
    def _():
        put(second_ref, first_ref)

    bias_ref[...] = refs[0][slab : slab + 8, :].astype(f32)[0:1, :]


def sum_kernel(*refs):
    total = refs[0][...].astype(f32)
    for ref in refs[1:-1]:
        total = total + ref[...].astype(f32)
    refs[-1][...] = total.astype(bf16)


def hidden_final_kernel(place_ref, *refs):
    core, chip = place_ref[0], place_ref[1]
    in_ref, out_ref = refs[-2:]
    chips = (len(refs) - 2) // 2
    for k in range(chips):
        for ref, half in ((refs[k], core), (refs[chips + k], 1 - core)):
            rows = in_ref.shape[2]
            in_ref[half, chip ^ k] = ref[:rows, :].astype(f32)
            out_ref[half, chip ^ k] = ref[rows : 2 * rows, :].astype(f32)


def mixing_one_kernel(place_ref, *refs):
    core, chip = place_ref[0], place_ref[1]
    in_ref, out_ref = refs[-2:]
    chips = (len(refs) - 2) // 4
    first = pl.program_id(0) == 0
    for k in range(chips):
        for ref, half in ((refs[k], core), (refs[chips + k], 1 - core)):
            in_ref[half, chip ^ k] = ref[0].astype(f32)

    @pl.when(first)
    def _():
        for k in range(chips):
            for ref, half in ((refs[2 * chips + k], core), (refs[3 * chips + k], 1 - core)):
                part = ref.shape[2]
                for b in range(2):
                    out_ref[half, chip ^ k, :, b * part : (b + 1) * part] = ref[b].astype(f32)


def mixing_two_kernel(place_ref, before_ref, mine_ref, recv_ref, in_ref):
    core = place_ref[0]
    for j in range(mine_ref.shape[0]):
        for ref, half in ((mine_ref, core), (recv_ref, 1 - core)):
            in_ref[half, j] = ref[j, 0].astype(f32)


def per_device(
    n_dp,
    n_tp,
    tokens,
    first_gain,
    first_shift,
    mixing_in,
    query_bias,
    value_bias,
    relative_table,
    mixing_out,
    out_bias,
    scale_attention,
    second_gain,
    second_shift,
    hidden_in,
    hidden_bias,
    hidden_out,
    output_bias,
    scale_hidden,
    cotangent,
):
    images, patches, width = tokens.shape
    heads = relative_table.shape[1]
    count = images * ROWS
    hidden = hidden_in.shape[1]
    chips = n_dp // 2
    half = width // 2
    part = half
    chip_rows = half // chips
    plane = [[2 * i + c for i in range(chips)] for c in range(2)]
    dp, tp = lax.axis_index("dp"), lax.axis_index("tp")
    core, chip = dp % 2, dp // 2
    mate = lambda a: lax.ppermute(a, "tp", [(i, i ^ 1) for i in range(n_tp)])
    far = lambda a: lax.ppermute(a, "tp", [(i, i ^ 2) for i in range(n_tp)])
    twin = lambda a: lax.ppermute(a, "dp", [(i, i ^ 1) for i in range(n_dp)])
    over_plane = lambda a: lax.all_to_all(a, "dp", 0, 0, axis_index_groups=plane, tiled=True)
    over_line = lambda a: lax.all_to_all(a, "tp", 0, 0, tiled=True)
    copies = lambda a, n: jnp.broadcast_to(a[None], (n, *a.shape))
    by_core = lambda a, b: (jnp.where(core == 0, a, b), jnp.where(core == 0, b, a))
    add = lambda a, b: (a.astype(f32) + b.astype(f32)).astype(bf16)
    def hop(value, k):
        return lax.ppermute(value, "dp", [(i, i ^ (2 * k)) for i in range(n_dp)])

    def to_chips(values):
        if chips <= 4:
            return [hop(value, k) for k, value in enumerate(values) if k]
        order = lambda a, k: lax.dynamic_index_in_dim(a, chip ^ k, 0, keepdims=False)
        stacked = jnp.stack(values)
        stacked = jnp.stack([order(stacked, j) for j in range(chips)])
        stacked = over_plane(stacked)
        return [order(stacked, k) for k in range(1, chips)]

    shape = jax.ShapeDtypeStruct
    core_index = core.astype(jnp.int32).reshape(1)
    chip_index = chip.astype(jnp.int32).reshape(1)
    place = jnp.concatenate([core_index, chip_index])
    rows = (count, width)

    order = Order()
    tie, step = order.tie, order.step

    slab = width // chips
    piece = lax.dynamic_slice_in_dim(jnp.where(core == 0, hidden_in, hidden_out), chip * slab, slab, 0)
    piece = jnp.concatenate([piece, jnp.broadcast_to(hidden_bias[None], (16, hidden))])
    far_piece = far(step(piece))
    bg = (scale_hidden.astype(f32) * tie(cotangent).astype(f32)).astype(bf16)
    bg = step(jnp.pad(bg, ((0, 0), (0, ROWS - patches), (0, 0))).reshape(rows))
    bg_mate = mate(bg)

    vecs = jnp.stack(
        [
            first_gain,
            first_shift,
            query_bias,
            value_bias,
            out_bias,
            scale_attention,
            second_gain,
            second_shift,
            output_bias,
            scale_hidden,
        ]
    ).astype(f32)
    inner = (2 * GRID - 1) ** 2
    table = relative_table.astype(f32)
    table = jnp.concatenate([table[:inner][::-1], table[inner:]]).T
    table = jnp.pad(table, ((0, 0), (0, LANES - table.shape[1])))

    normed, packed, attend, mixed, branch, middle, n2 = call(
        functools.partial(forward_kernel, images, heads),
        "attention_forward",
        [
            shape(rows, bf16),
            shape((count, 3 * width), bf16),
            shape((images * heads, ROWS, ROWS), bf16),
            shape(rows, bf16),
            shape(rows, bf16),
            shape(rows, f32),
            shape(rows, bf16),
        ],
        [
            pltpu.VMEM(rows, f32),
            pltpu.VMEM((heads * 16, LANES), f32),
            pltpu.VMEM((heads, ROWS, 256), f32),
        ],
        stream=True,
    )(tokens, tie(vecs), mixing_in, table, mixing_out)

    n2_mate = mate(step(n2))
    pieces = step(tie(far_piece))
    pieces = [pieces, *to_chips([pieces] * chips)]

    weight = shape((chips, 2, half // chips, width), bf16)
    low_rows = shape(rows, bf16)
    hidden_cols = shape((count, hidden), bf16)

    def hidden_rows(name, n2, bg, w1, w2, bias, carried):
        return call(
            functools.partial(hidden_rows_kernel, bool(carried)),
            name,
            [hidden_cols, hidden_cols, low_rows, low_rows],
        )(n2, bg, w1, w2, tie(bias), *carried)

    near_bias = hidden_bias.astype(f32)[None]
    def hidden_own(name, n2, bg, part):
        return call(
            functools.partial(hidden_own_kernel, bool(part)),
            name,
            [low_rows, low_rows, weight, weight, shape((1, hidden), f32)],
            [pltpu.VMEM((count, hidden), bf16), pltpu.VMEM((count, hidden), bf16)],
            scalars=1,
        )(tie(core_index), n2, bg, hidden_in, hidden_out, near_bias, *part)

    out_own, grad_own, *near = hidden_own("hidden_near_own", n2, bg, ())
    step(out_own)
    bg_mate = step(tie(bg_mate))
    n2_mate = step(tie(n2_mate))
    pieces = [step(tie(a)) for a in pieces]
    other_pieces = [twin(a) for a in pieces]
    out_mate, grad_mate, keep_near, send_near, hb_near = hidden_own("hidden_near_mate", n2_mate, bg_mate, near)
    recv_near = twin(step(send_near))
    slabs = shape((chips, slab, hidden), bf16)
    far_in, far_out, far_bias, act_fm, slope_fm, grad_mate = call(
        hidden_first_kernel,
        "hidden_far_mate",
        [slabs, slabs, shape((1, hidden), f32), hidden_cols, hidden_cols, low_rows],
        scalars=1,
    )(tie(place), n2_mate, bg_mate, grad_mate, *pieces, *other_pieces)
    far_in, far_out = far_in.reshape(width, hidden), far_out.reshape(width, hidden)
    grad_recv = mate(step(grad_mate))
    block = shape((1, 2, chip_rows, width), bf16)
    nears = call(add_kernel, "add_near", [block] * chips, scalars=1)(tie(chip_index), keep_near, recv_near)
    step(nears[0])
    nears = [nears[0], *to_chips(nears)]
    out_own, grad_own, out_mate, keep_far, send_far, hb_far = call(
        hidden_both_kernel,
        "hidden_far_own",
        [low_rows, low_rows, low_rows, weight, weight, shape((1, hidden), f32)],
        [pltpu.VMEM((count, hidden), bf16), pltpu.VMEM((count, hidden), bf16)],
        scalars=1,
    )(
        tie(core_index),
        n2,
        bg,
        far_in,
        far_out,
        far_bias,
        out_own,
        grad_own,
        out_mate,
        n2_mate,
        bg_mate,
        act_fm,
        slope_fm,
    )
    out_recv = mate(step(out_mate))
    recv_far = twin(step(send_far))

    spread, classes = shape((GRID * 16, SPREAD), f32), shape((16, LANES), f32)
    nears = [step(tie(a)) for a in nears]
    middle_grad, mixed_grad, attention_grad, sums_one = call(
        functools.partial(backward_zero_kernel, images, patches),
        "backward_zero",
        [shape(rows, f32), shape(rows, bf16), shape(rows, bf16), shape((4, width), f32)],
    )(cotangent, middle, branch, grad_own, grad_recv, mixing_out, tie(vecs))
    step(attention_grad)
    fars = call(add_kernel, "add_far", [block] * chips, scalars=1)(tie(chip_index), keep_far, recv_far)
    step(fars[0])
    fars = [fars[0], *to_chips(fars)]
    packed_grad, spread, classes, keep_one, send_one, keep_two, send_two = call(
        functools.partial(backward_one_kernel, images, heads, part),
        "backward_one",
        [
            shape((count, 3 * width), bf16),
            spread,
            classes,
            shape((chips, 5, chip_rows, part), bf16),
            shape((chips, 5, chip_rows, part), bf16),
            shape((chips, 3, chip_rows, part), bf16),
            shape((chips, 3, chip_rows, part), bf16),
        ],
        [pltpu.VMEM((ROWS, SPREAD), f32)],
        scalars=1,
        stream=True,
    )(tie(core_index), attention_grad, mixed, mixed_grad, packed, attend, normed)
    step(send_one)
    recv_one = twin(send_one)
    recv_two = twin(send_two)
    share_near, share_far = call(sum_pair_kernel, "sum_hidden", [shape((2, chip_rows, width), bf16)] * 2)(
        *nears, tie(fars[0]), *fars[1:]
    )
    share_far = far(step(share_far))
    block = shape((1, 5, chip_rows, part), bf16)
    ones = call(add_kernel, "add_one", [block] * chips, scalars=1)(tie(chip_index), keep_one, recv_one)
    step(ones[0])
    ones = [ones[0], *to_chips(ones)]
    token_grad, sums = call(
        functools.partial(backward_three_kernel, images, heads, patches),
        "backward_three",
        [shape(tokens.shape, bf16), shape((24, width), f32)],
        [pltpu.VMEM((ROWS, width), f32)],
    )(
        tokens,
        middle_grad,
        packed_grad,
        spread,
        classes,
        sums_one,
        mixing_in,
        tie(vecs),
    )
    step(token_grad)
    two_shape = shape((3, chip_rows, part), bf16)
    (twos,) = call(add_two_kernel, "add_two", [shape(keep_two.shape, bf16)])(tie(keep_two), recv_two)
    twos = over_plane(step(twos))
    share_far = step(tie(share_far))
    result, sums_out = call(
        functools.partial(result_kernel, images, patches),
        "result",
        [shape(tokens.shape, bf16), shape((2, width), f32)],
    )(middle, cotangent, out_own, out_recv, tie(vecs))
    step(sums_out)
    (one,) = call(sum_kernel, "sum_one", [block])(tie(ones[0]), *ones[1:])
    one_near = mate(step(one))
    line_index = jnp.stack([tp, tp ^ 2]).astype(jnp.int32)
    (share,) = call(
        share_kernel,
        "share",
        [shape((2 * chip_rows + 32, width), bf16)],
        [pltpu.VMEM((32, width), f32)],
        scalars=1,
    )(line_index, share_near, tie(share_far), sums, sums_out, hb_near, hb_far)
    step(share)
    share = [share, *to_chips([share] * chips)]
    (two,) = call(sum_all_kernel, "sum_two", [two_shape])(tie(twos))
    two_near = mate(step(two))
    (one,) = call(add_two_kernel, "add_line_one", [block])(one, tie(one_near))
    one_far = far(step(one))
    (two,) = call(add_two_kernel, "add_line_two", [two_shape])(two, tie(two_near))
    two_far = far(step(two))
    share = [step(tie(a)) for a in share]
    (sums,) = call(sum_sums_kernel, "sum_sums", [shape((32, width), f32)])(*share)
    sums_near = mate(step(sums))
    share_recv = [twin(a) for a in share]
    (one,) = call(add_two_kernel, "last_one", [shape(block.shape[1:], bf16)])(one[0], tie(one_far)[0])
    step(one)
    one = [one, *to_chips([one] * chips)]
    wide = shape((2, chips, chip_rows, width), f32)
    hidden_in_grad, hidden_out_grad = call(hidden_final_kernel, "hidden_final", [wide, wide], scalars=1)(
        tie(place), *share, *share_recv
    )
    step(hidden_in_grad)
    (sums,) = call(add_single_kernel, "add_sums", [shape((32, width), f32)])(sums, tie(sums_near))
    sums_far = far(step(sums))
    (two,) = call(add_spread_kernel, "spread_two", [shape((chips, *two_shape.shape), bf16)])(two, tie(two_far))
    two = over_plane(step(two))
    one = [step(tie(a)) for a in one]
    one_recv = [twin(a) for a in one]
    scalar = pl.BlockSpec(memory_space=pltpu.SMEM)
    third = (1, chip_rows, part)
    params = pltpu.CompilerParams(vmem_limit_bytes=2 * SMALL)
    in_shape = shape((2, chips, chip_rows, 3 * width), f32)
    mixing_in_grad, mixing_out_grad = pl.pallas_call(
        mixing_one_kernel,
        grid=(3,),
        out_shape=(in_shape, wide),
        in_specs=[scalar]
        + [pl.BlockSpec(third, lambda b: (2 + b, 0, 0))] * (2 * chips)
        + [pl.BlockSpec((2, chip_rows, part), lambda b: (0, 0, 0))] * (2 * chips),
        out_specs=(
            pl.BlockSpec((2, chips, chip_rows, part), lambda b: (0, 0, 0, 2 * b)),
            pl.BlockSpec((2, chips, chip_rows, width), lambda b: (0, 0, 0, 0)),
        ),
        name="mixing_one",
        compiler_params=params,
        cost_estimate=cost(0.01),
    )(tie(place), *one, *one_recv, *one, *one_recv)
    step(mixing_out_grad)
    (sums,) = call(add_single_kernel, "add_sums_far", [shape((32, width), f32)])(sums, tie(sums_far))
    sums = step(sums + twin(step(sums)))
    table_grad = sums[8 : 8 + heads].T
    table_grad = jnp.concatenate([table_grad[:inner][::-1], table_grad[inner : relative_table.shape[0]]])
    hidden_bias_grad = lax.dynamic_index_in_dim(sums[26 : 26 + n_tp], tp, 0, keepdims=False)
    step(table_grad)
    two = tie(two)
    mixing_in_grad = pl.pallas_call(
        mixing_two_kernel,
        grid=(3,),
        out_shape=in_shape,
        in_specs=[scalar, pl.BlockSpec(memory_space=pl.ANY)]
        + [pl.BlockSpec((chips, *third), lambda b: (0, b, 0, 0))] * 2,
        out_specs=pl.BlockSpec((2, chips, chip_rows, part), lambda b: (0, 0, 0, 2 * b + 1)),
        input_output_aliases={1: 0},
        name="mixing_two",
        compiler_params=params,
        cost_estimate=cost(0.01),
    )(place, mixing_in_grad, two, twin(two))

    return (
        result,
        token_grad,
        sums[4],
        sums[5],
        mixing_in_grad.reshape(width, 3 * width),
        sums[6],
        sums[7],
        table_grad,
        mixing_out_grad.reshape(width, width),
        sums[0],
        sums[1],
        sums[2],
        sums[3],
        hidden_in_grad.reshape(width, width),
        hidden_bias_grad,
        hidden_out_grad.reshape(width, width),
        sums[24],
        sums[25],
    )


def solution(mesh):
    everywhere = P()
    rows = P("dp", "tp", None)
    hidden = (P(None, "tp"), P("tp"), P("tp", None))
    return jax.shard_map(
        functools.partial(per_device, mesh.shape["dp"], mesh.shape["tp"]),
        mesh=mesh,
        in_specs=(rows, *[everywhere] * 11, *hidden, everywhere, everywhere, rows),
        out_specs=(rows, rows, *[everywhere] * 11, *hidden, everywhere, everywhere),
        check_vma=False,
    )
```

```python
import functools

import jax
import jax.numpy as jnp
from jax import lax
from jax.experimental import pallas as pl
from jax.experimental.pallas import tpu as pltpu
from jax.sharding import PartitionSpec as P

GRID = 14
EPSILON = 1e-06
ROWS = 208
LANES = 768
SPREAD = 384
VMEM = 56 * 1024 * 1024
SMALL = 8 * 1024 * 1024
LIGHT = ("add", "sum", "share", "last", "spread")

f32 = jnp.float32
bf16 = jnp.bfloat16

NN = (((1,), (0,)), ((), ()))
NT = (((1,), (1,)), ((), ()))
TN = (((0,), (0,)), ((), ()))

(
    FIRST_GAIN,
    FIRST_SHIFT,
    QUERY_BIAS,
    VALUE_BIAS,
    OUT_BIAS,
    SCALE_ATTENTION,
    SECOND_GAIN,
    SECOND_SHIFT,
    OUTPUT_BIAS,
    SCALE_HIDDEN,
) = range(10)


def dot(a, b, dims=NN):
    return lax.dot_general(a, b, dims, preferred_element_type=f32)


class Order:
    def __init__(self):
        self.last = None

    def tie(self, value):
        if self.last is not None:
            value, _ = lax.optimization_barrier((value, self.last))
        return value

    def step(self, value):
        self.last = value
        return value


US = {
    "hidden_near_own": 3,
    "hidden_near_mate": 20,
    "hidden_far_mate": 20,
    "backward_zero": 20,
    "backward_three": 20,
    "sum_hidden": 20,
    "sum_two": 0.01,
    "sum_one": 20,
}


def cost(us):
    return pl.CostEstimate(flops=int(us * 1.15e9), bytes_accessed=1000, transcendentals=0)


class Arriving:
    def __init__(self, ref, copy):
        self.ref, self.copy, self.shape = ref, copy, ref.shape

    def __getitem__(self, index):
        if self.copy is not None:
            self.copy.wait()
            self.copy = None
        return self.ref[index]


class Leaving:
    def __init__(self, ref, target, semaphores):
        self.ref, self.target, self.semaphores = ref, target, semaphores
        self.shape, self.dtype, self.copies = ref.shape, ref.dtype, []

    def __getitem__(self, index):
        return self.ref[index]

    def __setitem__(self, index, value):
        self.ref[index] = value

    def done(self, index=None):
        source = self.ref if index is None else self.ref.at[index]
        target = self.target if index is None else self.target.at[index]
        self.copies.append(pltpu.make_async_copy(source, target, self.semaphores.at[len(self.copies)]))
        self.copies[-1].start()


LARGE = 1 << 16


def streamed(kernel, n_in, n_out, scalars, moved, sent, n_own):
    def body(*refs):
        ins, rest = list(refs[:n_in]), refs[n_in:]
        targets, rest = list(rest[:n_out]), rest[n_out:]
        own, rest = rest[:n_own], rest[n_own:]
        buffers, (in_sem, out_sem) = list(rest[:-2]), rest[-2:]
        for i in range(n_in):
            if moved[i]:
                copy = pltpu.make_async_copy(ins[i], buffers[0], in_sem.at[i])
                copy.start()
                ins[i] = Arriving(buffers.pop(0), copy)
        leaving = []
        for o in range(n_out):
            if sent[o]:
                targets[o] = Leaving(buffers.pop(0), targets[o], out_sem.at[o])
                leaving.append(targets[o])
        kernel(*ins, *targets, *own)
        for ref in ins:
            if isinstance(ref, Arriving) and ref.copy is not None:
                ref.copy.wait()
        for ref in leaving:
            if not ref.copies:
                ref.done()
        for ref in leaving:
            for copy in ref.copies:
                copy.wait()

    return body


def call(kernel, name, outs, scratch=(), scalars=0, stream=False):
    def run(*args):
        size = lambda a: a.size * a.dtype.itemsize
        moved = [stream and i >= scalars and size(a) > LARGE for i, a in enumerate(args)]
        sent = [stream and size(o) > LARGE for o in outs]
        vmem, smem = pl.BlockSpec(memory_space=pltpu.VMEM), pl.BlockSpec(memory_space=pltpu.SMEM)
        anywhere = pl.BlockSpec(memory_space=pl.ANY)
        body, shapes = kernel, list(scratch)
        if stream:
            body = streamed(kernel, len(args), len(outs), scalars, moved, sent, len(scratch))
            shapes += [pltpu.VMEM(a.shape, a.dtype) for i, a in enumerate(args) if moved[i]]
            shapes += [pltpu.VMEM(o.shape, o.dtype) for i, o in enumerate(outs) if sent[i]]
            shapes += [pltpu.SemaphoreType.DMA((len(args),)), pltpu.SemaphoreType.DMA((len(outs), 4))]
        return pl.pallas_call(
            body,
            out_shape=outs,
            in_specs=[smem if i < scalars else anywhere if moved[i] else vmem for i in range(len(args))],
            out_specs=tuple(anywhere if flag else vmem for flag in sent),
            scratch_shapes=shapes,
            name=name,
            compiler_params=pltpu.CompilerParams(
                vmem_limit_bytes=SMALL if name.split("_")[0] in LIGHT else VMEM
            ),
            cost_estimate=cost(US.get(name, 0.01)),
        )(*args)

    return run


def norm_parts(values):
    center = values - jnp.mean(values, axis=-1, keepdims=True)
    spread = jnp.mean(center * center, axis=-1, keepdims=True)
    rate = lax.rsqrt(spread + EPSILON)
    return center * rate, rate


def spread_onehot():
    entry = lax.broadcasted_iota(jnp.int32, (LANES, SPREAD), 0)
    column = lax.broadcasted_iota(jnp.int32, (LANES, SPREAD), 1)
    d = lax.div(column, GRID)
    x = column - d * GRID
    return entry == d * (2 * GRID - 1) + x + GRID - 1


def expand_table(table_ref, spread_ref, bias_ref, heads):
    onehot = spread_onehot().astype(bf16)
    reach = 2 * GRID - 1
    inner = reach * reach
    for h in range(heads):
        rows = jnp.broadcast_to(table_ref[h : h + 1, :], (16, LANES))
        spread_ref[h * 16 : (h + 1) * 16, :] = pltpu.roll(rows, 0, 1, stride=1, stride_axis=0)
    rolled = spread_ref[...].astype(bf16)
    wide = dot(rolled, onehot)
    lane = lax.broadcasted_iota(jnp.int32, (16, 256), 1)
    hidden = lane > GRID * GRID
    for h in range(heads):
        bias_ref[h, 192:ROWS, :] = jnp.where(hidden, -1e30, 0.0)
        own = wide[h * 16 : (h + 1) * 16, :]
        to_class = table_ref[h : h + 1, inner + 1 : inner + 2]
        for y in range(GRID):
            part = pltpu.roll(own, (1 - GRID * (GRID - 1 - y)) % SPREAD, 1)[:, :256]
            part = jnp.where(lane == 0, to_class, jnp.where(hidden, -1e30, part))
            bias_ref[h, 1 + GRID * y : 1 + GRID * (y + 1), :] = part[:GRID, :]
        from_class = table_ref[h : h + 1, inner : inner + 1]
        corner = table_ref[h : h + 1, inner + 2 : inner + 3]
        top = jnp.where(lane == 0, corner, jnp.where(hidden, -1e30, from_class))
        bias_ref[h, 0:1, :] = top[:1, :]


def forward_kernel(
    images,
    heads,
    tok_ref,
    vec_ref,
    mixing_in_ref,
    table_ref,
    mixing_out_ref,
    normed_ref,
    packed_ref,
    attend_ref,
    mixed_ref,
    branch_ref,
    middle_ref,
    n2_ref,
    tok_pad,
    spread_ref,
    bias_ref,
):
    width = tok_ref.shape[2]
    patches = tok_ref.shape[1]
    vec = lambda i: vec_ref[i : i + 1, :]
    expand_table(table_ref, spread_ref, bias_ref, heads)
    for n in range(images):
        lo = n * ROWS
        tok_pad[lo + 192 : lo + ROWS, :] = jnp.zeros((ROWS - 192, width), f32)
        tok_pad[lo : lo + patches, :] = tok_ref[n].astype(f32)
    hat, _ = norm_parts(tok_pad[...])
    normed_ref[...] = (hat * vec(FIRST_GAIN) + vec(FIRST_SHIFT)).astype(bf16)
    normed_ref.done()
    for part in range(3):
        cols = slice(part * width, (part + 1) * width)
        value = dot(normed_ref[...], mixing_in_ref[:, cols])
        if part == 0:
            value = value + vec(QUERY_BIAS)
        if part == 2:
            value = value + vec(VALUE_BIAS)
        packed_ref[:, cols] = value.astype(bf16)
    packed_ref.done()
    first = lax.broadcasted_iota(jnp.int32, (1, 128), 1) < 64
    for n in range(images):
        rows = slice(n * ROWS, (n + 1) * ROWS)
        for pair in range(heads // 2):
            cols = [slice(k * width + pair * 128, k * width + (pair + 1) * 128) for k in range(3)]
            q, k, v = (packed_ref[rows, c] for c in cols)
            q = q * jnp.asarray(0.125, bf16)
            zero = jnp.zeros_like(q)
            outs = []
            for side in range(2):
                h = pair * 2 + side
                keep = first if side == 0 else jnp.logical_not(first)
                scores = dot(jnp.where(keep, q, zero), k, NT) + bias_ref[h, :, :ROWS]
                top = jnp.max(scores, axis=-1, keepdims=True)
                weights = jnp.exp(scores - top)
                total = jnp.sum(weights, axis=-1, keepdims=True)
                attend = (weights * (1.0 / total)).astype(bf16)
                attend_ref[n * heads + h] = attend
                outs.append(dot(attend, v))
            mixed_ref[rows, cols[0]] = jnp.where(first, outs[0], outs[1]).astype(bf16)
        attend_ref.done(pl.ds(n * heads, heads))
    mixed_ref.done()
    branch = dot(mixed_ref[...], mixing_out_ref[...]) + vec(OUT_BIAS)
    branch_ref[...] = branch.astype(bf16)
    branch_ref.done()
    middle = tok_pad[...] + vec(SCALE_ATTENTION) * branch
    middle_ref[...] = middle
    middle_ref.done()
    hat, _ = norm_parts(middle)
    n2_ref[...] = (hat * vec(SECOND_GAIN) + vec(SECOND_SHIFT)).astype(bf16)


def gelu_and_slope(v):
    cdf = 0.5 * (1.0 + lax.erf(v * 0.7071067811865476))
    density = jnp.exp(-0.5 * v * v) * 0.3989422804014327
    return v * cdf, cdf + v * density


def hidden_rows_kernel(carried, n2_ref, bg_ref, w1_ref, w2_ref, hb_ref, *rest):
    if carried:
        out_in, grad_in = rest[:2]
        rest = rest[2:]
    act_ref, slope_ref, out_ref, grad_ref = rest
    width, hidden = w1_ref.shape
    for f in range(hidden // 256):
        cols = slice(f * 256, (f + 1) * 256)
        before = dot(n2_ref[...], w1_ref[:, cols]) + hb_ref[0:1, cols]
        value, slope = gelu_and_slope(before)
        act_ref[:, cols] = value.astype(bf16)
        slope_ref[:, cols] = (dot(bg_ref[...], w2_ref[cols, :], NT) * slope).astype(bf16)
    for f in range(width // 256):
        cols = slice(f * 256, (f + 1) * 256)
        if out_ref is not None:
            hidden_out_columns(act_ref, w2_ref, out_in if carried else None, out_ref, cols)
        back = dot(slope_ref[...], w1_ref[cols, :], NT)
        if carried:
            back = back + grad_in[:, cols].astype(f32)
        grad_ref[:, cols] = back.astype(grad_ref.dtype)


def hidden_out_columns(act_ref, w2_ref, out_in, out_ref, cols):
    value = dot(act_ref[...], w2_ref[:, cols])
    if out_in is not None:
        value = value + out_in[:, cols].astype(f32)
    out_ref[:, cols] = value.astype(out_ref.dtype)


def half_columns(ref, half):
    width = ref.shape[1] // 2
    return ref[:, pl.ds(pl.multiple_of(half * width, 128), width)]


def put_chips(ref, block, value):
    chips, rows = ref.shape[0], ref.shape[2]
    for j in range(chips):
        ref[j, block] = value[j * rows : (j + 1) * rows, :].astype(ref.dtype)


def hidden_weights_kernel(
    core_ref, n2_ref, bg_ref, act_ref, slope_ref, n2_mate, bg_mate, act_mate, slope_mate, keep_ref, send_ref, hb_ref
):
    core = core_ref[0]
    for ref, half in ((send_ref, 1 - core), (keep_ref, core)):
        total = dot(half_columns(n2_ref, half), slope_ref[...], TN)
        put_chips(ref, 0, total + dot(half_columns(n2_mate, half), slope_mate[...], TN))
        total = dot(half_columns(act_ref, half), bg_ref[...], TN)
        put_chips(ref, 1, total + dot(half_columns(act_mate, half), bg_mate[...], TN))
    total = jnp.sum(slope_ref[...].astype(f32), axis=0, keepdims=True)
    hb_ref[...] = total + jnp.sum(slope_mate[...].astype(f32), axis=0, keepdims=True)


def hidden_own_kernel(part, core_ref, n2_ref, bg_ref, w1_ref, w2_ref, hb_ref, *rest):
    if part:
        keep_in, send_in, hb_in = rest[:3]
        rest = rest[3:]
    out, grad, keep_ref, send_ref, hb_grad, act, slope = rest
    hidden_rows_kernel(False, n2_ref, bg_ref, w1_ref, w2_ref, hb_ref, act, slope, out, grad)
    core = core_ref[0]
    chips, _, rows, _ = keep_ref.shape
    sides = [(send_ref, 1 - core), (keep_ref, core)]
    for i, (ref, half) in enumerate(sides):
        for m in range(2):
            if m == 0:
                total = dot(half_columns(n2_ref, half), slope[...], TN)
            else:
                total = dot(half_columns(act, half), bg_ref[...], TN)
            for j in range(chips):
                block = total[j * rows : (j + 1) * rows, :]
                if part:
                    block = block + (send_in, keep_in)[i][j, m].astype(f32)
                ref[j, m] = block.astype(bf16)
    total = jnp.sum(slope[...].astype(f32), axis=0, keepdims=True)
    hb_grad[...] = total + hb_in[...] if part else total


def hidden_first_kernel(place_ref, n2_ref, bg_ref, grad_in, *refs):
    pieces, (first_ref, second_ref, bias_ref, act_ref, slope_ref, grad_ref) = refs[:-6], refs[-6:]
    assemble(place_ref, pieces, first_ref, second_ref, bias_ref)
    weights = Whole(first_ref), Whole(second_ref)
    outs = act_ref, slope_ref, None, grad_ref
    hidden_rows_kernel(True, n2_ref, bg_ref, *weights, bias_ref, None, grad_in, *outs)


class Whole:
    def __init__(self, ref):
        self.ref = ref
        self.slab = ref.shape[1]
        self.shape = (ref.shape[0] * ref.shape[1], ref.shape[2])

    def __getitem__(self, index):
        rows, cols = index
        value = self.ref[:, :, cols]
        return value.reshape(self.shape[0], value.shape[2])[rows, :]


def hidden_both_kernel(core_ref, n2_ref, bg_ref, w1_ref, w2_ref, hb_ref, *rest):
    out_in, grad_in, mate_in, n2_other, bg_other, act_other, slope_other = rest[:7]
    out, grad, mate_out, keep, send, hb_grad, act, slope = rest[7:]
    hidden_rows_kernel(True, n2_ref, bg_ref, w1_ref, w2_ref, hb_ref, out_in, grad_in, act, slope, out, grad)
    for f in range(w2_ref.shape[1] // 256):
        hidden_out_columns(act_other, w2_ref, mate_in, mate_out, slice(f * 256, (f + 1) * 256))
    hidden_weights_kernel(
        core_ref, n2_other, bg_other, act_other, slope_other, n2_ref, bg_ref, act, slope, keep, send, hb_grad
    )


def result_kernel(images, patches, middle_ref, cot_ref, own_ref, recv_ref, vec_ref, result_ref, sums_ref):
    vec = lambda i: vec_ref[i : i + 1, :]
    scale_sum = jnp.zeros((1, middle_ref.shape[1]), f32)
    bias_sum = jnp.zeros((1, middle_ref.shape[1]), f32)
    for n in range(images):
        rows = slice(n * ROWS, n * ROWS + patches)
        cot = cot_ref[n].astype(f32)
        full = own_ref[rows, :].astype(f32) + recv_ref[rows, :].astype(f32) + vec(OUTPUT_BIAS)
        result_ref[n] = (middle_ref[rows, :] + vec(SCALE_HIDDEN) * full).astype(bf16)
        scale_sum = scale_sum + jnp.sum(cot * full, axis=0, keepdims=True)
        low = (vec(SCALE_HIDDEN) * cot).astype(bf16).astype(f32)
        bias_sum = bias_sum + jnp.sum(low, axis=0, keepdims=True)
    sums_ref[0:1, :] = bias_sum
    sums_ref[1:2, :] = scale_sum


def norm_back(grad, hat, rate, gain):
    scaled = grad * gain
    mean = jnp.mean(scaled, axis=-1, keepdims=True)
    cross = jnp.mean(scaled * hat, axis=-1, keepdims=True)
    return rate * (scaled - mean - hat * cross)


def attention_back(
    images, heads, packed_ref, attend_ref, mixed_grad, packed_grad, spread_ref, class_ref, table_ref
):
    width = mixed_grad.shape[1]
    first = lax.broadcasted_iota(jnp.int32, (1, 128), 1) < 64
    lane = lax.broadcasted_iota(jnp.int32, (ROWS, ROWS), 1)
    inner = (2 * GRID - 1) ** 2
    lane_out = lax.broadcasted_iota(jnp.int32, (1, LANES), 1)
    table_ref[...] = jnp.zeros(table_ref.shape, f32)
    spread_ref[...] = jnp.zeros(spread_ref.shape, f32)
    class_ref[...] = jnp.zeros(class_ref.shape, f32)
    for pair in range(heads // 2):
        cols = [slice(k * width + pair * 128, k * width + (pair + 1) * 128) for k in range(3)]
        totals = [None, None]
        for n in range(images):
            rows = slice(n * ROWS, (n + 1) * ROWS)
            q, k, v = (packed_ref[rows, c] for c in cols)
            back = mixed_grad[rows, cols[0]]
            zero = jnp.zeros_like(back)
            q_across, back_across = q.T, back.T
            grads = []
            for side in range(2):
                h = pair * 2 + side
                keep = first if side == 0 else jnp.logical_not(first)
                attend = attend_ref[n * heads + h]
                wide = attend.astype(f32)
                attend_grad = dot(jnp.where(keep, back, zero), v, NT)
                carried = jnp.sum(wide * attend_grad, axis=-1, keepdims=True)
                low = (wide * (attend_grad - carried)).astype(bf16)
                totals[side] = low.astype(f32) if n == 0 else totals[side] + low.astype(f32)
                scaled = low * jnp.asarray(0.125, bf16)
                own = slice(side * 64, side * 64 + 64)
                grads.append((dot(scaled, k), dot(q_across[own, :], scaled), dot(back_across[own, :], attend)))
            packed_grad[rows, cols[0]] = jnp.where(first, grads[0][0], grads[1][0]).astype(bf16)
            for i in range(1, 3):
                both = jnp.concatenate([grads[0][i], grads[1][i]], axis=0).astype(bf16)
                packed_grad[rows, cols[i]] = both.T
        for side in range(2):
            h = pair * 2 + side
            total = totals[side]
            top = total[0:1, :]
            corner = top[:, 0:1]
            from_class = jnp.sum(top, axis=-1, keepdims=True) - corner
            to_class = jnp.sum(total[:, 0:1], axis=0, keepdims=True) - corner
            class_ref[h : h + 1, :] = (
                jnp.where(lane_out == inner, from_class, 0.0)
                + jnp.where(lane_out == inner + 1, to_class, 0.0)
                + jnp.where(lane_out == inner + 2, corner, 0.0)
            )
            table_ref[:, :ROWS] = jnp.where(lane == 0, 0.0, total)
            gathered = jnp.zeros((GRID, SPREAD), f32)
            for y in range(GRID):
                block = table_ref[1 + GRID * y : 1 + GRID * (y + 1), :]
                gathered = gathered + pltpu.roll(block, (GRID * (GRID - 1 - y) - 1) % SPREAD, 1)
            for x in range(GRID):
                spread_ref[x * 16 + h : x * 16 + h + 1, :] = gathered[x : x + 1, :]


def backward_zero_kernel(
    images,
    patches,
    cot_ref,
    middle_ref,
    branch_ref,
    own_ref,
    recv_ref,
    mixing_out_ref,
    vec_ref,
    middle_grad,
    mixed_grad,
    low_ref,
    sums_ref,
):
    width = middle_ref.shape[1]
    vec = lambda i: vec_ref[i : i + 1, :]
    column_sum = lambda v: jnp.sum(v, axis=0, keepdims=True)
    for n in range(images):
        middle_grad[n * ROWS + 192 : (n + 1) * ROWS, :] = jnp.zeros((ROWS - 192, width), f32)
        middle_grad[n * ROWS : n * ROWS + patches, :] = cot_ref[n].astype(f32)
    sums = [jnp.zeros((1, width), f32) for _ in range(4)]
    for n in range(images):
        rows = slice(n * ROWS, (n + 1) * ROWS)
        grad = own_ref[rows, :].astype(f32) + recv_ref[rows, :].astype(f32)
        hat, rate = norm_parts(middle_ref[rows, :])
        sums[0] = sums[0] + column_sum(grad * hat)
        sums[1] = sums[1] + column_sum(grad)
        total = middle_grad[rows, :] + norm_back(grad, hat, rate, vec(SECOND_GAIN))
        middle_grad[rows, :] = total
        sums[2] = sums[2] + column_sum(total * branch_ref[rows, :].astype(f32))
        low = (vec(SCALE_ATTENTION) * total).astype(bf16)
        sums[3] = sums[3] + column_sum(low.astype(f32))
        low_ref[rows, :] = low
    for i, at in enumerate((2, 3, 1, 0)):
        sums_ref[at : at + 1, :] = sums[i]
    mixed_grad[...] = dot(low_ref[...], mixing_out_ref[...], NT).astype(bf16)


def backward_one_kernel(
    images,
    heads,
    part,
    core_ref,
    low_ref,
    mixed_ref,
    mixed_grad,
    packed_ref,
    attend_ref,
    normed_ref,
    packed_grad,
    spread_ref,
    class_ref,
    keep_one,
    send_one,
    keep_two,
    send_two,
    table_ref,
):
    core = core_ref[0]
    order = ((send_one, send_two, 1 - core), (keep_one, keep_two, core))
    for one, _, half in order:
        across = half_columns(mixed_ref, half).T
        for b in range(2):
            put_chips(one, b, dot(across, low_ref[:, b * part : (b + 1) * part]))
    attention_back(images, heads, packed_ref, attend_ref, mixed_grad, packed_grad, spread_ref, class_ref, table_ref)
    packed_grad.done()
    for one, two, half in order:
        across = half_columns(normed_ref, half).T
        for b in range(6):
            value = dot(across, packed_grad[:, b * part : (b + 1) * part])
            put_chips(two if b % 2 else one, b // 2 if b % 2 else 2 + b // 2, value)
        one.done()
        two.done()


def backward_three_kernel(
    images,
    heads,
    patches,
    tok_ref,
    middle_grad,
    packed_grad,
    spread_ref,
    class_ref,
    sums_one,
    mixing_in_ref,
    vec_ref,
    token_grad_ref,
    sums_ref,
    tok_pad,
):
    width = tok_ref.shape[2]
    vec = lambda i: vec_ref[i : i + 1, :]
    column_sum = lambda v: jnp.sum(v, axis=0, keepdims=True)
    onehot = spread_onehot().astype(bf16)
    value = spread_ref[...]
    high = value.astype(bf16)
    rest = (value - high.astype(f32)).astype(bf16)
    spread = dot(high, onehot, NT) + dot(rest, onehot, NT)
    entries = class_ref[...]
    for x in range(GRID):
        block = spread[x * 16 : (x + 1) * 16, :]
        entries = entries + (pltpu.roll(block, LANES - x, 1) if x else block)
    sums_ref[8:24, :] = entries
    sums_ref[0:4, :] = sums_one[0:4, :]
    sums_ref[6:7, :] = column_sum(packed_grad[:, :width].astype(f32))
    sums_ref[7:8, :] = column_sum(packed_grad[:, 2 * width :].astype(f32))
    sums = [jnp.zeros((1, width), f32) for _ in range(2)]
    for n in range(images):
        rows = slice(n * ROWS, (n + 1) * ROWS)
        grad = dot(packed_grad[rows, :], mixing_in_ref[...], NT)
        tok_pad[192:ROWS, :] = jnp.zeros((ROWS - 192, width), f32)
        tok_pad[:patches, :] = tok_ref[n].astype(f32)
        hat, rate = norm_parts(tok_pad[...])
        sums[0] = sums[0] + column_sum(grad * hat)
        sums[1] = sums[1] + column_sum(grad)
        total = middle_grad[rows, :] + norm_back(grad, hat, rate, vec(FIRST_GAIN))
        token_grad_ref[n] = total[:patches, :].astype(bf16)
    sums_ref[4:5, :] = sums[0]
    sums_ref[5:6, :] = sums[1]


def add_kernel(chip_ref, *refs):
    chip = chip_ref[0]
    chips = refs[0].shape[0]
    pairs, outs = refs[:-chips], refs[-chips:]
    for k, out in enumerate(outs):
        for i in range(0, len(pairs), 2):
            total = pairs[i][chip ^ k].astype(f32) + pairs[i + 1][chip ^ k].astype(f32)
            out[i // 2] = total.astype(bf16)


def add_two_kernel(keep_ref, recv_ref, out_ref):
    out_ref[...] = (keep_ref[...].astype(f32) + recv_ref[...].astype(f32)).astype(bf16)


def add_single_kernel(one_ref, two_ref, out_ref):
    out_ref[...] = one_ref[...] + two_ref[...]


def share_kernel(line_ref, near_ref, far_ref, sums_ref, out_sums_ref, hb_near, hb_far, out_ref, small):
    rows = near_ref.shape[1]
    for m in range(2):
        total = near_ref[m].astype(f32) + far_ref[m].astype(f32)
        out_ref[m * rows : (m + 1) * rows, :] = total.astype(bf16)
    count = sums_ref.shape[0]
    small[...] = jnp.zeros(small.shape, f32)
    small[0:count, :] = sums_ref[...]
    small[count : count + 2, :] = out_sums_ref[...]
    small[pl.ds(count + 2 + line_ref[0], 1), :] = hb_near[...]
    small[pl.ds(count + 2 + line_ref[1], 1), :] = hb_far[...]
    out_ref[2 * rows :, :] = small[...].astype(bf16)


def sum_sums_kernel(*refs):
    count = refs[-1].shape[0]
    at = slice(refs[0].shape[0] - count, refs[0].shape[0])
    total = refs[0][at, :].astype(f32)
    for ref in refs[1:-1]:
        total = total + ref[at, :].astype(f32)
    refs[-1][...] = total


def add_spread_kernel(one_ref, two_ref, out_ref):
    total = (one_ref[...].astype(f32) + two_ref[...].astype(f32)).astype(bf16)
    for j in range(out_ref.shape[0]):
        out_ref[j] = total


def sum_pair_kernel(*refs):
    count = (len(refs) - 2) // 2
    for parts, out in ((refs[:count], refs[-2]), (refs[count:-2], refs[-1])):
        total = parts[0][0].astype(f32)
        for ref in parts[1:]:
            total = total + ref[0].astype(f32)
        out[...] = total.astype(bf16)


def sum_all_kernel(parts_ref, total_ref):
    total = parts_ref[0].astype(f32)
    for j in range(1, parts_ref.shape[0]):
        total = total + parts_ref[j].astype(f32)
    total_ref[...] = total.astype(bf16)


def assemble(place_ref, refs, first_ref, second_ref, bias_ref):
    core, chip = place_ref[0], place_ref[1]
    chips, slab, _ = first_ref.shape

    def put(mine, other):
        for k in range(chips):
            mine[chip ^ k] = refs[k][:slab, :]
            other[chip ^ k] = refs[chips + k][:slab, :]

    @pl.when(core == 0)
    def _():
        put(first_ref, second_ref)

    @pl.when(core != 0)
    def _():
        put(second_ref, first_ref)

    bias_ref[...] = refs[0][slab : slab + 8, :].astype(f32)[0:1, :]


def sum_kernel(*refs):
    total = refs[0][...].astype(f32)
    for ref in refs[1:-1]:
        total = total + ref[...].astype(f32)
    refs[-1][...] = total.astype(bf16)


def hidden_final_kernel(place_ref, *refs):
    core, chip = place_ref[0], place_ref[1]
    in_ref, out_ref = refs[-2:]
    chips = (len(refs) - 2) // 2
    for k in range(chips):
        for ref, half in ((refs[k], core), (refs[chips + k], 1 - core)):
            rows = in_ref.shape[2]
            in_ref[half, chip ^ k] = ref[:rows, :].astype(f32)
            out_ref[half, chip ^ k] = ref[rows : 2 * rows, :].astype(f32)


def mixing_one_kernel(place_ref, *refs):
    core, chip = place_ref[0], place_ref[1]
    in_ref, out_ref = refs[-2:]
    chips = (len(refs) - 2) // 4
    first = pl.program_id(0) == 0
    for k in range(chips):
        for ref, half in ((refs[k], core), (refs[chips + k], 1 - core)):
            in_ref[half, chip ^ k] = ref[0].astype(f32)

    @pl.when(first)
    def _():
        for k in range(chips):
            for ref, half in ((refs[2 * chips + k], core), (refs[3 * chips + k], 1 - core)):
                part = ref.shape[2]
                for b in range(2):
                    out_ref[half, chip ^ k, :, b * part : (b + 1) * part] = ref[b].astype(f32)


def mixing_two_kernel(place_ref, before_ref, mine_ref, recv_ref, in_ref):
    core = place_ref[0]
    for j in range(mine_ref.shape[0]):
        for ref, half in ((mine_ref, core), (recv_ref, 1 - core)):
            in_ref[half, j] = ref[j, 0].astype(f32)


def per_device(
    n_dp,
    n_tp,
    tokens,
    first_gain,
    first_shift,
    mixing_in,
    query_bias,
    value_bias,
    relative_table,
    mixing_out,
    out_bias,
    scale_attention,
    second_gain,
    second_shift,
    hidden_in,
    hidden_bias,
    hidden_out,
    output_bias,
    scale_hidden,
    cotangent,
):
    images, patches, width = tokens.shape
    heads = relative_table.shape[1]
    count = images * ROWS
    hidden = hidden_in.shape[1]
    chips = n_dp // 2
    half = width // 2
    part = half
    chip_rows = half // chips
    plane = [[2 * i + c for i in range(chips)] for c in range(2)]
    dp, tp = lax.axis_index("dp"), lax.axis_index("tp")
    core, chip = dp % 2, dp // 2
    mate = lambda a: lax.ppermute(a, "tp", [(i, i ^ 1) for i in range(n_tp)])
    far = lambda a: lax.ppermute(a, "tp", [(i, i ^ 2) for i in range(n_tp)])
    twin = lambda a: lax.ppermute(a, "dp", [(i, i ^ 1) for i in range(n_dp)])
    over_plane = lambda a: lax.all_to_all(a, "dp", 0, 0, axis_index_groups=plane, tiled=True)
    over_line = lambda a: lax.all_to_all(a, "tp", 0, 0, tiled=True)
    copies = lambda a, n: jnp.broadcast_to(a[None], (n, *a.shape))
    by_core = lambda a, b: (jnp.where(core == 0, a, b), jnp.where(core == 0, b, a))
    add = lambda a, b: (a.astype(f32) + b.astype(f32)).astype(bf16)
    def hop(value, k):
        return lax.ppermute(value, "dp", [(i, i ^ (2 * k)) for i in range(n_dp)])

    def to_chips(values):
        if chips <= 4:
            return [hop(value, k) for k, value in enumerate(values) if k]
        order = lambda a, k: lax.dynamic_index_in_dim(a, chip ^ k, 0, keepdims=False)
        stacked = jnp.stack(values)
        stacked = jnp.stack([order(stacked, j) for j in range(chips)])
        stacked = over_plane(stacked)
        return [order(stacked, k) for k in range(1, chips)]

    shape = jax.ShapeDtypeStruct
    core_index = core.astype(jnp.int32).reshape(1)
    chip_index = chip.astype(jnp.int32).reshape(1)
    place = jnp.concatenate([core_index, chip_index])
    rows = (count, width)

    order = Order()
    tie, step = order.tie, order.step

    slab = width // chips
    piece = lax.dynamic_slice_in_dim(jnp.where(core == 0, hidden_in, hidden_out), chip * slab, slab, 0)
    piece = jnp.concatenate([piece, jnp.broadcast_to(hidden_bias[None], (16, hidden))])
    far_piece = far(step(piece))
    bg = (scale_hidden.astype(f32) * tie(cotangent).astype(f32)).astype(bf16)
    bg = step(jnp.pad(bg, ((0, 0), (0, ROWS - patches), (0, 0))).reshape(rows))
    bg_mate = mate(bg)

    vecs = jnp.stack(
        [
            first_gain,
            first_shift,
            query_bias,
            value_bias,
            out_bias,
            scale_attention,
            second_gain,
            second_shift,
            output_bias,
            scale_hidden,
        ]
    ).astype(f32)
    inner = (2 * GRID - 1) ** 2
    table = relative_table.astype(f32)
    table = jnp.concatenate([table[:inner][::-1], table[inner:]]).T
    table = jnp.pad(table, ((0, 0), (0, LANES - table.shape[1])))

    normed, packed, attend, mixed, branch, middle, n2 = call(
        functools.partial(forward_kernel, images, heads),
        "attention_forward",
        [
            shape(rows, bf16),
            shape((count, 3 * width), bf16),
            shape((images * heads, ROWS, ROWS), bf16),
            shape(rows, bf16),
            shape(rows, bf16),
            shape(rows, f32),
            shape(rows, bf16),
        ],
        [
            pltpu.VMEM(rows, f32),
            pltpu.VMEM((heads * 16, LANES), f32),
            pltpu.VMEM((heads, ROWS, 256), f32),
        ],
        stream=True,
    )(tokens, tie(vecs), mixing_in, table, mixing_out)

    n2_mate = mate(step(n2))
    pieces = step(tie(far_piece))
    pieces = [pieces, *to_chips([pieces] * chips)]

    weight = shape((chips, 2, half // chips, width), bf16)
    low_rows = shape(rows, bf16)
    hidden_cols = shape((count, hidden), bf16)

    def hidden_rows(name, n2, bg, w1, w2, bias, carried):
        return call(
            functools.partial(hidden_rows_kernel, bool(carried)),
            name,
            [hidden_cols, hidden_cols, low_rows, low_rows],
        )(n2, bg, w1, w2, tie(bias), *carried)

    near_bias = hidden_bias.astype(f32)[None]
    def hidden_own(name, n2, bg, part):
        return call(
            functools.partial(hidden_own_kernel, bool(part)),
            name,
            [low_rows, low_rows, weight, weight, shape((1, hidden), f32)],
            [pltpu.VMEM((count, hidden), bf16), pltpu.VMEM((count, hidden), bf16)],
            scalars=1,
        )(tie(core_index), n2, bg, hidden_in, hidden_out, near_bias, *part)

    out_own, grad_own, *near = hidden_own("hidden_near_own", n2, bg, ())
    step(out_own)
    bg_mate = step(tie(bg_mate))
    n2_mate = step(tie(n2_mate))
    pieces = [step(tie(a)) for a in pieces]
    other_pieces = [twin(a) for a in pieces]
    out_mate, grad_mate, keep_near, send_near, hb_near = hidden_own("hidden_near_mate", n2_mate, bg_mate, near)
    recv_near = twin(step(send_near))
    slabs = shape((chips, slab, hidden), bf16)
    far_in, far_out, far_bias, act_fm, slope_fm, grad_mate = call(
        hidden_first_kernel,
        "hidden_far_mate",
        [slabs, slabs, shape((1, hidden), f32), hidden_cols, hidden_cols, low_rows],
        scalars=1,
    )(tie(place), n2_mate, bg_mate, grad_mate, *pieces, *other_pieces)
    far_in, far_out = far_in.reshape(width, hidden), far_out.reshape(width, hidden)
    grad_recv = mate(step(grad_mate))
    block = shape((1, 2, chip_rows, width), bf16)
    nears = call(add_kernel, "add_near", [block] * chips, scalars=1)(tie(chip_index), keep_near, recv_near)
    step(nears[0])
    nears = [nears[0], *to_chips(nears)]
    out_own, grad_own, out_mate, keep_far, send_far, hb_far = call(
        hidden_both_kernel,
        "hidden_far_own",
        [low_rows, low_rows, low_rows, weight, weight, shape((1, hidden), f32)],
        [pltpu.VMEM((count, hidden), bf16), pltpu.VMEM((count, hidden), bf16)],
        scalars=1,
    )(
        tie(core_index),
        n2,
        bg,
        far_in,
        far_out,
        far_bias,
        out_own,
        grad_own,
        out_mate,
        n2_mate,
        bg_mate,
        act_fm,
        slope_fm,
    )
    out_recv = mate(step(out_mate))
    recv_far = twin(step(send_far))

    spread, classes = shape((GRID * 16, SPREAD), f32), shape((16, LANES), f32)
    nears = [step(tie(a)) for a in nears]
    middle_grad, mixed_grad, attention_grad, sums_one = call(
        functools.partial(backward_zero_kernel, images, patches),
        "backward_zero",
        [shape(rows, f32), shape(rows, bf16), shape(rows, bf16), shape((4, width), f32)],
    )(cotangent, middle, branch, grad_own, grad_recv, mixing_out, tie(vecs))
    step(attention_grad)
    fars = call(add_kernel, "add_far", [block] * chips, scalars=1)(tie(chip_index), keep_far, recv_far)
    step(fars[0])
    fars = [fars[0], *to_chips(fars)]
    packed_grad, spread, classes, keep_one, send_one, keep_two, send_two = call(
        functools.partial(backward_one_kernel, images, heads, part),
        "backward_one",
        [
            shape((count, 3 * width), bf16),
            spread,
            classes,
            shape((chips, 5, chip_rows, part), bf16),
            shape((chips, 5, chip_rows, part), bf16),
            shape((chips, 3, chip_rows, part), bf16),
            shape((chips, 3, chip_rows, part), bf16),
        ],
        [pltpu.VMEM((ROWS, SPREAD), f32)],
        scalars=1,
        stream=True,
    )(tie(core_index), attention_grad, mixed, mixed_grad, packed, attend, normed)
    step(send_one)
    recv_one = twin(send_one)
    recv_two = twin(send_two)
    share_near, share_far = call(sum_pair_kernel, "sum_hidden", [shape((2, chip_rows, width), bf16)] * 2)(
        *nears, tie(fars[0]), *fars[1:]
    )
    share_far = far(step(share_far))
    block = shape((1, 5, chip_rows, part), bf16)
    ones = call(add_kernel, "add_one", [block] * chips, scalars=1)(tie(chip_index), keep_one, recv_one)
    step(ones[0])
    ones = [ones[0], *to_chips(ones)]
    token_grad, sums = call(
        functools.partial(backward_three_kernel, images, heads, patches),
        "backward_three",
        [shape(tokens.shape, bf16), shape((24, width), f32)],
        [pltpu.VMEM((ROWS, width), f32)],
    )(
        tokens,
        middle_grad,
        packed_grad,
        spread,
        classes,
        sums_one,
        mixing_in,
        tie(vecs),
    )
    step(token_grad)
    two_shape = shape((3, chip_rows, part), bf16)
    (twos,) = call(add_two_kernel, "add_two", [shape(keep_two.shape, bf16)])(tie(keep_two), recv_two)
    twos = over_plane(step(twos))
    share_far = step(tie(share_far))
    result, sums_out = call(
        functools.partial(result_kernel, images, patches),
        "result",
        [shape(tokens.shape, bf16), shape((2, width), f32)],
    )(middle, cotangent, out_own, out_recv, tie(vecs))
    step(sums_out)
    (one,) = call(sum_kernel, "sum_one", [block])(tie(ones[0]), *ones[1:])
    one_near = mate(step(one))
    line_index = jnp.stack([tp, tp ^ 2]).astype(jnp.int32)
    (share,) = call(
        share_kernel,
        "share",
        [shape((2 * chip_rows + 32, width), bf16)],
        [pltpu.VMEM((32, width), f32)],
        scalars=1,
    )(line_index, share_near, tie(share_far), sums, sums_out, hb_near, hb_far)
    step(share)
    share = [share, *to_chips([share] * chips)]
    (two,) = call(sum_all_kernel, "sum_two", [two_shape])(tie(twos))
    two_near = mate(step(two))
    (one,) = call(add_two_kernel, "add_line_one", [block])(one, tie(one_near))
    one_far = far(step(one))
    (two,) = call(add_two_kernel, "add_line_two", [two_shape])(two, tie(two_near))
    two_far = far(step(two))
    share = [step(tie(a)) for a in share]
    (sums,) = call(sum_sums_kernel, "sum_sums", [shape((32, width), f32)])(*share)
    sums_near = mate(step(sums))
    share_recv = [twin(a) for a in share]
    (one,) = call(add_two_kernel, "last_one", [shape(block.shape[1:], bf16)])(one[0], tie(one_far)[0])
    step(one)
    one = [one, *to_chips([one] * chips)]
    wide = shape((2, chips, chip_rows, width), f32)
    hidden_in_grad, hidden_out_grad = call(hidden_final_kernel, "hidden_final", [wide, wide], scalars=1)(
        tie(place), *share, *share_recv
    )
    step(hidden_in_grad)
    (sums,) = call(add_single_kernel, "add_sums", [shape((32, width), f32)])(sums, tie(sums_near))
    sums_far = far(step(sums))
    (two,) = call(add_spread_kernel, "spread_two", [shape((chips, *two_shape.shape), bf16)])(two, tie(two_far))
    two = over_plane(step(two))
    one = [step(tie(a)) for a in one]
    one_recv = [twin(a) for a in one]
    scalar = pl.BlockSpec(memory_space=pltpu.SMEM)
    third = (1, chip_rows, part)
    params = pltpu.CompilerParams(vmem_limit_bytes=2 * SMALL)
    in_shape = shape((2, chips, chip_rows, 3 * width), f32)
    mixing_in_grad, mixing_out_grad = pl.pallas_call(
        mixing_one_kernel,
        grid=(3,),
        out_shape=(in_shape, wide),
        in_specs=[scalar]
        + [pl.BlockSpec(third, lambda b: (2 + b, 0, 0))] * (2 * chips)
        + [pl.BlockSpec((2, chip_rows, part), lambda b: (0, 0, 0))] * (2 * chips),
        out_specs=(
            pl.BlockSpec((2, chips, chip_rows, part), lambda b: (0, 0, 0, 2 * b)),
            pl.BlockSpec((2, chips, chip_rows, width), lambda b: (0, 0, 0, 0)),
        ),
        name="mixing_one",
        compiler_params=params,
        cost_estimate=cost(0.01),
    )(tie(place), *one, *one_recv, *one, *one_recv)
    step(mixing_out_grad)
    (sums,) = call(add_single_kernel, "add_sums_far", [shape((32, width), f32)])(sums, tie(sums_far))
    sums = step(sums + twin(step(sums)))
    table_grad = sums[8 : 8 + heads].T
    table_grad = jnp.concatenate([table_grad[:inner][::-1], table_grad[inner : relative_table.shape[0]]])
    hidden_bias_grad = lax.dynamic_index_in_dim(sums[26 : 26 + n_tp], tp, 0, keepdims=False)
    step(table_grad)
    two = tie(two)
    mixing_in_grad = pl.pallas_call(
        mixing_two_kernel,
        grid=(3,),
        out_shape=in_shape,
        in_specs=[scalar, pl.BlockSpec(memory_space=pl.ANY)]
        + [pl.BlockSpec((chips, *third), lambda b: (0, b, 0, 0))] * 2,
        out_specs=pl.BlockSpec((2, chips, chip_rows, part), lambda b: (0, 0, 0, 2 * b + 1)),
        input_output_aliases={1: 0},
        name="mixing_two",
        compiler_params=params,
        cost_estimate=cost(0.01),
    )(place, mixing_in_grad, two, twin(two))

    return (
        result,
        token_grad,
        sums[4],
        sums[5],
        mixing_in_grad.reshape(width, 3 * width),
        sums[6],
        sums[7],
        table_grad,
        mixing_out_grad.reshape(width, width),
        sums[0],
        sums[1],
        sums[2],
        sums[3],
        hidden_in_grad.reshape(width, width),
        hidden_bias_grad,
        hidden_out_grad.reshape(width, width),
        sums[24],
        sums[25],
    )


def solution(mesh):
    everywhere = P()
    rows = P("dp", "tp", None)
    hidden = (P(None, "tp"), P("tp"), P("tp", None))
    return jax.shard_map(
        functools.partial(per_device, mesh.shape["dp"], mesh.shape["tp"]),
        mesh=mesh,
        in_specs=(rows, *[everywhere] * 11, *hidden, everywhere, everywhere, rows),
        out_specs=(rows, rows, *[everywhere] * 11, *hidden, everywhere, everywhere),
        check_vma=False,
    )
```

```python
import functools

import jax
import jax.numpy as jnp
from jax import lax
from jax.experimental import pallas as pl
from jax.experimental.pallas import tpu as pltpu
from jax.sharding import PartitionSpec as P

GRID = 14
EPSILON = 1e-06
ROWS = 208
LANES = 768
SPREAD = 384
VMEM = 56 * 1024 * 1024
SMALL = 8 * 1024 * 1024
MEDIUM = 16 * 1024 * 1024
MIDDLE = ("hidden_final",)
LIGHT = ("add", "sum", "share", "last", "spread")

f32 = jnp.float32
bf16 = jnp.bfloat16

NN = (((1,), (0,)), ((), ()))
NT = (((1,), (1,)), ((), ()))
TN = (((0,), (0,)), ((), ()))

(
    FIRST_GAIN,
    FIRST_SHIFT,
    QUERY_BIAS,
    VALUE_BIAS,
    OUT_BIAS,
    SCALE_ATTENTION,
    SECOND_GAIN,
    SECOND_SHIFT,
    OUTPUT_BIAS,
    SCALE_HIDDEN,
) = range(10)


def dot(a, b, dims=NN):
    return lax.dot_general(a, b, dims, preferred_element_type=f32)


class Order:
    def __init__(self):
        self.last = None

    def tie(self, value):
        if self.last is not None:
            value, _ = lax.optimization_barrier((value, self.last))
        return value

    def step(self, value):
        self.last = value
        return value


US = {
    "hidden_near_own": 3,
    "hidden_near_mate": 20,
    "hidden_far_mate": 20,
    "backward_zero": 20,
    "backward_three": 20,
    "sum_hidden": 20,
    "sum_two": 0.01,
    "sum_one": 20,
}


def cost(us):
    return pl.CostEstimate(flops=int(us * 1.15e9), bytes_accessed=1000, transcendentals=0)


class Arriving:
    def __init__(self, ref, copy):
        self.ref, self.copy, self.shape = ref, copy, ref.shape

    def __getitem__(self, index):
        if self.copy is not None:
            self.copy.wait()
            self.copy = None
        return self.ref[index]


class Leaving:
    def __init__(self, ref, target, semaphores):
        self.ref, self.target, self.semaphores = ref, target, semaphores
        self.shape, self.dtype, self.copies = ref.shape, ref.dtype, []

    def __getitem__(self, index):
        return self.ref[index]

    def __setitem__(self, index, value):
        self.ref[index] = value

    def done(self, index=None):
        source = self.ref if index is None else self.ref.at[index]
        target = self.target if index is None else self.target.at[index]
        self.copies.append(pltpu.make_async_copy(source, target, self.semaphores.at[len(self.copies)]))
        self.copies[-1].start()


LARGE = 1 << 16


def streamed(kernel, n_in, n_out, scalars, moved, sent, n_own):
    def body(*refs):
        ins, rest = list(refs[:n_in]), refs[n_in:]
        targets, rest = list(rest[:n_out]), rest[n_out:]
        own, rest = rest[:n_own], rest[n_own:]
        buffers, (in_sem, out_sem) = list(rest[:-2]), rest[-2:]
        for i in range(n_in):
            if moved[i]:
                copy = pltpu.make_async_copy(ins[i], buffers[0], in_sem.at[i])
                copy.start()
                ins[i] = Arriving(buffers.pop(0), copy)
        leaving = []
        for o in range(n_out):
            if sent[o]:
                targets[o] = Leaving(buffers.pop(0), targets[o], out_sem.at[o])
                leaving.append(targets[o])
        kernel(*ins, *targets, *own)
        for ref in ins:
            if isinstance(ref, Arriving) and ref.copy is not None:
                ref.copy.wait()
        for ref in leaving:
            if not ref.copies:
                ref.done()
        for ref in leaving:
            for copy in ref.copies:
                copy.wait()

    return body


def call(kernel, name, outs, scratch=(), scalars=0, stream=False):
    def run(*args):
        size = lambda a: a.size * a.dtype.itemsize
        moved = [stream and i >= scalars and size(a) > LARGE for i, a in enumerate(args)]
        sent = [stream and size(o) > LARGE for o in outs]
        vmem, smem = pl.BlockSpec(memory_space=pltpu.VMEM), pl.BlockSpec(memory_space=pltpu.SMEM)
        anywhere = pl.BlockSpec(memory_space=pl.ANY)
        body, shapes = kernel, list(scratch)
        if stream:
            body = streamed(kernel, len(args), len(outs), scalars, moved, sent, len(scratch))
            shapes += [pltpu.VMEM(a.shape, a.dtype) for i, a in enumerate(args) if moved[i]]
            shapes += [pltpu.VMEM(o.shape, o.dtype) for i, o in enumerate(outs) if sent[i]]
            shapes += [pltpu.SemaphoreType.DMA((len(args),)), pltpu.SemaphoreType.DMA((len(outs), 4))]
        return pl.pallas_call(
            body,
            out_shape=outs,
            in_specs=[smem if i < scalars else anywhere if moved[i] else vmem for i in range(len(args))],
            out_specs=tuple(anywhere if flag else vmem for flag in sent),
            scratch_shapes=shapes,
            name=name,
            compiler_params=pltpu.CompilerParams(
                vmem_limit_bytes=SMALL if name.split("_")[0] in LIGHT else MEDIUM if name in MIDDLE else VMEM
            ),
            cost_estimate=cost(US.get(name, 0.01)),
        )(*args)

    return run


def norm_parts(values):
    center = values - jnp.mean(values, axis=-1, keepdims=True)
    spread = jnp.mean(center * center, axis=-1, keepdims=True)
    rate = lax.rsqrt(spread + EPSILON)
    return center * rate, rate


def spread_onehot():
    entry = lax.broadcasted_iota(jnp.int32, (LANES, SPREAD), 0)
    column = lax.broadcasted_iota(jnp.int32, (LANES, SPREAD), 1)
    d = lax.div(column, GRID)
    x = column - d * GRID
    return entry == d * (2 * GRID - 1) + x + GRID - 1


def expand_table(table_ref, spread_ref, bias_ref, heads):
    onehot = spread_onehot().astype(bf16)
    reach = 2 * GRID - 1
    inner = reach * reach
    for h in range(heads):
        rows = jnp.broadcast_to(table_ref[h : h + 1, :], (16, LANES))
        spread_ref[h * 16 : (h + 1) * 16, :] = pltpu.roll(rows, 0, 1, stride=1, stride_axis=0)
    rolled = spread_ref[...].astype(bf16)
    wide = dot(rolled, onehot)
    lane = lax.broadcasted_iota(jnp.int32, (16, 256), 1)
    hidden = lane > GRID * GRID
    for h in range(heads):
        bias_ref[h, 192:ROWS, :] = jnp.where(hidden, -1e30, 0.0)
        own = wide[h * 16 : (h + 1) * 16, :]
        to_class = table_ref[h : h + 1, inner + 1 : inner + 2]
        for y in range(GRID):
            part = pltpu.roll(own, (1 - GRID * (GRID - 1 - y)) % SPREAD, 1)[:, :256]
            part = jnp.where(lane == 0, to_class, jnp.where(hidden, -1e30, part))
            bias_ref[h, 1 + GRID * y : 1 + GRID * (y + 1), :] = part[:GRID, :]
        from_class = table_ref[h : h + 1, inner : inner + 1]
        corner = table_ref[h : h + 1, inner + 2 : inner + 3]
        top = jnp.where(lane == 0, corner, jnp.where(hidden, -1e30, from_class))
        bias_ref[h, 0:1, :] = top[:1, :]


def forward_kernel(
    images,
    heads,
    tok_ref,
    vec_ref,
    mixing_in_ref,
    table_ref,
    mixing_out_ref,
    normed_ref,
    packed_ref,
    attend_ref,
    mixed_ref,
    branch_ref,
    middle_ref,
    n2_ref,
    tok_pad,
    spread_ref,
    bias_ref,
):
    width = tok_ref.shape[2]
    patches = tok_ref.shape[1]
    vec = lambda i: vec_ref[i : i + 1, :]
    expand_table(table_ref, spread_ref, bias_ref, heads)
    for n in range(images):
        lo = n * ROWS
        tok_pad[lo + 192 : lo + ROWS, :] = jnp.zeros((ROWS - 192, width), f32)
        tok_pad[lo : lo + patches, :] = tok_ref[n].astype(f32)
    hat, _ = norm_parts(tok_pad[...])
    normed_ref[...] = (hat * vec(FIRST_GAIN) + vec(FIRST_SHIFT)).astype(bf16)
    normed_ref.done()
    for part in range(3):
        cols = slice(part * width, (part + 1) * width)
        value = dot(normed_ref[...], mixing_in_ref[:, cols])
        if part == 0:
            value = value + vec(QUERY_BIAS)
        if part == 2:
            value = value + vec(VALUE_BIAS)
        packed_ref[:, cols] = value.astype(bf16)
    packed_ref.done()
    first = lax.broadcasted_iota(jnp.int32, (1, 128), 1) < 64
    for n in range(images):
        rows = slice(n * ROWS, (n + 1) * ROWS)
        for pair in range(heads // 2):
            cols = [slice(k * width + pair * 128, k * width + (pair + 1) * 128) for k in range(3)]
            q, k, v = (packed_ref[rows, c] for c in cols)
            q = q * jnp.asarray(0.125, bf16)
            zero = jnp.zeros_like(q)
            outs = []
            for side in range(2):
                h = pair * 2 + side
                keep = first if side == 0 else jnp.logical_not(first)
                scores = dot(jnp.where(keep, q, zero), k, NT) + bias_ref[h, :, :ROWS]
                top = jnp.max(scores, axis=-1, keepdims=True)
                weights = jnp.exp(scores - top)
                total = jnp.sum(weights, axis=-1, keepdims=True)
                attend = (weights * (1.0 / total)).astype(bf16)
                attend_ref[n * heads + h] = attend
                outs.append(dot(attend, v))
            mixed_ref[rows, cols[0]] = jnp.where(first, outs[0], outs[1]).astype(bf16)
        attend_ref.done(pl.ds(n * heads, heads))
    mixed_ref.done()
    branch = dot(mixed_ref[...], mixing_out_ref[...]) + vec(OUT_BIAS)
    branch_ref[...] = branch.astype(bf16)
    branch_ref.done()
    middle = tok_pad[...] + vec(SCALE_ATTENTION) * branch
    middle_ref[...] = middle
    middle_ref.done()
    hat, _ = norm_parts(middle)
    n2_ref[...] = (hat * vec(SECOND_GAIN) + vec(SECOND_SHIFT)).astype(bf16)


def gelu_and_slope(v):
    cdf = 0.5 * (1.0 + lax.erf(v * 0.7071067811865476))
    density = jnp.exp(-0.5 * v * v) * 0.3989422804014327
    return v * cdf, cdf + v * density


def hidden_rows_kernel(carried, n2_ref, bg_ref, w1_ref, w2_ref, hb_ref, *rest):
    if carried:
        out_in, grad_in = rest[:2]
        rest = rest[2:]
    act_ref, slope_ref, out_ref, grad_ref = rest
    width, hidden = w1_ref.shape
    for f in range(hidden // 256):
        cols = slice(f * 256, (f + 1) * 256)
        before = dot(n2_ref[...], w1_ref[:, cols]) + hb_ref[0:1, cols]
        value, slope = gelu_and_slope(before)
        act_ref[:, cols] = value.astype(bf16)
        slope_ref[:, cols] = (dot(bg_ref[...], w2_ref[cols, :], NT) * slope).astype(bf16)
    for f in range(width // 256):
        cols = slice(f * 256, (f + 1) * 256)
        if out_ref is not None:
            hidden_out_columns(act_ref, w2_ref, out_in if carried else None, out_ref, cols)
        back = dot(slope_ref[...], w1_ref[cols, :], NT)
        if carried:
            back = back + grad_in[:, cols].astype(f32)
        grad_ref[:, cols] = back.astype(grad_ref.dtype)


def hidden_out_columns(act_ref, w2_ref, out_in, out_ref, cols):
    value = dot(act_ref[...], w2_ref[:, cols])
    if out_in is not None:
        value = value + out_in[:, cols].astype(f32)
    out_ref[:, cols] = value.astype(out_ref.dtype)


def half_columns(ref, half):
    width = ref.shape[1] // 2
    return ref[:, pl.ds(pl.multiple_of(half * width, 128), width)]


def put_chips(ref, block, value):
    chips, rows = ref.shape[0], ref.shape[2]
    for j in range(chips):
        ref[j, block] = value[j * rows : (j + 1) * rows, :].astype(ref.dtype)


def hidden_weights_kernel(
    core_ref, n2_ref, bg_ref, act_ref, slope_ref, n2_mate, bg_mate, act_mate, slope_mate, keep_ref, send_ref, hb_ref
):
    core = core_ref[0]
    for ref, half in ((send_ref, 1 - core), (keep_ref, core)):
        total = dot(half_columns(n2_ref, half), slope_ref[...], TN)
        put_chips(ref, 0, total + dot(half_columns(n2_mate, half), slope_mate[...], TN))
        total = dot(half_columns(act_ref, half), bg_ref[...], TN)
        put_chips(ref, 1, total + dot(half_columns(act_mate, half), bg_mate[...], TN))
    total = jnp.sum(slope_ref[...].astype(f32), axis=0, keepdims=True)
    hb_ref[...] = total + jnp.sum(slope_mate[...].astype(f32), axis=0, keepdims=True)


def hidden_own_kernel(part, core_ref, n2_ref, bg_ref, w1_ref, w2_ref, hb_ref, *rest):
    if part:
        keep_in, send_in, hb_in = rest[:3]
        rest = rest[3:]
    out, grad, keep_ref, send_ref, hb_grad, act, slope = rest
    hidden_rows_kernel(False, n2_ref, bg_ref, w1_ref, w2_ref, hb_ref, act, slope, out, grad)
    core = core_ref[0]
    chips, _, rows, _ = keep_ref.shape
    sides = [(send_ref, 1 - core), (keep_ref, core)]
    for i, (ref, half) in enumerate(sides):
        for m in range(2):
            if m == 0:
                total = dot(half_columns(n2_ref, half), slope[...], TN)
            else:
                total = dot(half_columns(act, half), bg_ref[...], TN)
            for j in range(chips):
                block = total[j * rows : (j + 1) * rows, :]
                if part:
                    block = block + (send_in, keep_in)[i][j, m].astype(f32)
                ref[j, m] = block.astype(bf16)
    total = jnp.sum(slope[...].astype(f32), axis=0, keepdims=True)
    hb_grad[...] = total + hb_in[...] if part else total


def hidden_first_kernel(place_ref, n2_ref, bg_ref, grad_in, *refs):
    pieces, (first_ref, second_ref, bias_ref, act_ref, slope_ref, grad_ref) = refs[:-6], refs[-6:]
    assemble(place_ref, pieces, first_ref, second_ref, bias_ref)
    weights = Whole(first_ref), Whole(second_ref)
    outs = act_ref, slope_ref, None, grad_ref
    hidden_rows_kernel(True, n2_ref, bg_ref, *weights, bias_ref, None, grad_in, *outs)


class Whole:
    def __init__(self, ref):
        self.ref = ref
        self.slab = ref.shape[1]
        self.shape = (ref.shape[0] * ref.shape[1], ref.shape[2])

    def __getitem__(self, index):
        rows, cols = index
        value = self.ref[:, :, cols]
        return value.reshape(self.shape[0], value.shape[2])[rows, :]


def hidden_both_kernel(core_ref, n2_ref, bg_ref, w1_ref, w2_ref, hb_ref, *rest):
    out_in, grad_in, mate_in, n2_other, bg_other, act_other, slope_other = rest[:7]
    out, grad, mate_out, keep, send, hb_grad, act, slope = rest[7:]
    hidden_rows_kernel(True, n2_ref, bg_ref, w1_ref, w2_ref, hb_ref, out_in, grad_in, act, slope, out, grad)
    for f in range(w2_ref.shape[1] // 256):
        hidden_out_columns(act_other, w2_ref, mate_in, mate_out, slice(f * 256, (f + 1) * 256))
    hidden_weights_kernel(
        core_ref, n2_other, bg_other, act_other, slope_other, n2_ref, bg_ref, act, slope, keep, send, hb_grad
    )


def result_kernel(images, patches, middle_ref, cot_ref, own_ref, recv_ref, vec_ref, result_ref, sums_ref):
    vec = lambda i: vec_ref[i : i + 1, :]
    scale_sum = jnp.zeros((1, middle_ref.shape[1]), f32)
    bias_sum = jnp.zeros((1, middle_ref.shape[1]), f32)
    for n in range(images):
        rows = slice(n * ROWS, n * ROWS + patches)
        cot = cot_ref[n].astype(f32)
        full = own_ref[rows, :].astype(f32) + recv_ref[rows, :].astype(f32) + vec(OUTPUT_BIAS)
        result_ref[n] = (middle_ref[rows, :] + vec(SCALE_HIDDEN) * full).astype(bf16)
        scale_sum = scale_sum + jnp.sum(cot * full, axis=0, keepdims=True)
        low = (vec(SCALE_HIDDEN) * cot).astype(bf16).astype(f32)
        bias_sum = bias_sum + jnp.sum(low, axis=0, keepdims=True)
    sums_ref[0:1, :] = bias_sum
    sums_ref[1:2, :] = scale_sum


def norm_back(grad, hat, rate, gain):
    scaled = grad * gain
    mean = jnp.mean(scaled, axis=-1, keepdims=True)
    cross = jnp.mean(scaled * hat, axis=-1, keepdims=True)
    return rate * (scaled - mean - hat * cross)


def attention_back(
    images, heads, packed_ref, attend_ref, mixed_grad, packed_grad, spread_ref, class_ref, table_ref
):
    width = mixed_grad.shape[1]
    first = lax.broadcasted_iota(jnp.int32, (1, 128), 1) < 64
    lane = lax.broadcasted_iota(jnp.int32, (ROWS, ROWS), 1)
    inner = (2 * GRID - 1) ** 2
    lane_out = lax.broadcasted_iota(jnp.int32, (1, LANES), 1)
    table_ref[...] = jnp.zeros(table_ref.shape, f32)
    spread_ref[...] = jnp.zeros(spread_ref.shape, f32)
    class_ref[...] = jnp.zeros(class_ref.shape, f32)
    for pair in range(heads // 2):
        cols = [slice(k * width + pair * 128, k * width + (pair + 1) * 128) for k in range(3)]
        totals = [None, None]
        for n in range(images):
            rows = slice(n * ROWS, (n + 1) * ROWS)
            q, k, v = (packed_ref[rows, c] for c in cols)
            back = mixed_grad[rows, cols[0]]
            zero = jnp.zeros_like(back)
            q_across, back_across = q.T, back.T
            grads = []
            for side in range(2):
                h = pair * 2 + side
                keep = first if side == 0 else jnp.logical_not(first)
                attend = attend_ref[n * heads + h]
                wide = attend.astype(f32)
                attend_grad = dot(jnp.where(keep, back, zero), v, NT)
                carried = jnp.sum(wide * attend_grad, axis=-1, keepdims=True)
                low = (wide * (attend_grad - carried)).astype(bf16)
                totals[side] = low.astype(f32) if n == 0 else totals[side] + low.astype(f32)
                scaled = low * jnp.asarray(0.125, bf16)
                own = slice(side * 64, side * 64 + 64)
                grads.append((dot(scaled, k), dot(q_across[own, :], scaled), dot(back_across[own, :], attend)))
            packed_grad[rows, cols[0]] = jnp.where(first, grads[0][0], grads[1][0]).astype(bf16)
            for i in range(1, 3):
                both = jnp.concatenate([grads[0][i], grads[1][i]], axis=0).astype(bf16)
                packed_grad[rows, cols[i]] = both.T
        for side in range(2):
            h = pair * 2 + side
            total = totals[side]
            top = total[0:1, :]
            corner = top[:, 0:1]
            from_class = jnp.sum(top, axis=-1, keepdims=True) - corner
            to_class = jnp.sum(total[:, 0:1], axis=0, keepdims=True) - corner
            class_ref[h : h + 1, :] = (
                jnp.where(lane_out == inner, from_class, 0.0)
                + jnp.where(lane_out == inner + 1, to_class, 0.0)
                + jnp.where(lane_out == inner + 2, corner, 0.0)
            )
            table_ref[:, :ROWS] = jnp.where(lane == 0, 0.0, total)
            gathered = jnp.zeros((GRID, SPREAD), f32)
            for y in range(GRID):
                block = table_ref[1 + GRID * y : 1 + GRID * (y + 1), :]
                gathered = gathered + pltpu.roll(block, (GRID * (GRID - 1 - y) - 1) % SPREAD, 1)
            for x in range(GRID):
                spread_ref[x * 16 + h : x * 16 + h + 1, :] = gathered[x : x + 1, :]


def backward_zero_kernel(
    images,
    patches,
    cot_ref,
    middle_ref,
    branch_ref,
    own_ref,
    recv_ref,
    mixing_out_ref,
    vec_ref,
    middle_grad,
    mixed_grad,
    low_ref,
    sums_ref,
):
    width = middle_ref.shape[1]
    vec = lambda i: vec_ref[i : i + 1, :]
    column_sum = lambda v: jnp.sum(v, axis=0, keepdims=True)
    for n in range(images):
        middle_grad[n * ROWS + 192 : (n + 1) * ROWS, :] = jnp.zeros((ROWS - 192, width), f32)
        middle_grad[n * ROWS : n * ROWS + patches, :] = cot_ref[n].astype(f32)
    sums = [jnp.zeros((1, width), f32) for _ in range(4)]
    for n in range(images):
        rows = slice(n * ROWS, (n + 1) * ROWS)
        grad = own_ref[rows, :].astype(f32) + recv_ref[rows, :].astype(f32)
        hat, rate = norm_parts(middle_ref[rows, :])
        sums[0] = sums[0] + column_sum(grad * hat)
        sums[1] = sums[1] + column_sum(grad)
        total = middle_grad[rows, :] + norm_back(grad, hat, rate, vec(SECOND_GAIN))
        middle_grad[rows, :] = total
        sums[2] = sums[2] + column_sum(total * branch_ref[rows, :].astype(f32))
        low = (vec(SCALE_ATTENTION) * total).astype(bf16)
        sums[3] = sums[3] + column_sum(low.astype(f32))
        low_ref[rows, :] = low
    for i, at in enumerate((2, 3, 1, 0)):
        sums_ref[at : at + 1, :] = sums[i]
    mixed_grad[...] = dot(low_ref[...], mixing_out_ref[...], NT).astype(bf16)


def backward_one_kernel(
    images,
    heads,
    part,
    core_ref,
    low_ref,
    mixed_ref,
    mixed_grad,
    packed_ref,
    attend_ref,
    normed_ref,
    packed_grad,
    spread_ref,
    class_ref,
    keep_one,
    send_one,
    keep_two,
    send_two,
    table_ref,
):
    core = core_ref[0]
    order = ((send_one, send_two, 1 - core), (keep_one, keep_two, core))
    for one, _, half in order:
        across = half_columns(mixed_ref, half).T
        for b in range(2):
            put_chips(one, b, dot(across, low_ref[:, b * part : (b + 1) * part]))
    attention_back(images, heads, packed_ref, attend_ref, mixed_grad, packed_grad, spread_ref, class_ref, table_ref)
    packed_grad.done()
    for one, two, half in order:
        across = half_columns(normed_ref, half).T
        for b in range(6):
            value = dot(across, packed_grad[:, b * part : (b + 1) * part])
            put_chips(two if b % 2 else one, b // 2 if b % 2 else 2 + b // 2, value)
        one.done()
        two.done()


def backward_three_kernel(
    images,
    heads,
    patches,
    tok_ref,
    middle_grad,
    packed_grad,
    spread_ref,
    class_ref,
    sums_one,
    mixing_in_ref,
    vec_ref,
    token_grad_ref,
    sums_ref,
    tok_pad,
):
    width = tok_ref.shape[2]
    vec = lambda i: vec_ref[i : i + 1, :]
    column_sum = lambda v: jnp.sum(v, axis=0, keepdims=True)
    onehot = spread_onehot().astype(bf16)
    value = spread_ref[...]
    high = value.astype(bf16)
    rest = (value - high.astype(f32)).astype(bf16)
    spread = dot(high, onehot, NT) + dot(rest, onehot, NT)
    entries = class_ref[...]
    for x in range(GRID):
        block = spread[x * 16 : (x + 1) * 16, :]
        entries = entries + (pltpu.roll(block, LANES - x, 1) if x else block)
    sums_ref[8:24, :] = entries
    sums_ref[0:4, :] = sums_one[0:4, :]
    sums_ref[6:7, :] = column_sum(packed_grad[:, :width].astype(f32))
    sums_ref[7:8, :] = column_sum(packed_grad[:, 2 * width :].astype(f32))
    sums = [jnp.zeros((1, width), f32) for _ in range(2)]
    for n in range(images):
        rows = slice(n * ROWS, (n + 1) * ROWS)
        grad = dot(packed_grad[rows, :], mixing_in_ref[...], NT)
        tok_pad[192:ROWS, :] = jnp.zeros((ROWS - 192, width), f32)
        tok_pad[:patches, :] = tok_ref[n].astype(f32)
        hat, rate = norm_parts(tok_pad[...])
        sums[0] = sums[0] + column_sum(grad * hat)
        sums[1] = sums[1] + column_sum(grad)
        total = middle_grad[rows, :] + norm_back(grad, hat, rate, vec(FIRST_GAIN))
        token_grad_ref[n] = total[:patches, :].astype(bf16)
    sums_ref[4:5, :] = sums[0]
    sums_ref[5:6, :] = sums[1]


def add_kernel(chip_ref, *refs):
    chip = chip_ref[0]
    chips = refs[0].shape[0]
    pairs, outs = refs[:-chips], refs[-chips:]
    for k, out in enumerate(outs):
        for i in range(0, len(pairs), 2):
            total = pairs[i][chip ^ k].astype(f32) + pairs[i + 1][chip ^ k].astype(f32)
            out[i // 2] = total.astype(bf16)


def add_two_kernel(keep_ref, recv_ref, out_ref):
    out_ref[...] = (keep_ref[...].astype(f32) + recv_ref[...].astype(f32)).astype(bf16)


def add_single_kernel(one_ref, two_ref, out_ref):
    out_ref[...] = one_ref[...] + two_ref[...]


def share_kernel(line_ref, near_ref, far_ref, sums_ref, out_sums_ref, hb_near, hb_far, out_ref, small):
    rows = near_ref.shape[1]
    for m in range(2):
        total = near_ref[m].astype(f32) + far_ref[m].astype(f32)
        out_ref[m * rows : (m + 1) * rows, :] = total.astype(bf16)
    count = sums_ref.shape[0]
    small[...] = jnp.zeros(small.shape, f32)
    small[0:count, :] = sums_ref[...]
    small[count : count + 2, :] = out_sums_ref[...]
    small[pl.ds(count + 2 + line_ref[0], 1), :] = hb_near[...]
    small[pl.ds(count + 2 + line_ref[1], 1), :] = hb_far[...]
    out_ref[2 * rows :, :] = small[...].astype(bf16)


def sum_sums_kernel(*refs):
    count = refs[-1].shape[0]
    at = slice(refs[0].shape[0] - count, refs[0].shape[0])
    total = refs[0][at, :].astype(f32)
    for ref in refs[1:-1]:
        total = total + ref[at, :].astype(f32)
    refs[-1][...] = total


def add_spread_kernel(one_ref, two_ref, out_ref):
    total = (one_ref[...].astype(f32) + two_ref[...].astype(f32)).astype(bf16)
    for j in range(out_ref.shape[0]):
        out_ref[j] = total


def sum_pair_kernel(*refs):
    count = (len(refs) - 2) // 2
    for parts, out in ((refs[:count], refs[-2]), (refs[count:-2], refs[-1])):
        total = parts[0][0].astype(f32)
        for ref in parts[1:]:
            total = total + ref[0].astype(f32)
        out[...] = total.astype(bf16)


def sum_all_kernel(parts_ref, total_ref):
    total = parts_ref[0].astype(f32)
    for j in range(1, parts_ref.shape[0]):
        total = total + parts_ref[j].astype(f32)
    total_ref[...] = total.astype(bf16)


def assemble(place_ref, refs, first_ref, second_ref, bias_ref):
    core, chip = place_ref[0], place_ref[1]
    chips, slab, _ = first_ref.shape

    def put(mine, other):
        for k in range(chips):
            mine[chip ^ k] = refs[k][:slab, :]
            other[chip ^ k] = refs[chips + k][:slab, :]

    @pl.when(core == 0)
    def _():
        put(first_ref, second_ref)

    @pl.when(core != 0)
    def _():
        put(second_ref, first_ref)

    bias_ref[...] = refs[0][slab : slab + 8, :].astype(f32)[0:1, :]


def sum_kernel(*refs):
    total = refs[0][...].astype(f32)
    for ref in refs[1:-1]:
        total = total + ref[...].astype(f32)
    refs[-1][...] = total.astype(bf16)


def hidden_final_kernel(place_ref, *refs):
    core, chip = place_ref[0], place_ref[1]
    in_ref, out_ref = refs[-2:]
    chips = (len(refs) - 2) // 2
    for k in range(chips):
        for ref, half in ((refs[k], core), (refs[chips + k], 1 - core)):
            rows = in_ref.shape[2]
            in_ref[half, chip ^ k] = ref[:rows, :].astype(f32)
            out_ref[half, chip ^ k] = ref[rows : 2 * rows, :].astype(f32)


def mixing_one_kernel(place_ref, *refs):
    core, chip = place_ref[0], place_ref[1]
    in_ref, out_ref = refs[-2:]
    chips = (len(refs) - 2) // 4
    first = pl.program_id(0) == 0
    for k in range(chips):
        for ref, half in ((refs[k], core), (refs[chips + k], 1 - core)):
            in_ref[half, chip ^ k] = ref[0].astype(f32)

    @pl.when(first)
    def _():
        for k in range(chips):
            for ref, half in ((refs[2 * chips + k], core), (refs[3 * chips + k], 1 - core)):
                part = ref.shape[2]
                for b in range(2):
                    out_ref[half, chip ^ k, :, b * part : (b + 1) * part] = ref[b].astype(f32)


def mixing_two_kernel(place_ref, before_ref, mine_ref, recv_ref, in_ref):
    core = place_ref[0]
    for j in range(mine_ref.shape[0]):
        for ref, half in ((mine_ref, core), (recv_ref, 1 - core)):
            in_ref[half, j] = ref[j, 0].astype(f32)


def per_device(
    n_dp,
    n_tp,
    tokens,
    first_gain,
    first_shift,
    mixing_in,
    query_bias,
    value_bias,
    relative_table,
    mixing_out,
    out_bias,
    scale_attention,
    second_gain,
    second_shift,
    hidden_in,
    hidden_bias,
    hidden_out,
    output_bias,
    scale_hidden,
    cotangent,
):
    images, patches, width = tokens.shape
    heads = relative_table.shape[1]
    count = images * ROWS
    hidden = hidden_in.shape[1]
    chips = n_dp // 2
    half = width // 2
    part = half
    chip_rows = half // chips
    plane = [[2 * i + c for i in range(chips)] for c in range(2)]
    dp, tp = lax.axis_index("dp"), lax.axis_index("tp")
    core, chip = dp % 2, dp // 2
    mate = lambda a: lax.ppermute(a, "tp", [(i, i ^ 1) for i in range(n_tp)])
    far = lambda a: lax.ppermute(a, "tp", [(i, i ^ 2) for i in range(n_tp)])
    twin = lambda a: lax.ppermute(a, "dp", [(i, i ^ 1) for i in range(n_dp)])
    over_plane = lambda a: lax.all_to_all(a, "dp", 0, 0, axis_index_groups=plane, tiled=True)
    over_line = lambda a: lax.all_to_all(a, "tp", 0, 0, tiled=True)
    copies = lambda a, n: jnp.broadcast_to(a[None], (n, *a.shape))
    by_core = lambda a, b: (jnp.where(core == 0, a, b), jnp.where(core == 0, b, a))
    add = lambda a, b: (a.astype(f32) + b.astype(f32)).astype(bf16)
    def hop(value, k):
        return lax.ppermute(value, "dp", [(i, i ^ (2 * k)) for i in range(n_dp)])

    def to_chips(values):
        if chips <= 4:
            return [hop(value, k) for k, value in enumerate(values) if k]
        order = lambda a, k: lax.dynamic_index_in_dim(a, chip ^ k, 0, keepdims=False)
        stacked = jnp.stack(values)
        stacked = jnp.stack([order(stacked, j) for j in range(chips)])
        stacked = over_plane(stacked)
        return [order(stacked, k) for k in range(1, chips)]

    shape = jax.ShapeDtypeStruct
    core_index = core.astype(jnp.int32).reshape(1)
    chip_index = chip.astype(jnp.int32).reshape(1)
    place = jnp.concatenate([core_index, chip_index])
    rows = (count, width)

    order = Order()
    tie, step = order.tie, order.step

    slab = width // chips
    piece = lax.dynamic_slice_in_dim(jnp.where(core == 0, hidden_in, hidden_out), chip * slab, slab, 0)
    piece = jnp.concatenate([piece, jnp.broadcast_to(hidden_bias[None], (16, hidden))])
    far_piece = far(step(piece))
    bg = (scale_hidden.astype(f32) * tie(cotangent).astype(f32)).astype(bf16)
    bg = step(jnp.pad(bg, ((0, 0), (0, ROWS - patches), (0, 0))).reshape(rows))
    bg_mate = mate(bg)

    vecs = jnp.stack(
        [
            first_gain,
            first_shift,
            query_bias,
            value_bias,
            out_bias,
            scale_attention,
            second_gain,
            second_shift,
            output_bias,
            scale_hidden,
        ]
    ).astype(f32)
    inner = (2 * GRID - 1) ** 2
    table = relative_table.astype(f32)
    table = jnp.concatenate([table[:inner][::-1], table[inner:]]).T
    table = jnp.pad(table, ((0, 0), (0, LANES - table.shape[1])))

    normed, packed, attend, mixed, branch, middle, n2 = call(
        functools.partial(forward_kernel, images, heads),
        "attention_forward",
        [
            shape(rows, bf16),
            shape((count, 3 * width), bf16),
            shape((images * heads, ROWS, ROWS), bf16),
            shape(rows, bf16),
            shape(rows, bf16),
            shape(rows, f32),
            shape(rows, bf16),
        ],
        [
            pltpu.VMEM(rows, f32),
            pltpu.VMEM((heads * 16, LANES), f32),
            pltpu.VMEM((heads, ROWS, 256), f32),
        ],
        stream=True,
    )(tokens, tie(vecs), mixing_in, table, mixing_out)

    n2_mate = mate(step(n2))
    pieces = step(tie(far_piece))
    pieces = [pieces, *to_chips([pieces] * chips)]

    weight = shape((chips, 2, half // chips, width), bf16)
    low_rows = shape(rows, bf16)
    hidden_cols = shape((count, hidden), bf16)

    def hidden_rows(name, n2, bg, w1, w2, bias, carried):
        return call(
            functools.partial(hidden_rows_kernel, bool(carried)),
            name,
            [hidden_cols, hidden_cols, low_rows, low_rows],
        )(n2, bg, w1, w2, tie(bias), *carried)

    near_bias = hidden_bias.astype(f32)[None]
    def hidden_own(name, n2, bg, part):
        return call(
            functools.partial(hidden_own_kernel, bool(part)),
            name,
            [low_rows, low_rows, weight, weight, shape((1, hidden), f32)],
            [pltpu.VMEM((count, hidden), bf16), pltpu.VMEM((count, hidden), bf16)],
            scalars=1,
        )(tie(core_index), n2, bg, hidden_in, hidden_out, near_bias, *part)

    out_own, grad_own, *near = hidden_own("hidden_near_own", n2, bg, ())
    step(out_own)
    bg_mate = step(tie(bg_mate))
    n2_mate = step(tie(n2_mate))
    pieces = [step(tie(a)) for a in pieces]
    other_pieces = [twin(a) for a in pieces]
    out_mate, grad_mate, keep_near, send_near, hb_near = hidden_own("hidden_near_mate", n2_mate, bg_mate, near)
    recv_near = twin(step(send_near))
    slabs = shape((chips, slab, hidden), bf16)
    far_in, far_out, far_bias, act_fm, slope_fm, grad_mate = call(
        hidden_first_kernel,
        "hidden_far_mate",
        [slabs, slabs, shape((1, hidden), f32), hidden_cols, hidden_cols, low_rows],
        scalars=1,
    )(tie(place), n2_mate, bg_mate, grad_mate, *pieces, *other_pieces)
    far_in, far_out = far_in.reshape(width, hidden), far_out.reshape(width, hidden)
    grad_recv = mate(step(grad_mate))
    block = shape((1, 2, chip_rows, width), bf16)
    nears = call(add_kernel, "add_near", [block] * chips, scalars=1)(tie(chip_index), keep_near, recv_near)
    step(nears[0])
    nears = [nears[0], *to_chips(nears)]
    out_own, grad_own, out_mate, keep_far, send_far, hb_far = call(
        hidden_both_kernel,
        "hidden_far_own",
        [low_rows, low_rows, low_rows, weight, weight, shape((1, hidden), f32)],
        [pltpu.VMEM((count, hidden), bf16), pltpu.VMEM((count, hidden), bf16)],
        scalars=1,
    )(
        tie(core_index),
        n2,
        bg,
        far_in,
        far_out,
        far_bias,
        out_own,
        grad_own,
        out_mate,
        n2_mate,
        bg_mate,
        act_fm,
        slope_fm,
    )
    out_recv = mate(step(out_mate))
    recv_far = twin(step(send_far))

    spread, classes = shape((GRID * 16, SPREAD), f32), shape((16, LANES), f32)
    nears = [step(tie(a)) for a in nears]
    middle_grad, mixed_grad, attention_grad, sums_one = call(
        functools.partial(backward_zero_kernel, images, patches),
        "backward_zero",
        [shape(rows, f32), shape(rows, bf16), shape(rows, bf16), shape((4, width), f32)],
    )(cotangent, middle, branch, grad_own, grad_recv, mixing_out, tie(vecs))
    step(attention_grad)
    fars = call(add_kernel, "add_far", [block] * chips, scalars=1)(tie(chip_index), keep_far, recv_far)
    step(fars[0])
    fars = [fars[0], *to_chips(fars)]
    packed_grad, spread, classes, keep_one, send_one, keep_two, send_two = call(
        functools.partial(backward_one_kernel, images, heads, part),
        "backward_one",
        [
            shape((count, 3 * width), bf16),
            spread,
            classes,
            shape((chips, 5, chip_rows, part), bf16),
            shape((chips, 5, chip_rows, part), bf16),
            shape((chips, 3, chip_rows, part), bf16),
            shape((chips, 3, chip_rows, part), bf16),
        ],
        [pltpu.VMEM((ROWS, SPREAD), f32)],
        scalars=1,
        stream=True,
    )(tie(core_index), attention_grad, mixed, mixed_grad, packed, attend, normed)
    step(send_one)
    recv_one = twin(send_one)
    recv_two = twin(send_two)
    share_near, share_far = call(sum_pair_kernel, "sum_hidden", [shape((2, chip_rows, width), bf16)] * 2)(
        *nears, tie(fars[0]), *fars[1:]
    )
    share_far = far(step(share_far))
    block = shape((1, 5, chip_rows, part), bf16)
    ones = call(add_kernel, "add_one", [block] * chips, scalars=1)(tie(chip_index), keep_one, recv_one)
    step(ones[0])
    ones = [ones[0], *to_chips(ones)]
    token_grad, sums = call(
        functools.partial(backward_three_kernel, images, heads, patches),
        "backward_three",
        [shape(tokens.shape, bf16), shape((24, width), f32)],
        [pltpu.VMEM((ROWS, width), f32)],
    )(
        tokens,
        middle_grad,
        packed_grad,
        spread,
        classes,
        sums_one,
        mixing_in,
        tie(vecs),
    )
    step(token_grad)
    two_shape = shape((3, chip_rows, part), bf16)
    (twos,) = call(add_two_kernel, "add_two", [shape(keep_two.shape, bf16)])(tie(keep_two), recv_two)
    twos = over_plane(step(twos))
    share_far = step(tie(share_far))
    result, sums_out = call(
        functools.partial(result_kernel, images, patches),
        "result",
        [shape(tokens.shape, bf16), shape((2, width), f32)],
    )(middle, cotangent, out_own, out_recv, tie(vecs))
    step(sums_out)
    (one,) = call(sum_kernel, "sum_one", [block])(tie(ones[0]), *ones[1:])
    one_near = mate(step(one))
    line_index = jnp.stack([tp, tp ^ 2]).astype(jnp.int32)
    (share,) = call(
        share_kernel,
        "share",
        [shape((2 * chip_rows + 32, width), bf16)],
        [pltpu.VMEM((32, width), f32)],
        scalars=1,
    )(line_index, share_near, tie(share_far), sums, sums_out, hb_near, hb_far)
    step(share)
    share = [share, *to_chips([share] * chips)]
    (two,) = call(sum_all_kernel, "sum_two", [two_shape])(tie(twos))
    two_near = mate(step(two))
    (one,) = call(add_two_kernel, "add_line_one", [block])(one, tie(one_near))
    one_far = far(step(one))
    (two,) = call(add_two_kernel, "add_line_two", [two_shape])(two, tie(two_near))
    two_far = far(step(two))
    share = [step(tie(a)) for a in share]
    (sums,) = call(sum_sums_kernel, "sum_sums", [shape((32, width), f32)])(*share)
    sums_near = mate(step(sums))
    share_recv = [twin(a) for a in share]
    (one,) = call(add_two_kernel, "last_one", [shape(block.shape[1:], bf16)])(one[0], tie(one_far)[0])
    step(one)
    one = [one, *to_chips([one] * chips)]
    wide = shape((2, chips, chip_rows, width), f32)
    hidden_in_grad, hidden_out_grad = call(hidden_final_kernel, "hidden_final", [wide, wide], scalars=1)(
        tie(place), *share, *share_recv
    )
    step(hidden_in_grad)
    (sums,) = call(add_single_kernel, "add_sums", [shape((32, width), f32)])(sums, tie(sums_near))
    sums_far = far(step(sums))
    (two,) = call(add_spread_kernel, "spread_two", [shape((chips, *two_shape.shape), bf16)])(two, tie(two_far))
    two = over_plane(step(two))
    one = [step(tie(a)) for a in one]
    one_recv = [twin(a) for a in one]
    scalar = pl.BlockSpec(memory_space=pltpu.SMEM)
    third = (1, chip_rows, part)
    params = pltpu.CompilerParams(vmem_limit_bytes=2 * SMALL)
    in_shape = shape((2, chips, chip_rows, 3 * width), f32)
    mixing_in_grad, mixing_out_grad = pl.pallas_call(
        mixing_one_kernel,
        grid=(3,),
        out_shape=(in_shape, wide),
        in_specs=[scalar]
        + [pl.BlockSpec(third, lambda b: (2 + b, 0, 0))] * (2 * chips)
        + [pl.BlockSpec((2, chip_rows, part), lambda b: (0, 0, 0))] * (2 * chips),
        out_specs=(
            pl.BlockSpec((2, chips, chip_rows, part), lambda b: (0, 0, 0, 2 * b)),
            pl.BlockSpec((2, chips, chip_rows, width), lambda b: (0, 0, 0, 0)),
        ),
        name="mixing_one",
        compiler_params=params,
        cost_estimate=cost(0.01),
    )(tie(place), *one, *one_recv, *one, *one_recv)
    step(mixing_out_grad)
    (sums,) = call(add_single_kernel, "add_sums_far", [shape((32, width), f32)])(sums, tie(sums_far))
    sums = step(sums + twin(step(sums)))
    table_grad = sums[8 : 8 + heads].T
    table_grad = jnp.concatenate([table_grad[:inner][::-1], table_grad[inner : relative_table.shape[0]]])
    hidden_bias_grad = lax.dynamic_index_in_dim(sums[26 : 26 + n_tp], tp, 0, keepdims=False)
    step(table_grad)
    two = tie(two)
    mixing_in_grad = pl.pallas_call(
        mixing_two_kernel,
        grid=(3,),
        out_shape=in_shape,
        in_specs=[scalar, pl.BlockSpec(memory_space=pl.ANY)]
        + [pl.BlockSpec((chips, *third), lambda b: (0, b, 0, 0))] * 2,
        out_specs=pl.BlockSpec((2, chips, chip_rows, part), lambda b: (0, 0, 0, 2 * b + 1)),
        input_output_aliases={1: 0},
        name="mixing_two",
        compiler_params=params,
        cost_estimate=cost(0.01),
    )(place, mixing_in_grad, two, twin(two))

    return (
        result,
        token_grad,
        sums[4],
        sums[5],
        mixing_in_grad.reshape(width, 3 * width),
        sums[6],
        sums[7],
        table_grad,
        mixing_out_grad.reshape(width, width),
        sums[0],
        sums[1],
        sums[2],
        sums[3],
        hidden_in_grad.reshape(width, width),
        hidden_bias_grad,
        hidden_out_grad.reshape(width, width),
        sums[24],
        sums[25],
    )


def solution(mesh):
    everywhere = P()
    rows = P("dp", "tp", None)
    hidden = (P(None, "tp"), P("tp"), P("tp", None))
    return jax.shard_map(
        functools.partial(per_device, mesh.shape["dp"], mesh.shape["tp"]),
        mesh=mesh,
        in_specs=(rows, *[everywhere] * 11, *hidden, everywhere, everywhere, rows),
        out_specs=(rows, rows, *[everywhere] * 11, *hidden, everywhere, everywhere),
        check_vma=False,
    )
```
